32 devices in a mesh: lat: 16 (over z, y, x), lev: 2 (over core).
Axes of the slice: x: 2, y: 2, z: 4, core: 2. Of those that a mesh axis runs over, the one named last changes fastest.
Arguments:
- winds: float32 [2, 8, 512, 1440], P(None, 'lev', 'lat'), may hold values from -6 to 6
- thickness: float32 [8, 512, 1440], P('lev', 'lat'), may hold values from 0.5 to 2
- cutoff: int32 [512], P('lat'), may hold values from 1 to 720, as said below
Outputs:
- new_winds: float32 [2, 8, 512, 1440], P(None, 'lev', 'lat')
- new_thickness: float32 [8, 512, 1440], P('lev', 'lat')
The draws below stay inside these ranges and needn't reach their ends.
Inputs may be any that keep to these rules, and one draw needn't show every extreme that they name: Rows outside the 96 latitudes nearest each pole have a cutoff of half of 1440; rows inside have smaller cutoffs.
All inputs are finite; a program needn't handle non-finite values.
Results may differ from the reference program's by a relative error of at most 0.0003.
Values sent between devices are 32-bit elements; how exact they have to be, the bound alone decides.
No kernel may reach another device: no remote copies, remote signals or barrier semaphores. Data moves between devices by JAX's collectives and lax.ppermute only.
A program may use at most 64 MiB of HBM per device.

```python
import math
import jax
import jax.numpy as jnp
from jax import lax

NLON = 1440
NLAT = 512
NLEV = 8
NPOLE = 96


def draw_cutoff(key, part):
    latitude = jnp.arange(NLAT).astype(jnp.int32)
    distance = jnp.minimum(latitude, NLAT - 1 - latitude)
    highest = NLON * 4 // 9
    jitter = jax.random.randint(key, (NLAT,), 0, max(2, NLON // 90)).astype(jnp.int32)
    polar_cut = 1 + (2 * distance + 1) * highest // (2 * NPOLE) + jitter
    return jnp.where(distance < NPOLE, polar_cut, NLON // 2).astype(jnp.int32)


def steps_of(own_key, shape, cuts, least, top_value):
    factor_of = 1.0
    for axis_at, shards_of in cuts:
        draws = jax.random.uniform(jax.random.fold_in(jax.random.fold_in(own_key, 6), axis_at), (shards_of,), jnp.float32, least / len(cuts), top_value / len(cuts))
        factor_of = factor_of * jnp.repeat(jnp.exp(draws), shape[axis_at] // shards_of).reshape((-1,) + (1,) * (len(shape) - 1 - axis_at))
    return factor_of


def centred(key, shape, width, most, shards=(), dtype=jnp.bfloat16):
    level = steps_of(key, shape, shards, -0.22, 0.18) if shards else 1.0
    values = jax.random.normal(key, shape, jnp.float32) * width * level
    return jnp.minimum(jnp.maximum(values, -most), most).astype(dtype)


def setup_inputs(seed: int = 0) -> dict:
    key_of = jax.random.split(jax.random.key(seed), 4)
    winds = centred(key_of[0], (2, NLEV, NLAT, NLON), 1.0, 6.0, ((1, 2), (2, 16)), jnp.float32)
    thickness = jnp.clip(jnp.exp(math.log(2.0) - 1.3862944 * jax.random.uniform(key_of[1], (NLEV, NLAT, NLON), jnp.float32) ** steps_of(key_of[1], (NLEV, NLAT, NLON), ((0, 2), (1, 16)), -0.2, 0.2)), 0.5, 2.0)
    cutoff = draw_cutoff(jax.random.fold_in(key_of[3], 71), 0)
    return dict(winds=winds, thickness=thickness, cutoff=cutoff)


time_step = 0.2
coriolis = 1.0

def fourier_table(lon_count):
    column = jnp.arange(lon_count).astype(jnp.int32)
    middle = lon_count // 2
    wavenumber = jnp.where(column <= middle, column, column - middle).astype(jnp.int32)
    points = jnp.arange(lon_count).astype(jnp.int32)
    phase = points[:, None] * wavenumber[None, :] % lon_count
    angle = phase.astype(jnp.float32) * (2.0 * math.pi / lon_count)
    single = (wavenumber == 0) | (wavenumber == middle)
    weight = jnp.where(single, 1.0 / math.sqrt(lon_count), math.sqrt(2.0 / lon_count)).astype(jnp.float32)
    values = jnp.where((column <= middle)[None, :], jnp.cos(angle), jnp.sin(angle)) * weight[None, :]
    return (values, wavenumber.astype(jnp.float32))

def remove_high(vectors, cuts, fourier, wavenumber):
    coeffs = jnp.dot(vectors, fourier, precision=lax.Precision.HIGHEST)
    coeffs = jnp.where(wavenumber[None, :] > cuts[:, None], coeffs, 0.0)
    return vectors - jnp.dot(coeffs, fourier.T, precision=lax.Precision.HIGHEST)

def filter_band(block, cuts, fourier, wavenumber):
    band_rows = block.shape[2]
    rows_first = jnp.transpose(block, (2, 0, 1, 3)).reshape(band_rows, -1, NLON)

    def one_row(pair):
        row_data, row_cut = pair
        return remove_high(row_data, jnp.full((row_data.shape[0],), row_cut, jnp.float32), fourier, wavenumber)
    result = lax.map(one_row, (rows_first, cuts.astype(jnp.float32)))
    return jnp.transpose(result.reshape(band_rows, 3, NLEV, NLON), (1, 2, 0, 3))

def step_fields(zonal, merid, depth, geo_pad, depth_pad, merid_pad, first_row, lat_total):
    lat_rows = depth.shape[1]
    row_index = (first_row + jnp.arange(lat_rows)).astype(jnp.float32)
    center = (row_index + 0.5) * (math.pi / lat_total) - 0.5 * math.pi
    cos_center = jnp.cos(center)[None, :, None]
    sin_center = jnp.sin(center)[None, :, None]
    edge_index = (first_row + jnp.arange(lat_rows + 1)).astype(jnp.float32)
    edge = jnp.sin(edge_index * (math.pi / lat_total))[None, :, None]
    zonal_flux = 0.25 * (depth + jnp.roll(depth, -1, axis=2)) * (zonal + jnp.roll(zonal, -1, axis=2))
    merid_flux = 0.25 * (depth_pad[:, :-1] + depth_pad[:, 1:]) * (merid_pad[:, :-1] + merid_pad[:, 1:]) * edge
    new_depth = depth - time_step * (zonal_flux - jnp.roll(zonal_flux, 1, axis=2) + (merid_flux[:, 1:] - merid_flux[:, :-1]))
    geo = geo_pad[:, 1:-1]
    new_zonal = zonal - time_step * (0.5 * (jnp.roll(geo, -1, axis=2) - jnp.roll(geo, 1, axis=2)) - coriolis * sin_center * merid)
    new_merid = merid - time_step * (0.5 * cos_center * (geo_pad[:, 2:] - geo_pad[:, :-2]) + coriolis * sin_center * zonal)
    return (new_zonal, new_merid, new_depth)

def reference(winds, thickness, cutoff):
    fields = jnp.concatenate([winds, thickness[None]], axis=0)
    fourier, wavenumber = fourier_table(NLON)
    north = filter_band(fields[:, :, :NPOLE], cutoff[:NPOLE], fourier, wavenumber)
    south = filter_band(fields[:, :, NLAT - NPOLE:], cutoff[NLAT - NPOLE:], fourier, wavenumber)
    fields = jnp.concatenate([north, fields[:, :, NPOLE:NLAT - NPOLE], south], axis=2)
    zonal, merid, depth = (fields[0], fields[1], fields[2])
    within = jnp.cumsum(depth[::-1], axis=0)[::-1] - depth
    geo = within + 0.5 * depth
    widths = ((0, 0), (1, 1), (0, 0))
    new_zonal, new_merid, new_depth = step_fields(zonal, merid, depth, jnp.pad(geo, widths), jnp.pad(depth, widths), jnp.pad(merid, widths), 0, NLAT)
    return (jnp.stack([new_zonal, new_merid], axis=0), new_depth)
```

```python
import functools
import math

import jax
import jax.numpy as jnp
import ml_dtypes
import numpy as np
from jax import lax
from jax.experimental import pallas as pl
from jax.experimental.pallas import tpu as pltpu
from jax.sharding import PartitionSpec as P

time_step = 0.2
coriolis = 1.0
RADIX = 12
LANES = 128
WIDE = 2 * LANES
HALF_ROOT3 = math.sqrt(3.0) / 2.0
f32 = jnp.float32
bf16 = jnp.bfloat16


def filter_tables(lon):
    chunk = lon // RADIX
    half = RADIX // 2
    table = np.zeros((half, WIDE, WIDE), np.float64)
    wave = np.zeros((half, WIDE), np.float64)
    point = np.arange(chunk, dtype=np.float64)
    unit = 2.0 * math.pi / lon

    def real_class(residue, at):
        column = at
        for q in range(chunk):
            m = RADIX * q + residue
            if m > lon // 2:
                break
            single = m == 0 or 2 * m == lon
            weight = math.sqrt((1.0 if single else 2.0) / (chunk * RADIX))
            for values in (np.cos, np.sin):
                if single and values is np.sin:
                    continue
                table[0, at : at + chunk, column] = weight * values(unit * ((m * point) % lon))
                wave[0, column] = m
                column += 1

    real_class(0, 0)
    real_class(half, LANES)
    weight = math.sqrt(2.0 / (chunk * RADIX))
    for k in range(1, half):
        for q in range(chunk):
            m = RADIX * q + k
            c = weight * np.cos(unit * ((m * point) % lon))
            s = weight * np.sin(unit * ((m * point) % lon))
            table[k, :chunk, q], table[k, LANES : LANES + chunk, q] = c, s
            table[k, :chunk, LANES + q], table[k, LANES : LANES + chunk, LANES + q] = -s, c
            wave[k, q] = wave[k, LANES + q] = min(m, lon - m)
    high = table.astype(np.float32).astype(ml_dtypes.bfloat16)
    low = (table - high.astype(np.float64)).astype(np.float32).astype(ml_dtypes.bfloat16)
    return high, low, wave.astype(np.float32)


def split_radix(c):
    s = [c[j] + c[j + 6] for j in range(6)]
    d = [c[j] - c[j + 6] for j in range(6)]
    t = [s[j] + s[j + 3] for j in range(3)]
    e = [s[j] - s[j + 3] for j in range(3)]
    t12 = t[1] + t[2]
    e12 = e[1] - e[2]
    y0 = t[0] + t12
    y4 = (t[0] - 0.5 * t12, HALF_ROOT3 * (t[2] - t[1]))
    y6 = e[0] - e12
    y2 = (e[0] + 0.5 * e12, -HALF_ROOT3 * (e[1] + e[2]))
    p, q = d[1] - d[5], d[2] - d[4]
    r, w = d[1] + d[5], d[2] + d[4]
    y3 = (d[0] - q, d[3] - r)
    u, v = d[0] + 0.5 * q, -0.5 * r - d[3]
    sp, sw = HALF_ROOT3 * p, HALF_ROOT3 * w
    y1 = (u + sp, v - sw)
    y5 = (u - sp, v + sw)
    return [(y0, y6), y1, y2, y3, y4, y5]


def join_radix(z):
    (z0, z6), (r1, i1), (r2, i2), (r3, i3), (r4, i4), (r5, i5) = z
    hp, sp = z0 - 0.5 * r4, HALF_ROOT3 * i4
    p = [z0 + r4, hp - sp, hp + sp]
    hq, sq = z6 - 0.5 * r2, HALF_ROOT3 * i2
    q = [z6 + r2, -hq - sq, hq - sq]
    e = [p[j] + q[j] for j in range(3)] + [p[j] - q[j] for j in range(3)]
    a, b, c, d = r1 + r5, HALF_ROOT3 * (r1 - r5), i1 + i5, HALF_ROOT3 * (i1 - i5)
    g = r3 - 0.5 * a
    f = -0.5 * c - i3
    o = [a + r3, b + f, -g - d, i3 - c, g - d, f - b]
    return [e[j] + o[j] for j in range(6)] + [e[j] - o[j] for j in range(6)]


def rolled(x, left):
    shift = (-left) % LANES
    return x if shift == 0 else pltpu.roll(x, shift, 1)


def lane_index(rows=8):
    return lax.broadcasted_iota(jnp.int32, (rows, LANES), 1)


def two_parts(x):
    high = x.astype(bf16)
    return high, (x - high.astype(f32)).astype(bf16)


def filter_kernel(
    lon, lat_total, winds, thick, cutoff, high_hbm, low_hbm, wave, out, column, trig,
    x, high, low, yh, yl, z, cut, sem,
):
    levels, rows = x.shape[1:3]
    tiles = out.shape[2]
    groups = rows // 8
    chunk = lon // RADIX
    gap = LANES - chunk
    tail = lon - (tiles - 1) * LANES
    half = RADIX // 2
    span = levels * rows
    copies = [
        pltpu.make_async_copy(winds.at[0], x.at[0], sem.at[0]),
        pltpu.make_async_copy(winds.at[1], x.at[1], sem.at[1]),
        pltpu.make_async_copy(thick, x.at[2], sem.at[2]),
    ]
    for copy in copies:
        copy.start()
    tables = [
        pltpu.make_async_copy(high_hbm, high, sem.at[3]),
        pltpu.make_async_copy(low_hbm, low, sem.at[4]),
    ]

    least = cutoff[0]
    for r in range(1, rows):
        least = jnp.minimum(least, cutoff[r])
    filtering = least < lon // 2

    @pl.when(filtering)
    def _():
        for copy in tables:
            copy.start()

    first = lax.axis_index("lat") * rows
    index = (first + lax.broadcasted_iota(jnp.int32, (rows, LANES), 0)).astype(f32)
    centre = (index + 0.5) * (math.pi / lat_total) - 0.5 * math.pi
    trig[0] = jnp.sin(centre)
    trig[1] = jnp.cos(centre)
    trig[2] = jnp.sin(index * (math.pi / lat_total))
    trig[3] = jnp.sin((index + 1.0) * (math.pi / lat_total))
    lane, lane16 = lane_index(), lane_index(16)

    def tiles_of(f, l, at):
        got = [x[f, l, at, pl.ds(LANES * j, LANES)] for j in range(tiles - 1)]
        last = x[f, l, at, pl.ds(LANES * (tiles - 1), tail)]
        if tail < LANES:
            last = jnp.concatenate([last, jnp.zeros((at.size, LANES - tail), f32)], axis=1)
        return got + [last]

    @pl.when(jnp.logical_not(filtering))
    def _():
        for copy in copies:
            copy.wait()

        def keep(n, _):
            f, l = n // levels, n % levels
            for g in range(groups):
                v = tiles_of(f, l, pl.ds(8 * g, 8))
                v[-1] = jnp.where(lane < tail, v[-1], rolled(v[0], LANES - tail))
                for j in range(tiles):
                    out[f, l, j, pl.ds(8 + 8 * g, 8), :] = v[j]
            return 0

        lax.fori_loop(0, 3 * levels, keep, 0)

    @pl.when(filtering)
    def _():
        for r in range(rows):
            cut[pl.ds(r, 1), :] = jnp.full((1, LANES), cutoff[r].astype(f32), f32)

        for f in range(3):
            copies[f].wait()

            def forward(l, _, f=f):
                for g in range(rows // 16):
                    v = tiles_of(f, l, pl.ds(16 * g, 16))
                    at = pl.ds(pl.multiple_of(f * span + l * rows + 16 * g, 16), 16)
                    c = []
                    for j in range(RADIX):
                        turn = gap * j
                        here = jnp.where(lane16 < LANES - turn, v[j], v[j - 1]) if turn else v[j]
                        c.append(rolled(here, -turn))
                    c[-1] = jnp.where(lane16 < chunk, c[-1], 0.0)
                    for t, pair in enumerate(split_radix(c)):
                        for part in range(2):
                            hi, lo = two_parts(pair[part])
                            yh[t, at, LANES * part : LANES * (part + 1)] = hi
                            yl[t, at, LANES * part : LANES * (part + 1)] = lo
                return 0

            lax.fori_loop(0, levels, forward, 0)
        for copy in tables:
            copy.wait()

        def product(a, b, side):
            return lax.dot_general(a, b, (((1,), (side,)), ((), ())), preferred_element_type=f32)

        def three(ah, al, t, side):
            th, tl = high[t], low[t]
            return product(ah, th, side) + (product(al, th, side) + product(ah, tl, side))

        kept = jnp.concatenate([cut[...], cut[...]], axis=1)
        for t in range(half):
            coeffs = three(yh[t], yl[t], t, 0).reshape(3 * levels, rows, WIDE)
            coeffs = jnp.where(wave[t : t + 1][None] <= kept[None], coeffs, 0.0)
            ch, cl = two_parts(coeffs.reshape(3 * span, WIDE))
            z[t] = three(ch, cl, t, 1)

        def backward(n, _):
            f, l = n // levels, n % levels
            for g in range(groups):
                at = pl.ds(pl.multiple_of(n * rows + 8 * g, 8), 8)
                c = join_radix([(z[t, at, :LANES], z[t, at, LANES:]) for t in range(half)])
                c = [rolled(c[j % RADIX], gap * j) for j in range(RADIX + 1)]
                for j in range(tiles):
                    out[f, l, j, pl.ds(8 + 8 * g, 8), :] = jnp.where(
                        lane < LANES - gap * (j + 1), c[j], c[j + 1]
                    )
            return 0

        lax.fori_loop(0, 3 * levels, backward, 0)

    for j in range(tiles):
        at = pl.ds(8, rows)
        total = out[2, 0, j, at, :]
        for l in range(1, levels):
            total = total + out[2, l, j, at, :]
        column[j] = total


def filtered_fields(winds, thick, cutoff, lat_total):
    levels, rows, lon = thick.shape
    tiles = -(-lon // LANES)
    assert lon % RADIX == 0 and lon // RADIX <= LANES and tiles == RADIX and rows % 16 == 0
    high, low, wave = filter_tables(lon)
    half = RADIX // 2
    count = 3 * levels * rows
    shape = jax.ShapeDtypeStruct
    vmem = pl.BlockSpec(memory_space=pltpu.VMEM)
    hbm = pl.BlockSpec(memory_space=pltpu.HBM)
    return pl.pallas_call(
        functools.partial(filter_kernel, lon, lat_total),
        out_shape=[
            shape((3, levels, tiles, rows + 16, LANES), f32),
            shape((tiles, rows, LANES), f32),
            shape((4, rows, LANES), f32),
        ],
        in_specs=[hbm, hbm, pl.BlockSpec(memory_space=pltpu.SMEM), hbm, hbm, vmem],
        out_specs=[vmem, vmem, vmem],
        scratch_shapes=[
            pltpu.VMEM((3, levels, rows, lon), f32),
            pltpu.VMEM((half, WIDE, WIDE), bf16),
            pltpu.VMEM((half, WIDE, WIDE), bf16),
            pltpu.VMEM((half, count, WIDE), bf16),
            pltpu.VMEM((half, count, WIDE), bf16),
            pltpu.VMEM((half, count, WIDE), f32),
            pltpu.VMEM((rows, LANES), f32),
            pltpu.SemaphoreType.DMA((5,)),
        ],
        compiler_params=pltpu.CompilerParams(vmem_limit_bytes=40 << 20),
        name="filter",
    )(winds, thick, cutoff, jnp.asarray(high), jnp.asarray(low), jnp.asarray(wave))


def pack_kernel(fields, below, first, last):
    levels, tiles = fields.shape[1:3]
    rows = below.shape[1]
    each = 2 * levels + 1
    for j in range(tiles):
        for out, at in ((first, 0), (last, rows - 1)):
            for l in range(levels):
                out[pl.ds(each * j + l, 1), :] = fields[1, l, j, pl.ds(8 + at, 1), :]
                out[pl.ds(each * j + levels + l, 1), :] = fields[2, l, j, pl.ds(8 + at, 1), :]
            out[pl.ds(each * j + 2 * levels, 1), :] = below[j, pl.ds(at, 1), :]


def packed_edges(fields, below):
    levels, tiles = fields.shape[1:3]
    vmem = pl.BlockSpec(memory_space=pltpu.VMEM)
    edge = jax.ShapeDtypeStruct((tiles * (2 * levels + 1), LANES), f32)
    return pl.pallas_call(
        pack_kernel, out_shape=[edge, edge], in_specs=[vmem, vmem], out_specs=[vmem, vmem], name="pack"
    )(fields, below)


def step_kernel(
    lon, lat_count, lev_count, fields, below, before, after, trig, winds_hbm, thick_hbm, winds, thick, sem
):
    levels, tiles = fields.shape[1:3]
    rows = below.shape[1]
    groups = rows // 8
    each = 2 * levels + 1
    tail = lon - (tiles - 1) * LANES
    lane = lane_index()
    row = lax.broadcasted_iota(jnp.int32, (8, LANES), 0)
    place = lax.axis_index("lat")
    has_before = jnp.where(place > 0, 1.0, 0.0)
    has_after = jnp.where(place < lat_count - 1, 1.0, 0.0)

    def east(v):
        r = [rolled(a, 1) for a in v]
        return [jnp.where(lane < LANES - 1, r[j], r[j + 1]) for j in range(tiles - 1)] + [r[-1]]

    def west(v):
        r = [rolled(a, -1) for a in v]
        wrapped = [rolled(v[-1], tail - 1)] + r[:-1]
        return [jnp.where(lane > 0, r[j], wrapped[j]) for j in range(tiles)]

    def halo(ref, j, slot, present):
        return jnp.broadcast_to(ref[pl.ds(each * j + slot, 1), :], (8, LANES)) * present

    def beside(load, g, j, slot, toward):
        if toward < 0:
            value = load(8 * g - 1)
            return jnp.where(row > 0, value, halo(before, j, slot, has_before)) if g == 0 else value
        value = load(8 * g + 1)
        return jnp.where(row < 7, value, halo(after, j, slot, has_after)) if g == groups - 1 else value

    copies = []
    for g in range(groups):
        at = pl.ds(8 * g, 8)
        sine, cosine = trig[0, at, :], trig[1, at, :]
        south, north = trig[2, at, :], trig[3, at, :]
        sum_x, sum_y = None, None
        s = [below[j, at, :] for j in range(tiles)]
        se, sw = east(s), west(s)
        sum_x = [a - b for a, b in zip(se, sw)]
        sum_y = []
        for j in range(tiles):
            if g == 0:
                up = jnp.where(row > 0, pltpu.roll(s[j], 1, 0), halo(before, j, 2 * levels, has_before))
            else:
                up = below[j, pl.ds(8 * g - 1, 8), :]
            if g == groups - 1:
                down = jnp.where(row < 7, pltpu.roll(s[j], 7, 0), halo(after, j, 2 * levels, has_after))
            else:
                down = below[j, pl.ds(8 * g + 1, 8), :]
            sum_y.append(down - up)
        for l in reversed(range(levels)):
            u, v, h = ([fields[f, l, j, pl.ds(8 + 8 * g, 8), :] for j in range(tiles)] for f in range(3))
            he, hw, ue = east(h), west(h), east(u)
            flux = [(h[j] + he[j]) * (u[j] + ue[j]) for j in range(tiles)]
            flux_west = west(flux)
            for j in range(tiles):

                def rows_of(f, j=j, l=l):
                    return lambda at: fields[f, l, j, pl.ds(8 + at, 8), :]

                v_up, v_down = (beside(rows_of(1), g, j, l, to) for to in (-1, 1))
                h_up, h_down = (beside(rows_of(2), g, j, levels + l, to) for to in (-1, 1))
                merid = (h[j] + h_down) * (v[j] + v_down) * north - (h_up + h[j]) * (v_up + v[j]) * south
                dx, dy = he[j] - hw[j], h_down - h_up
                new_h = h[j] - (0.25 * time_step) * (flux[j] - flux_west[j] + merid)
                new_u = u[j] - time_step * (0.5 * (sum_x[j] + 0.5 * dx) - coriolis * sine * v[j])
                new_v = v[j] - time_step * (0.5 * cosine * (sum_y[j] + 0.5 * dy) + coriolis * sine * u[j])
                sum_x[j] = sum_x[j] + dx
                sum_y[j] = sum_y[j] + dy
                wide = LANES if j < tiles - 1 else tail
                here = pl.ds(LANES * j, wide)
                thick[l, at, here] = new_h[:, :wide]
                winds[0, l, at, here] = new_u[:, :wide]
                winds[1, l, at, here] = new_v[:, :wide]
        copies += [
            pltpu.make_async_copy(winds.at[:, :, at], winds_hbm.at[:, :, at], sem.at[2 * g]),
            pltpu.make_async_copy(thick.at[:, at], thick_hbm.at[:, at], sem.at[2 * g + 1]),
        ]
        copies[-2].start()
        copies[-1].start()
    for copy in copies:
        copy.wait()


def stepped(fields, below, before, after, trig, lon, lat_count, lev_count):
    levels, tiles = fields.shape[1:3]
    rows = below.shape[1]
    shape = jax.ShapeDtypeStruct
    vmem = pl.BlockSpec(memory_space=pltpu.VMEM)
    hbm = pl.BlockSpec(memory_space=pltpu.HBM)
    return pl.pallas_call(
        functools.partial(step_kernel, lon, lat_count, lev_count),
        out_shape=[shape((2, levels, rows, lon), f32), shape((levels, rows, lon), f32)],
        in_specs=[vmem] * 5,
        out_specs=[hbm, hbm],
        scratch_shapes=[
            pltpu.VMEM((2, levels, rows, lon), f32),
            pltpu.VMEM((levels, rows, lon), f32),
            pltpu.SemaphoreType.DMA((2 * (rows // 8),)),
        ],
        compiler_params=pltpu.CompilerParams(vmem_limit_bytes=40 << 20),
        name="step",
    )(fields, below, before, after, trig)


def per_device(winds, thick, cutoff):
    lat_count, lev_count = lax.axis_size("lat"), lax.axis_size("lev")
    levels, rows, lon = thick.shape
    fields, column, trig = filtered_fields(winds, thick, cutoff, rows * lat_count)
    below = jnp.zeros_like(column)
    place = lax.axis_index("lev")
    for hop in range(1, lev_count):
        got = lax.ppermute(column, "lev", [(i, (i - hop) % lev_count) for i in range(lev_count)])
        below = below + jnp.where(place + hop < lev_count, got, 0.0)
    first, last = packed_edges(fields, below)
    up = [(i, (i + 1) % lat_count) for i in range(lat_count)]
    before = lax.ppermute(last, "lat", up)
    after = lax.ppermute(first, "lat", [(j, i) for i, j in up])
    return tuple(stepped(fields, below, before, after, trig, lon, lat_count, lev_count))


def solution(mesh):
    return jax.shard_map(
        per_device,
        mesh=mesh,
        in_specs=(P(None, "lev", "lat", None), P("lev", "lat", None), P("lat")),
        out_specs=(P(None, "lev", "lat", None), P("lev", "lat", None)),
        check_vma=False,
    )
```

```python
import functools
import math

import jax
import jax.numpy as jnp
import ml_dtypes
import numpy as np
from jax import lax
from jax.experimental import pallas as pl
from jax.experimental.pallas import tpu as pltpu
from jax.sharding import PartitionSpec as P

time_step = 0.2
coriolis = 1.0
RADIX = 12
LANES = 128
WIDE = 2 * LANES
HALF_ROOT3 = math.sqrt(3.0) / 2.0
f32 = jnp.float32
bf16 = jnp.bfloat16


def waves(lon, t):
    at = lax.broadcasted_iota(jnp.int32, (1, WIDE), 1)
    second = at >= LANES
    q = jnp.where(second, at - LANES, at)
    if t == 0:
        m = jnp.where(second, RADIX * (q >> 1) + RADIX // 2, RADIX * ((q + 1) >> 1))
    else:
        m = RADIX * q + t
        m = jnp.minimum(m, lon - m)
    return m.astype(f32)


def filter_tables(lon):
    chunk = lon // RADIX
    half = RADIX // 2
    table = np.zeros((half, WIDE, WIDE), np.float64)
    point = np.arange(chunk, dtype=np.float64)
    unit = 2.0 * math.pi / lon

    def real_class(residue, at):
        column = at
        for m in range(residue, lon // 2 + 1, RADIX):
            single = m == 0 or 2 * m == lon
            weight = math.sqrt((1.0 if single else 2.0) / lon)
            for values in (np.cos, np.sin)[: 1 if single else 2]:
                table[0, at : at + chunk, column] = weight * values(unit * ((m * point) % lon))
                column += 1

    real_class(0, 0)
    real_class(half, LANES)
    weight = math.sqrt(2.0 / lon)
    for k in range(1, half):
        for q in range(chunk):
            m = RADIX * q + k
            c = weight * np.cos(unit * ((m * point) % lon))
            s = weight * np.sin(unit * ((m * point) % lon))
            table[k, :chunk, q], table[k, LANES : LANES + chunk, q] = c, s
            table[k, :chunk, LANES + q], table[k, LANES : LANES + chunk, LANES + q] = -s, c
    high = table.astype(np.float32).astype(ml_dtypes.bfloat16)
    low = (table - high.astype(np.float64)).astype(np.float32).astype(ml_dtypes.bfloat16)
    return np.stack([high, low], axis=1)


def split_radix(c):
    s = [c[j] + c[j + 6] for j in range(6)]
    d = [c[j] - c[j + 6] for j in range(6)]
    t = [s[j] + s[j + 3] for j in range(3)]
    e = [s[j] - s[j + 3] for j in range(3)]
    t12 = t[1] + t[2]
    e12 = e[1] - e[2]
    y0 = t[0] + t12
    y4 = (t[0] - 0.5 * t12, HALF_ROOT3 * (t[2] - t[1]))
    y6 = e[0] - e12
    y2 = (e[0] + 0.5 * e12, -HALF_ROOT3 * (e[1] + e[2]))
    p, q = d[1] - d[5], d[2] - d[4]
    r, w = d[1] + d[5], d[2] + d[4]
    y3 = (d[0] - q, d[3] - r)
    u, v = d[0] + 0.5 * q, -0.5 * r - d[3]
    sp, sw = HALF_ROOT3 * p, HALF_ROOT3 * w
    y1 = (u + sp, v - sw)
    y5 = (u - sp, v + sw)
    return [(y0, y6), y1, y2, y3, y4, y5]


def join_radix(z):
    (z0, z6), (r1, i1), (r2, i2), (r3, i3), (r4, i4), (r5, i5) = z
    hp, sp = z0 - 0.5 * r4, HALF_ROOT3 * i4
    p = [z0 + r4, hp - sp, hp + sp]
    hq, sq = z6 - 0.5 * r2, HALF_ROOT3 * i2
    q = [z6 + r2, -hq - sq, hq - sq]
    e = [p[j] + q[j] for j in range(3)] + [p[j] - q[j] for j in range(3)]
    a, b, c, d = r1 + r5, HALF_ROOT3 * (r1 - r5), i1 + i5, HALF_ROOT3 * (i1 - i5)
    g = r3 - 0.5 * a
    f = -0.5 * c - i3
    o = [a + r3, b + f, -g - d, i3 - c, g - d, f - b]
    return [e[j] + o[j] for j in range(6)] + [e[j] - o[j] for j in range(6)]


def rolled(x, left):
    shift = (-left) % LANES
    return x if shift == 0 else pltpu.roll(x, shift, 1)


def lane_index(rows=8):
    return lax.broadcasted_iota(jnp.int32, (rows, LANES), 1)


def two_parts(x):
    high = x.astype(bf16)
    return high, (x - high.astype(f32)).astype(bf16)


def rows_at(start, size=8):
    return pl.ds(start, size)


def edge_kernel(lat_count, winds, thick, cutoff_hbm, sent_a, sent_b, trig, cut, v, h, cutoff, sem):
    levels, lon = v.shape[1:]
    rows = thick.shape[1]
    tiles = -(-lon // LANES)
    tail = lon - (tiles - 1) * LANES
    copies = [pltpu.make_async_copy(cutoff_hbm, cutoff, sem.at[4])]
    for side, start in enumerate((0, rows - 1)):
        copies.append(pltpu.make_async_copy(winds.at[1, :, start], v.at[side], sem.at[2 * side]))
        copies.append(pltpu.make_async_copy(thick.at[:, start], h.at[side], sem.at[2 * side + 1]))
    for copy in copies:
        copy.start()

    place = lax.axis_index("lat")
    index = (place * rows + lax.broadcasted_iota(jnp.int32, (rows, LANES), 0)).astype(f32)
    step = math.pi / (lat_count * rows)
    centre = (index + 0.5) * step - 0.5 * math.pi
    trig[0] = jnp.sin(centre)
    trig[1] = jnp.cos(centre)
    trig[2] = jnp.sin(index * step)
    trig[3] = jnp.sin((index + 1.0) * step)

    copies[0].wait()
    for r in range(rows):
        cut[pl.ds(r, 1), :] = jnp.full((1, LANES), cutoff[r].astype(f32), f32)
    for copy in copies[1:]:
        copy.wait()
    last_first = 1 - place % 2
    for out, side in ((sent_a, last_first), (sent_b, 1 - last_first)):
        out[rows_at(2 * levels * tiles), :] = jnp.full((8, LANES), cutoff[side * (rows - 1)].astype(f32), f32)
        for j in range(tiles):
            wide = LANES if j < tiles - 1 else tail
            for f, block in enumerate((v, h)):
                got = block[side, :, pl.ds(LANES * j, wide)]
                if wide < LANES:
                    got = jnp.concatenate([got, jnp.zeros((levels, LANES - wide), f32)], axis=1)
                out[pl.ds((2 * j + f) * levels, levels), :] = got


def in_hbm(x):
    return pltpu.with_memory_space_constraint(x, pltpu.HBM)


def edges(winds, thick, cutoff, lat_count):
    levels, rows, lon = thick.shape
    tiles = -(-lon // LANES)
    vmem = pl.BlockSpec(memory_space=pltpu.VMEM)
    hbm = pl.BlockSpec(memory_space=pltpu.HBM)
    edge = jax.ShapeDtypeStruct((2 * levels * tiles + 8, LANES), f32)
    return pl.pallas_call(
        functools.partial(edge_kernel, lat_count),
        out_shape=[edge, edge, pltpu.VMEM((4, rows, LANES), f32), pltpu.VMEM((rows, LANES), f32)],
        in_specs=[hbm] * 3,
        out_specs=[vmem] * 4,
        scratch_shapes=[
            pltpu.VMEM((2, levels, lon), f32),
            pltpu.VMEM((2, levels, lon), f32),
            pltpu.SMEM((rows,), jnp.int32),
            pltpu.SemaphoreType.DMA((5,)),
        ],
        compiler_params=pltpu.CompilerParams(vmem_limit_bytes=16 << 20),
        name="edges",
    )(in_hbm(winds), in_hbm(thick), in_hbm(cutoff))


def forward(v, chunk, y, at):
    gap = LANES - chunk
    lane = lane_index(v[0].shape[0])
    c = []
    for j in range(RADIX):
        turn = gap * j
        here = jnp.where(lane < LANES - turn, v[j], v[j - 1]) if turn else v[j]
        c.append(rolled(here, -turn))
    c[-1] = jnp.where(lane < chunk, c[-1], 0.0)
    for t, pair in enumerate(split_radix(c)):
        for part in range(2):
            hi, lo = two_parts(pair[part])
            y[t, at, LANES * part : LANES * (part + 1)] = hi
            y[t, at, WIDE + LANES * part : WIDE + LANES * (part + 1)] = lo


def low_pass(lon, t, y, z, tables, keep):
    def three(ah, al, side):
        th, tl = tables[t, 0], tables[t, 1]
        a = jnp.concatenate([ah, al, ah], axis=1)
        b = jnp.concatenate([th, th, tl], axis=side)
        return lax.dot_general(a, b, (((1,), (side,)), ((), ())), preferred_element_type=f32)

    coeffs = three(y[t, :, :WIDE], y[t, :, WIDE:], 0)
    count, rows = coeffs.shape[0], keep.shape[0]
    coeffs = coeffs.reshape(count // rows, rows, WIDE)
    coeffs = jnp.where(waves(lon, t)[None] <= keep[None], coeffs, 0.0).reshape(count, WIDE)
    ch, cl = two_parts(coeffs)
    z[t] = three(ch, cl, 1)


def backward(z, at, chunk):
    gap = LANES - chunk
    lane = lane_index()
    c = join_radix([(z[t, at, :LANES], z[t, at, LANES:]) for t in range(RADIX // 2)])
    c = [rolled(c[j % RADIX], gap * j) for j in range(RADIX + 1)]
    return [jnp.where(lane < LANES - gap * (j + 1), c[j], c[j + 1]) for j in range(RADIX)]


def extended(v, tail):
    return v[:-1] + [jnp.where(lane_index() < tail, v[-1], rolled(v[0], LANES - tail))]


def filter_kernel(winds, thick, tables_hbm, cut, out, column, tables, x, y, z, sem):
    levels, rows, lon = x.shape[1:]
    tiles = out.shape[2]
    chunk = lon // RADIX
    tail = lon - (tiles - 1) * LANES
    span = levels * rows
    copies = [
        pltpu.make_async_copy(winds.at[0], x.at[0], sem.at[0]),
        pltpu.make_async_copy(winds.at[1], x.at[1], sem.at[1]),
        pltpu.make_async_copy(thick, x.at[2], sem.at[2]),
    ]
    fetch = pltpu.make_async_copy(tables_hbm, tables, sem.at[3])
    for copy in copies + [fetch]:
        copy.start()
    keep = cut[...]
    filtering = jnp.min(keep) < lon // 2

    def own_tiles(f, l, at):
        got = [x[f, l, at, pl.ds(LANES * j, LANES)] for j in range(tiles - 1)]
        last = x[f, l, at, pl.ds(LANES * (tiles - 1), tail)]
        return got + [jnp.concatenate([last, jnp.zeros((at.size, LANES - tail), f32)], axis=1)]

    @pl.when(jnp.logical_not(filtering))
    def _():
        for f in range(3):
            copies[f].wait()

            def as_is(l, _, f=f):
                for g in range(rows // 8):
                    v = extended(own_tiles(f, l, rows_at(8 * g)), tail)
                    for j in range(tiles):
                        out[f, l, j, rows_at(1 + 8 * g), :] = v[j]
                return 0

            lax.fori_loop(0, levels, as_is, 0)
        fetch.wait()

    @pl.when(filtering)
    def _():
        for f in range(3):
            copies[f].wait()

            def forward_level(l, _, f=f):
                for g in range(rows // 16):
                    at = pl.ds(pl.multiple_of(f * span + l * rows + 16 * g, 16), 16)
                    forward(own_tiles(f, l, rows_at(16 * g, 16)), chunk, y, at)
                return 0

            lax.fori_loop(0, levels, forward_level, 0)
        fetch.wait()
        wide = jnp.concatenate([keep, keep], axis=1)
        for t in range(RADIX // 2):
            low_pass(lon, t, y, z, tables, wide)

        def backward_level(n, _):
            f, l = n // levels, n % levels
            for g in range(rows // 8):
                v = backward(z, rows_at(pl.multiple_of(n * rows + 8 * g, 8)), chunk)
                for j in range(tiles):
                    out[f, l, j, rows_at(1 + 8 * g), :] = v[j]
            return 0

        lax.fori_loop(0, 3 * levels, backward_level, 0)

    at = pl.ds(1, rows)
    for j in range(tiles):
        column[j, at, :] = functools.reduce(jnp.add, [out[2, l, j, at, :] for l in range(levels)])


def filtered_fields(winds, thick, cut):
    levels, rows, lon = thick.shape
    tiles = -(-lon // LANES)
    assert lon % RADIX == 0 and lon // RADIX <= LANES and tiles == RADIX
    assert rows % 16 == 0
    tables = jnp.asarray(filter_tables(lon))
    half = RADIX // 2
    count = 3 * levels * rows
    vmem = pl.BlockSpec(memory_space=pltpu.VMEM)
    hbm = pl.BlockSpec(memory_space=pltpu.HBM)
    return pl.pallas_call(
        filter_kernel,
        out_shape=[
            pltpu.VMEM((3, levels, tiles, rows + 8, LANES), f32),
            pltpu.VMEM((tiles, rows + 8, LANES), f32),
            pltpu.VMEM(tables.shape, bf16),
        ],
        in_specs=[hbm, hbm, hbm, vmem],
        out_specs=[vmem] * 3,
        scratch_shapes=[
            pltpu.VMEM((3, levels, rows, lon), f32),
            pltpu.VMEM((half, count, 2 * WIDE), bf16),
            pltpu.VMEM((half, count, WIDE), f32),
            pltpu.SemaphoreType.DMA((4,)),
        ],
        compiler_params=pltpu.CompilerParams(vmem_limit_bytes=24 << 20),
        cost_estimate=pl.CostEstimate(flops=10_000_000_000, bytes_accessed=8_000_000, transcendentals=0),
        name="filter",
    )(in_hbm(winds), in_hbm(thick), in_hbm(tables), cut)


def halo_kernel(lon, lat_count, got_a, got_b, tables, _fields, _column, out, column, y, z):
    levels, tiles, rows = out.shape[1], out.shape[2], out.shape[3] - 8
    chunk = lon // RADIX
    tail = lon - (tiles - 1) * LANES
    place = lax.axis_index("lat")
    odd = place % 2
    refs = (got_a, got_b)
    at = (jnp.where(odd == 1, 0, rows + 1), jnp.where(odd == 1, rows + 1, 0))
    keep = jnp.concatenate([ref[rows_at(2 * levels * tiles), :] for ref in refs], axis=0)

    def edge_tiles(ref):
        return [ref[rows_at(2 * levels * j, 2 * levels), :] for j in range(tiles)]

    def put(side, v):
        end = jnp.where(at[side] == 0, place == 0, place == lat_count - 1)
        for j in range(tiles):
            value = jnp.where(end, 0.0, v[j])
            for f in range(2):
                lines = [value[f * levels + l : f * levels + l + 1] for l in range(levels)]
                for l in range(levels):
                    out[1 + f, l, j, pl.ds(at[side], 1), :] = lines[l]
            column[j, pl.ds(at[side], 1), :] = functools.reduce(jnp.add, lines)

    filtering = jnp.min(keep) < lon // 2

    @pl.when(jnp.logical_not(filtering))
    def _():
        for side in range(2):
            put(side, extended(edge_tiles(refs[side]), tail))

    @pl.when(filtering)
    def _():
        both = [jnp.concatenate(pair, axis=0) for pair in zip(edge_tiles(got_a), edge_tiles(got_b))]
        forward(both, chunk, y, pl.ds(0, 16))
        wide = jnp.concatenate([keep, keep], axis=1)
        for t in range(RADIX // 2):
            low_pass(lon, t, y, z, tables, wide)
        for side in range(2):
            put(side, backward(z, rows_at(8 * side), chunk))


def with_halo(fields, column, tables, got_a, got_b, lon, lat_count):
    assert 2 * fields.shape[1] == 8
    half = RADIX // 2
    vmem = pl.BlockSpec(memory_space=pltpu.VMEM)
    return pl.pallas_call(
        functools.partial(halo_kernel, lon, lat_count),
        out_shape=[pltpu.VMEM(fields.shape, f32), pltpu.VMEM(column.shape, f32)],
        in_specs=[vmem] * 5,
        out_specs=[vmem] * 2,
        scratch_shapes=[pltpu.VMEM((half, 16, 2 * WIDE), bf16), pltpu.VMEM((half, 16, WIDE), f32)],
        input_output_aliases={3: 0, 4: 1},
        compiler_params=pltpu.CompilerParams(vmem_limit_bytes=24 << 20),
        name="halo",
    )(got_a, got_b, tables, fields, column)


def step_kernel(lon, fields, trig, *refs):
    *hops, winds_hbm, thick_hbm, winds, thick, sem = refs
    levels, tiles = fields.shape[1:3]
    rows = trig.shape[1]
    tail = lon - (tiles - 1) * LANES
    lane = lane_index()
    place = lax.axis_index("lev")
    masks = [jnp.where(place + k + 1 <= len(hops), 1.0, 0.0) for k in range(len(hops))]

    def below(j, at):
        terms = [ref[j, rows_at(at), :] * mask for ref, mask in zip(hops, masks)]
        return functools.reduce(jnp.add, terms) if terms else jnp.zeros((8, LANES), f32)

    def east(v):
        r = [rolled(a, 1) for a in v]
        return [jnp.where(lane < LANES - 1, r[j], r[j + 1]) for j in range(tiles - 1)] + [r[-1]]

    def west(v):
        r = [rolled(a, -1) for a in v]
        r_before = [rolled(v[-1], tail - 1)] + r[:-1]
        return [jnp.where(lane > 0, r[j], r_before[j]) for j in range(tiles)]

    copies = []
    for g in range(rows // 8):
        at = rows_at(8 * g)
        up, here, down = 8 * g, 8 * g + 1, 8 * g + 2
        sine, cosine = trig[0, at, :], trig[1, at, :]
        south, north = trig[2, at, :], trig[3, at, :]
        s = [below(j, here) for j in range(tiles)]
        sum_x = [a - b for a, b in zip(east(s), west(s))]
        sum_y = [below(j, down) - below(j, up) for j in range(tiles)]
        for l in reversed(range(levels)):
            u, v, h = ([fields[f, l, j, rows_at(here), :] for j in range(tiles)] for f in range(3))
            he, hw, ue = east(h), west(h), east(u)
            flux = [(h[j] + he[j]) * (u[j] + ue[j]) for j in range(tiles)]
            flux_west = west(flux)
            for j in range(tiles):
                v_up, v_down = fields[1, l, j, rows_at(up), :], fields[1, l, j, rows_at(down), :]
                h_up, h_down = fields[2, l, j, rows_at(up), :], fields[2, l, j, rows_at(down), :]
                merid = (h[j] + h_down) * (v[j] + v_down) * north - (h_up + h[j]) * (v_up + v[j]) * south
                dx, dy = he[j] - hw[j], h_down - h_up
                new_h = h[j] - (0.25 * time_step) * (flux[j] - flux_west[j] + merid)
                new_u = u[j] - time_step * (0.5 * (sum_x[j] + 0.5 * dx) - coriolis * sine * v[j])
                new_v = v[j] - time_step * (0.5 * cosine * (sum_y[j] + 0.5 * dy) + coriolis * sine * u[j])
                sum_x[j] = sum_x[j] + dx
                sum_y[j] = sum_y[j] + dy
                wide = LANES if j < tiles - 1 else tail
                to = pl.ds(LANES * j, wide)
                thick[l, at, to] = new_h[:, :wide]
                winds[0, l, at, to] = new_u[:, :wide]
                winds[1, l, at, to] = new_v[:, :wide]
        copies += [
            pltpu.make_async_copy(winds.at[:, :, at], winds_hbm.at[:, :, at], sem.at[2 * g]),
            pltpu.make_async_copy(thick.at[:, at], thick_hbm.at[:, at], sem.at[2 * g + 1]),
        ]
        copies[-2].start()
        copies[-1].start()
    for copy in copies:
        copy.wait()


def stepped(fields, trig, hops, lon):
    levels = fields.shape[1]
    rows = trig.shape[1]
    shape = jax.ShapeDtypeStruct
    vmem = pl.BlockSpec(memory_space=pltpu.VMEM)
    hbm = pl.BlockSpec(memory_space=pltpu.HBM)
    return pl.pallas_call(
        functools.partial(step_kernel, lon),
        out_shape=[shape((2, levels, rows, lon), f32), shape((levels, rows, lon), f32)],
        in_specs=[vmem] * (2 + len(hops)),
        out_specs=[hbm, hbm],
        scratch_shapes=[
            pltpu.VMEM((2, levels, rows, lon), f32),
            pltpu.VMEM((levels, rows, lon), f32),
            pltpu.SemaphoreType.DMA((2 * (rows // 8),)),
        ],
        compiler_params=pltpu.CompilerParams(vmem_limit_bytes=32 << 20),
        name="step",
    )(fields, trig, *hops)


def swaps(lat_count, lev_count, first):
    pairs = []
    for i in range(lat_count):
        other = i + 1 if (i - first) % 2 == 0 else i - 1
        for l in range(lev_count):
            if 0 <= other < lat_count:
                pairs.append((i * lev_count + l, other * lev_count + l))
            else:
                pairs.append((i * lev_count + l, i * lev_count + (l + 1) % lev_count))
    return pairs


def per_device(winds, thick, cutoff):
    lat_count, lev_count = lax.axis_size("lat"), lax.axis_size("lev")
    lon = thick.shape[-1]
    sent_a, sent_b, trig, cut = edges(winds, thick, cutoff, lat_count)
    got_a = lax.ppermute(sent_a, ("lat", "lev"), swaps(lat_count, lev_count, 0))
    got_b = lax.ppermute(sent_b, ("lat", "lev"), swaps(lat_count, lev_count, 1))
    fields, column, tables = filtered_fields(winds, thick, cut)
    fields, column = with_halo(fields, column, tables, got_a, got_b, lon, lat_count)
    hops = [
        lax.ppermute(column, "lev", [(i, (i - hop) % lev_count) for i in range(lev_count)])
        for hop in range(1, lev_count)
    ]
    return tuple(stepped(fields, trig, hops, lon))


def solution(mesh):
    return jax.shard_map(
        per_device,
        mesh=mesh,
        in_specs=(P(None, "lev", "lat", None), P("lev", "lat", None), P("lat")),
        out_specs=(P(None, "lev", "lat", None), P("lev", "lat", None)),
        check_vma=False,
    )
```

```python
import functools
import math

import jax
import jax.numpy as jnp
import ml_dtypes
import numpy as np
from jax import lax
from jax.experimental import pallas as pl
from jax.experimental.pallas import tpu as pltpu
from jax.sharding import PartitionSpec as P

time_step = 0.2
coriolis = 1.0
RADIX = 12
LANES = 128
WIDE = 2 * LANES
HALF_ROOT3 = math.sqrt(3.0) / 2.0
f32 = jnp.float32
bf16 = jnp.bfloat16


def filter_tables(lon):
    chunk, half = lon // RADIX, RADIX // 2
    point = np.arange(chunk)
    angle = 2.0 * math.pi * (np.outer(point, point) % chunk) / chunk
    table = np.zeros((WIDE, WIDE), np.float64)
    near, far = slice(0, chunk), slice(LANES, LANES + chunk)
    table[near, near], table[near, far] = np.cos(angle), np.sin(angle)
    table[far, near], table[far, far] = np.sin(angle), -np.cos(angle)
    table /= math.sqrt(lon)
    high = table.astype(np.float32).astype(ml_dtypes.bfloat16)
    low = (table - high.astype(np.float64)).astype(np.float32).astype(ml_dtypes.bfloat16)
    twiddle = np.zeros((2, 2, 8, LANES), np.float64)
    for k in range(1, half + 1):
        turn = 2.0 * math.pi * (k * point % lon) / lon
        for way, scale in enumerate((1.0, 1.0 if k == half else 2.0)):
            twiddle[way, 0, k, :chunk] = scale * np.cos(turn)
            twiddle[way, 1, k, :chunk] = scale * np.sin(turn)
    return np.stack([high, low]), twiddle.astype(np.float32)


def split_radix(c):
    s = [c[j] + c[j + 6] for j in range(6)]
    d = [c[j] - c[j + 6] for j in range(6)]
    t = [s[j] + s[j + 3] for j in range(3)]
    e = [s[j] - s[j + 3] for j in range(3)]
    t12 = t[1] + t[2]
    e12 = e[1] - e[2]
    y0 = t[0] + t12
    y4 = (t[0] - 0.5 * t12, HALF_ROOT3 * (t[2] - t[1]))
    y6 = e[0] - e12
    y2 = (e[0] + 0.5 * e12, -HALF_ROOT3 * (e[1] + e[2]))
    p, q = d[1] - d[5], d[2] - d[4]
    r, w = d[1] + d[5], d[2] + d[4]
    y3 = (d[0] - q, d[3] - r)
    u, v = d[0] + 0.5 * q, -0.5 * r - d[3]
    sp, sw = HALF_ROOT3 * p, HALF_ROOT3 * w
    y1 = (u + sp, v - sw)
    y5 = (u - sp, v + sw)
    return [(y0, y6), y1, y2, y3, y4, y5]


def join_radix(z):
    (z0, z6), (r1, i1), (r2, i2), (r3, i3), (r4, i4), (r5, i5) = z
    hp, sp = z0 - 0.5 * r4, HALF_ROOT3 * i4
    p = [z0 + r4, hp - sp, hp + sp]
    hq, sq = z6 - 0.5 * r2, HALF_ROOT3 * i2
    q = [z6 + r2, -hq - sq, hq - sq]
    e = [p[j] + q[j] for j in range(3)] + [p[j] - q[j] for j in range(3)]
    a, b, c, d = r1 + r5, HALF_ROOT3 * (r1 - r5), i1 + i5, HALF_ROOT3 * (i1 - i5)
    g = r3 - 0.5 * a
    f = -0.5 * c - i3
    o = [a + r3, b + f, -g - d, i3 - c, g - d, f - b]
    return [e[j] + o[j] for j in range(6)] + [e[j] - o[j] for j in range(6)]


def rolled(x, left):
    shift = (-left) % LANES
    return x if shift == 0 else pltpu.roll(x, shift, 1)


def lane_index(rows=8):
    return lax.broadcasted_iota(jnp.int32, (rows, LANES), 1)


def two_parts(x):
    high = x.astype(bf16)
    return high, (x - high.astype(f32)).astype(bf16)


def rows_at(start, size=8):
    return pl.ds(start, size)


def edge_kernel(lat_count, winds, thick, cutoff_hbm, sent_a, sent_b, trig, cut, v, h, cutoff, sem):
    levels, lon = v.shape[1:]
    rows = thick.shape[1]
    tiles = -(-lon // LANES)
    tail = lon - (tiles - 1) * LANES
    copies = [pltpu.make_async_copy(cutoff_hbm, cutoff, sem.at[4])]
    for side, start in enumerate((0, rows - 1)):
        copies.append(pltpu.make_async_copy(winds.at[1, :, start], v.at[side], sem.at[2 * side]))
        copies.append(pltpu.make_async_copy(thick.at[:, start], h.at[side], sem.at[2 * side + 1]))
    for copy in copies:
        copy.start()

    place = lax.axis_index("lat")
    index = (place * rows + lax.broadcasted_iota(jnp.int32, (rows, LANES), 0)).astype(f32)
    step = math.pi / (lat_count * rows)
    centre = (index + 0.5) * step - 0.5 * math.pi
    trig[0] = jnp.sin(centre)
    trig[1] = jnp.cos(centre)
    trig[2] = jnp.sin(index * step)
    trig[3] = jnp.sin((index + 1.0) * step)

    copies[0].wait()
    for r in range(rows):
        cut[pl.ds(r, 1), :] = jnp.full((1, LANES), cutoff[r].astype(f32), f32)
    for copy in copies[1:]:
        copy.wait()
    last_first = 1 - place % 2
    for out, side in ((sent_a, last_first), (sent_b, 1 - last_first)):
        limit = cutoff[side * (rows - 1)].astype(f32)
        for j in range(tiles):
            wide = LANES if j < tiles - 1 else tail
            for f, block in enumerate((v, h)):
                got = block[side, :, pl.ds(LANES * j, wide)]
                if wide < LANES:
                    got = jnp.concatenate([got, jnp.full((levels, LANES - wide), limit, f32)], axis=1)
                out[pl.ds((2 * j + f) * levels, levels), :] = got


def in_vmem(x):
    return pltpu.with_memory_space_constraint(x, pltpu.VMEM)


def in_hbm(x):
    return pltpu.with_memory_space_constraint(x, pltpu.HBM)


def edges(winds, thick, cutoff, lat_count):
    levels, rows, lon = thick.shape
    tiles = -(-lon // LANES)
    vmem = pl.BlockSpec(memory_space=pltpu.VMEM)
    hbm = pl.BlockSpec(memory_space=pltpu.HBM)
    assert lon < tiles * LANES
    edge = jax.ShapeDtypeStruct((2 * levels * tiles, LANES), f32)
    return pl.pallas_call(
        functools.partial(edge_kernel, lat_count),
        out_shape=[edge, edge, pltpu.VMEM((4, rows, LANES), f32), pltpu.VMEM((rows, LANES), f32)],
        in_specs=[hbm] * 3,
        out_specs=[vmem] * 4,
        scratch_shapes=[
            pltpu.VMEM((2, levels, lon), f32),
            pltpu.VMEM((2, levels, lon), f32),
            pltpu.SMEM((rows,), jnp.int32),
            pltpu.SemaphoreType.DMA((5,)),
        ],
        compiler_params=pltpu.CompilerParams(vmem_limit_bytes=16 << 20),
        cost_estimate=pl.CostEstimate(flops=4_000_000_000, bytes_accessed=8_000_000, transcendentals=0),
        name="edges",
    )(in_hbm(winds), in_hbm(thick), in_hbm(cutoff))


def forward(v, chunk, y, at, twiddle):
    gap, half = LANES - chunk, RADIX // 2
    lane = lane_index(v[0].shape[0])
    c = []
    for j in range(RADIX):
        turn = gap * j
        here = jnp.where(lane < LANES - turn, v[j], v[j - 1]) if turn else v[j]
        c.append(rolled(here, -turn))
    c[-1] = jnp.where(lane < chunk, c[-1], 0.0)
    (y0, y6), *pairs = split_radix(c)
    for k in range(half + 1):
        cos, sin = twiddle[0, 0, k : k + 1, :], twiddle[0, 1, k : k + 1, :]
        if k == 0:
            both = (y0, jnp.zeros_like(y0))
        elif k == half:
            both = (y6 * cos, -(y6 * sin))
        else:
            re, im = pairs[k - 1]
            both = (re * cos + im * sin, im * cos - re * sin)
        for part, value in enumerate(both):
            hi, lo = two_parts(value)
            y[k, at, LANES * part : LANES * (part + 1)] = hi
            y[k, at, WIDE + LANES * part : WIDE + LANES * (part + 1)] = lo


def three(high, low, tables):
    a = jnp.concatenate([high, low, high], axis=1)
    b = jnp.concatenate([tables[0], tables[0], tables[1]], axis=0)
    return lax.dot_general(a, b, (((1,), (0,)), ((), ())), preferred_element_type=f32)


def low_pass(lon, y, z, tables, keep):
    classes, count = y.shape[:2]
    shape = (classes, count, WIDE)
    both = y[...].reshape(classes * count, 2 * WIDE)
    coeffs = three(both[:, :WIDE], both[:, WIDE:], tables).reshape(shape)
    at = lax.broadcasted_iota(jnp.int32, (1, WIDE), 1)
    at = jnp.where(at < LANES, at, at - LANES)
    masked = []
    for k in range(classes):
        m = RADIX * at + k
        masked.append(jnp.where(jnp.minimum(m, lon - m).astype(f32) <= keep, coeffs[k], 0.0))
    high, low = two_parts(jnp.concatenate(masked, axis=0))
    z[...] = three(high, low, tables).reshape(shape)


def backward(z, at, chunk, twiddle):
    gap, half = LANES - chunk, RADIX // 2
    lane = lane_index()
    pairs = [(z[0, at, :LANES], None)]
    for k in range(1, half + 1):
        re, im = z[k, at, :LANES], z[k, at, LANES:]
        cos, sin = twiddle[1, 0, k : k + 1, :], twiddle[1, 1, k : k + 1, :]
        pairs.append((re * cos - im * sin, re * sin + im * cos if k < half else None))
    c = join_radix([(pairs[0][0], pairs[half][0])] + pairs[1:half])
    c = [rolled(c[j % RADIX], gap * j) for j in range(RADIX + 1)]
    return [jnp.where(lane < LANES - gap * (j + 1), c[j], c[j + 1]) for j in range(RADIX)]


def extended(v, tail):
    return v[:-1] + [jnp.where(lane_index() < tail, v[-1], rolled(v[0], LANES - tail))]


def filter_kernel(winds, thick, tables, twiddle, cut, out, column, y, z):
    levels, rows, lon = thick.shape
    tiles = out.shape[2]
    chunk = lon // RADIX
    tail = lon - (tiles - 1) * LANES
    order = (2, 0, 1)
    keep = cut[...]
    filtering = jnp.min(keep) < lon // 2

    def own_tiles(f, l, at):
        block, lead = (winds, (f, l)) if f < 2 else (thick, (l,))
        got = [block[(*lead, at, pl.ds(LANES * j, LANES))] for j in range(tiles - 1)]
        last = block[(*lead, at, pl.ds(LANES * (tiles - 1), tail))]
        return got + [jnp.concatenate([last, jnp.zeros((at.size, LANES - tail), f32)], axis=1)]

    @pl.when(jnp.logical_not(filtering))
    def _():
        for f in order:

            def as_is(l, _, f=f):
                for g in range(rows // 8):
                    v = extended(own_tiles(f, l, rows_at(8 * g)), tail)
                    for j in range(tiles):
                        out[f, l, j, rows_at(1 + 8 * g), :] = v[j]
                return 0

            lax.fori_loop(0, levels, as_is, 0)

    @pl.when(filtering)
    def _():
        units = y.shape[0]
        per = 3 * levels // units
        wide = jnp.concatenate([jnp.concatenate([keep, keep], axis=1)] * per, axis=0)

        def members(n):
            return [(order[(n * per + i) // levels], (n * per + i) % levels, i * rows) for i in range(per)]


        def split(n):
            for f, l, start in members(n):
                for g in range(rows // 16):
                    at = pl.ds(start + 16 * g, 16)
                    forward(own_tiles(f, l, rows_at(16 * g, 16)), chunk, y.at[n], at, twiddle)

        def join(n):
            for f, l, start in members(n):
                for g in range(rows // 8):
                    v = backward(z.at[n], rows_at(start + 8 * g), chunk, twiddle)
                    for j in range(tiles):
                        out[f, l, j, rows_at(1 + 8 * g), :] = v[j]

        split(0)
        for n in range(units):
            low_pass(lon, y.at[n], z.at[n], tables, wide)
            if n + 1 < units:
                split(n + 1)
            if n > 0:
                join(n - 1)
        join(units - 1)

    at = pl.ds(1, rows)
    for j in range(tiles):
        column[j, at, :] = functools.reduce(jnp.add, [out[2, l, j, at, :] for l in range(levels)])


def filtered_fields(winds, thick, cut, tables, twiddle):
    levels, rows, lon = thick.shape
    tiles = -(-lon // LANES)
    assert lon % RADIX == 0 and lon // RADIX <= LANES and tiles == RADIX
    assert rows % 16 == 0 and levels % 2 == 0
    classes = RADIX // 2 + 1
    per = 2
    units = 3 * levels // per
    vmem = pl.BlockSpec(memory_space=pltpu.VMEM)
    hbm = pl.BlockSpec(memory_space=pltpu.HBM)
    return pl.pallas_call(
        filter_kernel,
        out_shape=[
            pltpu.VMEM((3, levels, tiles, rows + 8, LANES), f32),
            pltpu.VMEM((tiles, rows + 8, LANES), f32),
        ],
        in_specs=[vmem] * 5,
        out_specs=[vmem] * 2,
        scratch_shapes=[
            pltpu.VMEM((units, classes, per * rows, 2 * WIDE), bf16),
            pltpu.VMEM((units, classes, per * rows, WIDE), f32),
        ],
        compiler_params=pltpu.CompilerParams(vmem_limit_bytes=24 << 20),
        cost_estimate=pl.CostEstimate(flops=10_000_000_000, bytes_accessed=8_000_000, transcendentals=0),
        name="filter",
    )(in_vmem(winds), in_vmem(thick), in_vmem(tables), in_vmem(twiddle), cut)


def halo_kernel(lon, lat_count, got_a, got_b, tables, twiddle, _fields, _column, out, column, y, z):
    levels, tiles, rows = out.shape[1], out.shape[2], out.shape[3] - 8
    chunk = lon // RADIX
    tail = lon - (tiles - 1) * LANES
    place = lax.axis_index("lat")
    odd = place % 2
    refs = (got_a, got_b)
    at = (jnp.where(odd == 1, 0, rows + 1), jnp.where(odd == 1, rows + 1, 0))
    keep = jnp.concatenate([ref[rows_at(2 * levels * (tiles - 1), 2 * levels), :] for ref in refs], axis=0)
    keep = jnp.where(lane_index(16) < tail, rolled(keep, tail), keep)

    def edge_tiles(ref):
        v = [ref[rows_at(2 * levels * j, 2 * levels), :] for j in range(tiles)]
        return v[:-1] + [jnp.where(lane_index() < tail, v[-1], 0.0)]

    def put(side, v):
        end = jnp.where(at[side] == 0, place == 0, place == lat_count - 1)
        for j in range(tiles):
            value = jnp.where(end, 0.0, v[j])
            for f in range(2):
                lines = [value[f * levels + l : f * levels + l + 1] for l in range(levels)]
                for l in range(levels):
                    out[1 + f, l, j, pl.ds(at[side], 1), :] = lines[l]
            column[j, pl.ds(at[side], 1), :] = functools.reduce(jnp.add, lines)

    filtering = jnp.min(keep) < lon // 2

    @pl.when(jnp.logical_not(filtering))
    def _():
        for side in range(2):
            put(side, extended(edge_tiles(refs[side]), tail))

    @pl.when(filtering)
    def _():
        both = [jnp.concatenate(pair, axis=0) for pair in zip(edge_tiles(got_a), edge_tiles(got_b))]
        forward(both, chunk, y, pl.ds(0, 16), twiddle)
        wide = jnp.concatenate([keep, keep], axis=1)
        low_pass(lon, y, z, tables, wide)
        for side in range(2):
            put(side, backward(z, rows_at(8 * side), chunk, twiddle))


def with_halo(fields, column, tables, twiddle, got_a, got_b, lon, lat_count):
    assert 2 * fields.shape[1] == 8
    classes = RADIX // 2 + 1
    vmem = pl.BlockSpec(memory_space=pltpu.VMEM)
    return pl.pallas_call(
        functools.partial(halo_kernel, lon, lat_count),
        out_shape=[pltpu.VMEM(fields.shape, f32), pltpu.VMEM(column.shape, f32)],
        in_specs=[vmem] * 6,
        out_specs=[vmem] * 2,
        scratch_shapes=[pltpu.VMEM((classes, 16, 2 * WIDE), bf16), pltpu.VMEM((classes, 16, WIDE), f32)],
        input_output_aliases={4: 0, 5: 1},
        compiler_params=pltpu.CompilerParams(vmem_limit_bytes=24 << 20),
        name="halo",
    )(got_a, got_b, tables, twiddle, fields, column)


def east(v):
    lane = lane_index()
    r = [rolled(a, 1) for a in v]
    return [jnp.where(lane < LANES - 1, a, b) for a, b in zip(r[:-1], r[1:])] + [r[-1]]


def west(v, tail):
    lane = lane_index()
    r = [rolled(a, -1) for a in v]
    r_before = [rolled(v[-1], tail - 1)] + r[:-1]
    return [jnp.where(lane > 0, a, b) for a, b in zip(r, r_before)]


def thickness_kernel(lon, fields, trig, thick_hbm, thick, sem):
    levels, tiles = fields.shape[1:3]
    rows = trig.shape[1]
    tail = lon - (tiles - 1) * LANES
    copies = []
    for g in range(rows // 8):
        at = rows_at(8 * g)
        up, here, down = 8 * g, 8 * g + 1, 8 * g + 2
        south, north = trig[2, at, :], trig[3, at, :]
        for l in range(levels):
            u, h = ([fields[f, l, j, rows_at(here), :] for j in range(tiles)] for f in (0, 2))
            he, ue = east(h), east(u)
            flux = [(h[j] + he[j]) * (u[j] + ue[j]) for j in range(tiles)]
            flux_west = west(flux, tail)
            for j in range(tiles):
                v_up, v, v_down = (fields[1, l, j, rows_at(r), :] for r in (up, here, down))
                h_up, h_down = (fields[2, l, j, rows_at(r), :] for r in (up, down))
                merid = (h[j] + h_down) * (v + v_down) * north - (h_up + h[j]) * (v_up + v) * south
                new = h[j] - (0.25 * time_step) * (flux[j] - flux_west[j] + merid)
                wide = LANES if j < tiles - 1 else tail
                thick[l, at, pl.ds(LANES * j, wide)] = new[:, :wide]
        copies.append(pltpu.make_async_copy(thick.at[:, at], thick_hbm.at[:, at], sem.at[g]))
        copies[-1].start()
    for copy in copies:
        copy.wait()


def winds_kernel(lon, fields, trig, *refs):
    *hops, winds_hbm, winds, sem = refs
    levels, tiles = fields.shape[1:3]
    rows = trig.shape[1]
    tail = lon - (tiles - 1) * LANES
    place = lax.axis_index("lev")
    masks = [jnp.where(place + k + 1 <= len(hops), 1.0, 0.0) for k in range(len(hops))]

    def below(j, at):
        terms = [ref[j, rows_at(at), :] * mask for ref, mask in zip(hops, masks)]
        return functools.reduce(jnp.add, terms) if terms else jnp.zeros((8, LANES), f32)

    copies = []
    for g in range(rows // 8):
        at = rows_at(8 * g)
        up, here, down = 8 * g, 8 * g + 1, 8 * g + 2
        sine, cosine = trig[0, at, :], trig[1, at, :]
        s = [below(j, here) for j in range(tiles)]
        sum_x = [a - b for a, b in zip(east(s), west(s, tail))]
        sum_y = [below(j, down) - below(j, up) for j in range(tiles)]
        for l in reversed(range(levels)):
            h = [fields[2, l, j, rows_at(here), :] for j in range(tiles)]
            he, hw = east(h), west(h, tail)
            for j in range(tiles):
                u, v = (fields[f, l, j, rows_at(here), :] for f in range(2))
                dx = he[j] - hw[j]
                dy = fields[2, l, j, rows_at(down), :] - fields[2, l, j, rows_at(up), :]
                new_u = u - time_step * (0.5 * (sum_x[j] + 0.5 * dx) - coriolis * sine * v)
                new_v = v - time_step * (0.5 * cosine * (sum_y[j] + 0.5 * dy) + coriolis * sine * u)
                sum_x[j] = sum_x[j] + dx
                sum_y[j] = sum_y[j] + dy
                wide = LANES if j < tiles - 1 else tail
                to = pl.ds(LANES * j, wide)
                winds[0, l, at, to] = new_u[:, :wide]
                winds[1, l, at, to] = new_v[:, :wide]
        copies.append(pltpu.make_async_copy(winds.at[:, :, at], winds_hbm.at[:, :, at], sem.at[g]))
        copies[-1].start()
    for copy in copies:
        copy.wait()


def step_call(kernel, name, shape, flops, lon, operands):
    rows = operands[1].shape[1]
    return pl.pallas_call(
        functools.partial(kernel, lon),
        out_shape=jax.ShapeDtypeStruct(shape, f32),
        in_specs=[pl.BlockSpec(memory_space=pltpu.VMEM)] * len(operands),
        out_specs=pl.BlockSpec(memory_space=pltpu.HBM),
        scratch_shapes=[pltpu.VMEM(shape, f32), pltpu.SemaphoreType.DMA((rows // 8,))],
        compiler_params=pltpu.CompilerParams(vmem_limit_bytes=24 << 20),
        cost_estimate=pl.CostEstimate(flops=flops, bytes_accessed=4_000_000, transcendentals=0),
        name=name,
    )(*operands)


def swaps(lat_count, lev_count, first):
    pairs = []
    for i in range(lat_count):
        other = i + 1 if (i - first) % 2 == 0 else i - 1
        for l in range(lev_count):
            if 0 <= other < lat_count:
                pairs.append((i * lev_count + l, other * lev_count + l))
            else:
                pairs.append((i * lev_count + l, i * lev_count + (l + 1) % lev_count))
    return pairs


def per_device(winds, thick, cutoff):
    lat_count, lev_count = lax.axis_size("lat"), lax.axis_size("lev")
    lon = thick.shape[-1]
    sent_a, sent_b, trig, cut = edges(winds, thick, cutoff, lat_count)
    got_a = lax.ppermute(sent_a, ("lat", "lev"), swaps(lat_count, lev_count, 0))
    got_b = lax.ppermute(sent_b, ("lat", "lev"), swaps(lat_count, lev_count, 1))
    tables, twiddle = (jnp.asarray(constant) for constant in filter_tables(lon))
    fields, column = filtered_fields(winds, thick, cut, tables, twiddle)
    fields, column = with_halo(fields, column, tables, twiddle, got_a, got_b, lon, lat_count)
    hops = [
        lax.ppermute(column, "lev", [(i, (i - hop) % lev_count) for i in range(lev_count)])
        for hop in range(1, lev_count)
    ]
    new_thick = step_call(thickness_kernel, "thickness", thick.shape, 4_000_000_000, lon, (fields, trig))
    new_winds = step_call(winds_kernel, "winds", winds.shape, 1_000_000_000, lon, (fields, trig, *hops))
    return new_winds, new_thick


def solution(mesh):
    return jax.shard_map(
        per_device,
        mesh=mesh,
        in_specs=(P(None, "lev", "lat", None), P("lev", "lat", None), P("lat")),
        out_specs=(P(None, "lev", "lat", None), P("lev", "lat", None)),
        check_vma=False,
    )
```

```python
import functools
import math

import jax
import jax.numpy as jnp
import ml_dtypes
import numpy as np
from jax import lax
from jax.experimental import pallas as pl
from jax.experimental.pallas import tpu as pltpu
from jax.sharding import PartitionSpec as P

time_step = 0.2
coriolis = 1.0
RADIX = 12
LANES = 128
WIDE = 2 * LANES
HALF_ROOT3 = math.sqrt(3.0) / 2.0
SPLIT_BATCH = 2
JOIN_BATCH = 4
LEVEL_BATCH = 4
f32 = jnp.float32
bf16 = jnp.bfloat16


def filter_tables(lon):
    chunk, half = lon // RADIX, RADIX // 2
    point = np.arange(chunk)
    angle = 2.0 * math.pi * (np.outer(point, point) % chunk) / chunk
    table = np.zeros((WIDE, WIDE), np.float64)
    near, far = slice(0, chunk), slice(LANES, LANES + chunk)
    table[near, near], table[near, far] = np.cos(angle), np.sin(angle)
    table[far, near], table[far, far] = np.sin(angle), -np.cos(angle)
    table /= math.sqrt(lon)
    high = table.astype(np.float32).astype(ml_dtypes.bfloat16)
    low = (table - high.astype(np.float64)).astype(np.float32).astype(ml_dtypes.bfloat16)
    twiddle = np.zeros((2, 2, 8, LANES), np.float64)
    for k in range(1, half + 1):
        turn = 2.0 * math.pi * (k * point % lon) / lon
        for way, scale in enumerate((1.0, 1.0 if k == half else 2.0)):
            twiddle[way, 0, k, :chunk] = scale * np.cos(turn)
            twiddle[way, 1, k, :chunk] = scale * np.sin(turn)
    return np.stack([high, low]), twiddle.astype(np.float32)


def split_radix(c):
    s = [c[j] + c[j + 6] for j in range(6)]
    d = [c[j] - c[j + 6] for j in range(6)]
    t = [s[j] + s[j + 3] for j in range(3)]
    e = [s[j] - s[j + 3] for j in range(3)]
    t12 = t[1] + t[2]
    e12 = e[1] - e[2]
    y0 = t[0] + t12
    y4 = (t[0] - 0.5 * t12, HALF_ROOT3 * (t[2] - t[1]))
    y6 = e[0] - e12
    y2 = (e[0] + 0.5 * e12, -HALF_ROOT3 * (e[1] + e[2]))
    p, q = d[1] - d[5], d[2] - d[4]
    r, w = d[1] + d[5], d[2] + d[4]
    y3 = (d[0] - q, d[3] - r)
    u, v = d[0] + 0.5 * q, -0.5 * r - d[3]
    sp, sw = HALF_ROOT3 * p, HALF_ROOT3 * w
    y1 = (u + sp, v - sw)
    y5 = (u - sp, v + sw)
    return [(y0, y6), y1, y2, y3, y4, y5]


def join_radix(z):
    (z0, z6), (r1, i1), (r2, i2), (r3, i3), (r4, i4), (r5, i5) = z
    hp, sp = z0 - 0.5 * r4, HALF_ROOT3 * i4
    p = [z0 + r4, hp - sp, hp + sp]
    hq, sq = z6 - 0.5 * r2, HALF_ROOT3 * i2
    q = [z6 + r2, -hq - sq, hq - sq]
    e = [p[j] + q[j] for j in range(3)] + [p[j] - q[j] for j in range(3)]
    a, b, c, d = r1 + r5, HALF_ROOT3 * (r1 - r5), i1 + i5, HALF_ROOT3 * (i1 - i5)
    g = r3 - 0.5 * a
    f = -0.5 * c - i3
    o = [a + r3, b + f, -g - d, i3 - c, g - d, f - b]
    return [e[j] + o[j] for j in range(6)] + [e[j] - o[j] for j in range(6)]


def rolled(x, left):
    shift = (-left) % LANES
    return x if shift == 0 else pltpu.roll(x, shift, 1)


def lane_index(rows=8):
    return lax.broadcasted_iota(jnp.int32, (rows, LANES), 1)


def two_parts(x):
    high = x.astype(bf16)
    return high, (x - high.astype(f32)).astype(bf16)


def rows_at(start, size=8):
    return pl.ds(start, size)


def edge_kernel(lat_count, winds, thick, cutoff_hbm, sent_a, sent_b, trig, cut, v, h, cutoff, sem):
    levels, lon = v.shape[1:]
    rows = thick.shape[1]
    tiles = -(-lon // LANES)
    tail = lon - (tiles - 1) * LANES
    copies = [pltpu.make_async_copy(cutoff_hbm, cutoff, sem.at[4])]
    for side, start in enumerate((0, rows - 1)):
        copies.append(pltpu.make_async_copy(winds.at[1, :, start], v.at[side], sem.at[2 * side]))
        copies.append(pltpu.make_async_copy(thick.at[:, start], h.at[side], sem.at[2 * side + 1]))
    for copy in copies:
        copy.start()

    place = lax.axis_index("lat")
    index = (place * rows + lax.broadcasted_iota(jnp.int32, (rows, LANES), 0)).astype(f32)
    step = math.pi / (lat_count * rows)
    centre = (index + 0.5) * step - 0.5 * math.pi
    trig[0] = jnp.sin(centre)
    trig[1] = jnp.cos(centre)
    trig[2] = jnp.sin(index * step)
    trig[3] = jnp.sin((index + 1.0) * step)

    copies[0].wait()
    for r in range(rows):
        cut[pl.ds(r, 1), :] = jnp.full((1, LANES), cutoff[r].astype(f32), f32)
    for copy in copies[1:]:
        copy.wait()
    last_first = 1 - place % 2
    for out, side in ((sent_a, last_first), (sent_b, 1 - last_first)):
        limit = cutoff[side * (rows - 1)].astype(f32)
        for j in range(tiles):
            wide = LANES if j < tiles - 1 else tail
            for f, block in enumerate((v, h)):
                got = block[side, :, pl.ds(LANES * j, wide)]
                if wide < LANES:
                    got = jnp.concatenate([got, jnp.full((levels, LANES - wide), limit, f32)], axis=1)
                out[pl.ds((2 * j + f) * levels, levels), :] = got


def in_vmem(x):
    return pltpu.with_memory_space_constraint(x, pltpu.VMEM)


def in_hbm(x):
    return pltpu.with_memory_space_constraint(x, pltpu.HBM)


def edges(winds, thick, cutoff, lat_count):
    levels, rows, lon = thick.shape
    tiles = -(-lon // LANES)
    vmem = pl.BlockSpec(memory_space=pltpu.VMEM)
    hbm = pl.BlockSpec(memory_space=pltpu.HBM)
    assert lon < tiles * LANES
    edge = pltpu.VMEM((2 * levels * tiles, LANES), f32)
    return pl.pallas_call(
        functools.partial(edge_kernel, lat_count),
        out_shape=[edge, edge, pltpu.VMEM((4, rows, LANES), f32), pltpu.VMEM((rows, LANES), f32)],
        in_specs=[hbm] * 3,
        out_specs=[vmem] * 4,
        scratch_shapes=[
            pltpu.VMEM((2, levels, lon), f32),
            pltpu.VMEM((2, levels, lon), f32),
            pltpu.SMEM((rows,), jnp.int32),
            pltpu.SemaphoreType.DMA((5,)),
        ],
        compiler_params=pltpu.CompilerParams(vmem_limit_bytes=16 << 20),
        cost_estimate=pl.CostEstimate(flops=4_000_000_000, bytes_accessed=8_000_000, transcendentals=0),
        name="edges",
    )(in_hbm(winds), in_hbm(thick), in_hbm(cutoff))


def forward(v, chunk, twiddle):
    gap, half = LANES - chunk, RADIX // 2
    lane = lane_index(v[0].shape[0])
    c = []
    for j in range(RADIX):
        turn = gap * j
        here = jnp.where(lane < LANES - turn, v[j], v[j - 1]) if turn else v[j]
        c.append(rolled(here, -turn))
    c[-1] = jnp.where(lane < chunk, c[-1], 0.0)
    (y0, y6), *pairs = split_radix(c)
    found = []
    for k in range(half + 1):
        cos, sin = twiddle[0, 0, k : k + 1, :], twiddle[0, 1, k : k + 1, :]
        if k == 0:
            both = (y0, jnp.zeros_like(y0))
        elif k == half:
            both = (y6 * cos, -(y6 * sin))
        else:
            re, im = pairs[k - 1]
            both = (re * cos + im * sin, im * cos - re * sin)
        re, im = (two_parts(value) for value in both)
        found.append((re[0], im[0], re[1], im[1]))
    return found


def put_parts(y, at, found):
    for k, parts in enumerate(found):
        for i, part in enumerate(parts):
            y[k, at, LANES * i : LANES * (i + 1)] = part


def three(high, low, tables):
    a = jnp.concatenate([high, low, high], axis=1)
    b = jnp.concatenate([tables[0], tables[0], tables[1]], axis=0)
    return lax.dot_general(a, b, (((1,), (0,)), ((), ())), preferred_element_type=f32)


def low_pass(lon, y, z, tables, keep):
    classes, count = y.shape[:2]
    shape = (classes, count, WIDE)
    both = y[...].reshape(classes * count, 2 * WIDE)
    coeffs = three(both[:, :WIDE], both[:, WIDE:], tables).reshape(shape)
    at = lax.broadcasted_iota(jnp.int32, (1, WIDE), 1)
    at = jnp.where(at < LANES, at, at - LANES)
    masked = []
    for k in range(classes):
        m = RADIX * at + k
        masked.append(jnp.where(jnp.minimum(m, lon - m).astype(f32) <= keep, coeffs[k], 0.0))
    high, low = two_parts(jnp.concatenate(masked, axis=0))
    z[...] = three(high, low, tables).reshape(shape)


def backward(z, at, chunk, twiddle):
    gap, half = LANES - chunk, RADIX // 2
    lane = lane_index()
    pairs = [(z[0, at, :LANES], None)]
    for k in range(1, half + 1):
        re, im = z[k, at, :LANES], z[k, at, LANES:]
        cos, sin = twiddle[1, 0, k : k + 1, :], twiddle[1, 1, k : k + 1, :]
        pairs.append((re * cos - im * sin, re * sin + im * cos if k < half else None))
    c = join_radix([(pairs[0][0], pairs[half][0])] + pairs[1:half])
    c = [rolled(c[j % RADIX], gap * j) for j in range(RADIX + 1)]
    return [jnp.where(lane < LANES - gap * (j + 1), c[j], c[j + 1]) for j in range(RADIX)]


def extended(v, tail):
    return v[:-1] + [jnp.where(lane_index() < tail, v[-1], rolled(v[0], LANES - tail))]


def filter_kernel(winds, thick, tables, twiddle, cut, out, column, y, z):
    levels, rows, lon = thick.shape
    tiles = out.shape[2]
    chunk = lon // RADIX
    tail = lon - (tiles - 1) * LANES
    order = (2, 0, 1)
    keep = cut[...]
    filtering = jnp.min(keep) < lon // 2

    def own_tiles(f, l, at):
        block, lead = (winds, (f, l)) if f < 2 else (thick, (l,))
        got = [block[(*lead, at, pl.ds(LANES * j, LANES))] for j in range(tiles - 1)]
        last = block[(*lead, at, pl.ds(LANES * (tiles - 1), tail))]
        return got + [jnp.concatenate([last, jnp.zeros((at.size, LANES - tail), f32)], axis=1)]

    @pl.when(jnp.logical_not(filtering))
    def _():
        for f in order:

            def as_is(l, _, f=f):
                for g in range(rows // 8):
                    v = extended(own_tiles(f, l, rows_at(8 * g)), tail)
                    for j in range(tiles):
                        out[f, l, j, rows_at(1 + 8 * g), :] = v[j]
                return 0

            lax.fori_loop(0, levels, as_is, 0)

    @pl.when(filtering)
    def _():
        units = y.shape[0]
        per = 3 * levels // units
        wide = jnp.concatenate([jnp.concatenate([keep, keep], axis=1)] * per, axis=0)

        def members(n):
            return [(order[(n * per + i) // levels], (n * per + i) % levels, i * rows) for i in range(per)]


        def split(n):
            todo = [(f, l, start, g) for f, l, start in members(n) for g in range(rows // 16)]
            for i in range(0, len(todo), SPLIT_BATCH):
                batch = todo[i : i + SPLIT_BATCH]
                found = [forward(own_tiles(f, l, rows_at(16 * g, 16)), chunk, twiddle) for f, l, _, g in batch]
                for (f, l, start, g), parts in zip(batch, found):
                    put_parts(y.at[n], pl.ds(start + 16 * g, 16), parts)

        def join(n):
            todo = [(f, l, start, g) for f, l, start in members(n) for g in range(rows // 8)]
            for i in range(0, len(todo), JOIN_BATCH):
                batch = todo[i : i + JOIN_BATCH]
                found = [backward(z.at[n], rows_at(start + 8 * g), chunk, twiddle) for _, _, start, g in batch]
                for (f, l, _, g), v in zip(batch, found):
                    for j in range(tiles):
                        out[f, l, j, rows_at(1 + 8 * g), :] = v[j]

        split(0)
        for n in range(units):
            low_pass(lon, y.at[n], z.at[n], tables, wide)
            if n + 1 < units:
                split(n + 1)
            if n > 0:
                join(n - 1)
        join(units - 1)

    at = pl.ds(1, rows)
    for j in range(tiles):
        column[j, at, :] = functools.reduce(jnp.add, [out[2, l, j, at, :] for l in range(levels)])


def filtered_fields(winds, thick, cut, tables, twiddle):
    levels, rows, lon = thick.shape
    tiles = -(-lon // LANES)
    assert lon % RADIX == 0 and lon // RADIX <= LANES and tiles == RADIX
    assert rows % 16 == 0 and levels % 2 == 0
    classes = RADIX // 2 + 1
    per = 2
    units = 3 * levels // per
    vmem = pl.BlockSpec(memory_space=pltpu.VMEM)
    hbm = pl.BlockSpec(memory_space=pltpu.HBM)
    return pl.pallas_call(
        filter_kernel,
        out_shape=[
            pltpu.VMEM((3, levels, tiles, rows + 8, LANES), f32),
            pltpu.VMEM((tiles, rows + 8, LANES), f32),
        ],
        in_specs=[vmem] * 5,
        out_specs=[vmem] * 2,
        scratch_shapes=[
            pltpu.VMEM((units, classes, per * rows, 2 * WIDE), bf16),
            pltpu.VMEM((units, classes, per * rows, WIDE), f32),
        ],
        compiler_params=pltpu.CompilerParams(vmem_limit_bytes=24 << 20),
        cost_estimate=pl.CostEstimate(flops=10_000_000_000, bytes_accessed=8_000_000, transcendentals=0),
        name="filter",
    )(in_vmem(winds), in_vmem(thick), in_vmem(tables), in_vmem(twiddle), cut)


def halo_kernel(lon, lat_count, got_a, got_b, tables, twiddle, _fields, _column, out, column, y, z):
    levels, tiles, rows = out.shape[1], out.shape[2], out.shape[3] - 8
    chunk = lon // RADIX
    tail = lon - (tiles - 1) * LANES
    place = lax.axis_index("lat")
    odd = place % 2
    refs = (got_a, got_b)
    at = (jnp.where(odd == 1, 0, rows + 1), jnp.where(odd == 1, rows + 1, 0))
    keep = jnp.concatenate([ref[rows_at(2 * levels * (tiles - 1), 2 * levels), :] for ref in refs], axis=0)
    keep = jnp.where(lane_index(16) < tail, rolled(keep, tail), keep)

    def edge_tiles(ref):
        v = [ref[rows_at(2 * levels * j, 2 * levels), :] for j in range(tiles)]
        return v[:-1] + [jnp.where(lane_index() < tail, v[-1], 0.0)]

    def put(side, v):
        end = jnp.where(at[side] == 0, place == 0, place == lat_count - 1)
        for j in range(tiles):
            value = jnp.where(end, 0.0, v[j])
            for f in range(2):
                lines = [value[f * levels + l : f * levels + l + 1] for l in range(levels)]
                for l in range(levels):
                    out[1 + f, l, j, pl.ds(at[side], 1), :] = lines[l]
            column[j, pl.ds(at[side], 1), :] = functools.reduce(jnp.add, lines)

    filtering = jnp.min(keep) < lon // 2

    @pl.when(jnp.logical_not(filtering))
    def _():
        for side in range(2):
            put(side, extended(edge_tiles(refs[side]), tail))

    @pl.when(filtering)
    def _():
        both = [jnp.concatenate(pair, axis=0) for pair in zip(edge_tiles(got_a), edge_tiles(got_b))]
        put_parts(y, pl.ds(0, 16), forward(both, chunk, twiddle))
        wide = jnp.concatenate([keep, keep], axis=1)
        low_pass(lon, y, z, tables, wide)
        for side in range(2):
            put(side, backward(z, rows_at(8 * side), chunk, twiddle))


def with_halo(fields, column, tables, twiddle, got_a, got_b, lon, lat_count):
    assert 2 * fields.shape[1] == 8
    classes = RADIX // 2 + 1
    vmem = pl.BlockSpec(memory_space=pltpu.VMEM)
    return pl.pallas_call(
        functools.partial(halo_kernel, lon, lat_count),
        out_shape=[pltpu.VMEM(fields.shape, f32), pltpu.VMEM(column.shape, f32)],
        in_specs=[vmem] * 6,
        out_specs=[vmem] * 2,
        scratch_shapes=[pltpu.VMEM((classes, 16, 2 * WIDE), bf16), pltpu.VMEM((classes, 16, WIDE), f32)],
        input_output_aliases={4: 0, 5: 1},
        compiler_params=pltpu.CompilerParams(vmem_limit_bytes=24 << 20),
        name="halo",
    )(got_a, got_b, tables, twiddle, fields, column)


def east(v):
    lane = lane_index()
    r = [rolled(a, 1) for a in v]
    return [jnp.where(lane < LANES - 1, a, b) for a, b in zip(r[:-1], r[1:])] + [r[-1]]


def west(v, tail):
    lane = lane_index()
    r = [rolled(a, -1) for a in v]
    r_before = [rolled(v[-1], tail - 1)] + r[:-1]
    return [jnp.where(lane > 0, a, b) for a, b in zip(r, r_before)]


def thickness_kernel(lon, fields, trig, thick):
    levels, tiles = fields.shape[1:3]
    rows = trig.shape[1]
    tail = lon - (tiles - 1) * LANES
    for g in range(rows // 8):
        at = rows_at(8 * g)
        up, here, down = 8 * g, 8 * g + 1, 8 * g + 2
        south, north = trig[2, at, :], trig[3, at, :]
        for start in range(0, levels, LEVEL_BATCH):
            found = {}
            for l in range(start, min(start + LEVEL_BATCH, levels)):
                u, h = ([fields[f, l, j, rows_at(here), :] for j in range(tiles)] for f in (0, 2))
                he, ue = east(h), east(u)
                flux = [(h[j] + he[j]) * (u[j] + ue[j]) for j in range(tiles)]
                flux_west = west(flux, tail)
                for j in range(tiles):
                    v_up, v, v_down = (fields[1, l, j, rows_at(r), :] for r in (up, here, down))
                    h_up, h_down = (fields[2, l, j, rows_at(r), :] for r in (up, down))
                    merid = (h[j] + h_down) * (v + v_down) * north - (h_up + h[j]) * (v_up + v) * south
                    found[l, j] = h[j] - (0.25 * time_step) * (flux[j] - flux_west[j] + merid)
            for (l, j), new in found.items():
                wide = LANES if j < tiles - 1 else tail
                thick[l, at, pl.ds(LANES * j, wide)] = new[:, :wide]


def winds_kernel(lon, fields, trig, thick, *refs):
    *hops, winds_hbm, thick_hbm, winds, sem = refs
    levels, tiles = fields.shape[1:3]
    rows = trig.shape[1]
    tail = lon - (tiles - 1) * LANES
    place = lax.axis_index("lev")
    masks = [jnp.where(place + k + 1 <= len(hops), 1.0, 0.0) for k in range(len(hops))]
    copies = [pltpu.make_async_copy(thick, thick_hbm, sem.at[rows // 8])]
    copies[0].start()

    def below(j, at):
        terms = [ref[j, rows_at(at), :] * mask for ref, mask in zip(hops, masks)]
        return functools.reduce(jnp.add, terms) if terms else jnp.zeros((8, LANES), f32)

    for g in range(rows // 8):
        at = rows_at(8 * g)
        up, here, down = 8 * g, 8 * g + 1, 8 * g + 2
        sine, cosine = trig[0, at, :], trig[1, at, :]
        s = [below(j, here) for j in range(tiles)]
        sum_x = [a - b for a, b in zip(east(s), west(s, tail))]
        sum_y = [below(j, down) - below(j, up) for j in range(tiles)]
        found = {}
        for l in reversed(range(levels)):
            h = [fields[2, l, j, rows_at(here), :] for j in range(tiles)]
            he, hw = east(h), west(h, tail)
            for j in range(tiles):
                u, v = (fields[f, l, j, rows_at(here), :] for f in range(2))
                dx = he[j] - hw[j]
                dy = fields[2, l, j, rows_at(down), :] - fields[2, l, j, rows_at(up), :]
                new_u = u - time_step * (0.5 * (sum_x[j] + 0.5 * dx) - coriolis * sine * v)
                new_v = v - time_step * (0.5 * cosine * (sum_y[j] + 0.5 * dy) + coriolis * sine * u)
                sum_x[j] = sum_x[j] + dx
                sum_y[j] = sum_y[j] + dy
                found[l, j] = (new_u, new_v)
            if l % LEVEL_BATCH == 0:
                for (m, j), pair in found.items():
                    wide = LANES if j < tiles - 1 else tail
                    for f in range(2):
                        winds[f, m, at, pl.ds(LANES * j, wide)] = pair[f][:, :wide]
                found = {}
        copies.append(pltpu.make_async_copy(winds.at[:, :, at], winds_hbm.at[:, :, at], sem.at[g]))
        copies[-1].start()
    for copy in copies:
        copy.wait()


def stepped_thickness(fields, trig, shape, lon):
    vmem = pl.BlockSpec(memory_space=pltpu.VMEM)
    return pl.pallas_call(
        functools.partial(thickness_kernel, lon),
        out_shape=pltpu.VMEM(shape, f32),
        in_specs=[vmem] * 2,
        out_specs=vmem,
        compiler_params=pltpu.CompilerParams(vmem_limit_bytes=24 << 20),
        cost_estimate=pl.CostEstimate(flops=4_000_000_000, bytes_accessed=4_000_000, transcendentals=0),
        name="thickness",
    )(fields, trig)


def stepped_winds(fields, trig, thick, hops, shape, lon):
    hbm = pl.BlockSpec(memory_space=pltpu.HBM)
    return pl.pallas_call(
        functools.partial(winds_kernel, lon),
        out_shape=[jax.ShapeDtypeStruct(shape, f32), jax.ShapeDtypeStruct(thick.shape, f32)],
        in_specs=[pl.BlockSpec(memory_space=pltpu.VMEM)] * (3 + len(hops)),
        out_specs=[hbm, hbm],
        scratch_shapes=[pltpu.VMEM(shape, f32), pltpu.SemaphoreType.DMA((trig.shape[1] // 8 + 1,))],
        compiler_params=pltpu.CompilerParams(vmem_limit_bytes=24 << 20),
        name="winds",
    )(fields, trig, thick, *hops)


def swaps(lat_count, lev_count, first):
    pairs = []
    for i in range(lat_count):
        other = i + 1 if (i - first) % 2 == 0 else i - 1
        for l in range(lev_count):
            if 0 <= other < lat_count:
                pairs.append((i * lev_count + l, other * lev_count + l))
            else:
                pairs.append((i * lev_count + l, i * lev_count + (l + 1) % lev_count))
    return pairs


def per_device(winds, thick, cutoff):
    lat_count, lev_count = lax.axis_size("lat"), lax.axis_size("lev")
    lon = thick.shape[-1]
    sent_a, sent_b, trig, cut = edges(winds, thick, cutoff, lat_count)
    got_a = lax.ppermute(sent_a, ("lat", "lev"), swaps(lat_count, lev_count, 0))
    got_b = lax.ppermute(sent_b, ("lat", "lev"), swaps(lat_count, lev_count, 1))
    tables, twiddle = (jnp.asarray(constant) for constant in filter_tables(lon))
    fields, column = filtered_fields(winds, thick, cut, tables, twiddle)
    fields, column = with_halo(fields, column, tables, twiddle, got_a, got_b, lon, lat_count)
    hops = [
        lax.ppermute(column, "lev", [(i, (i - hop) % lev_count) for i in range(lev_count)])
        for hop in range(1, lev_count)
    ]
    new_thick = stepped_thickness(fields, trig, thick.shape, lon)
    return tuple(stepped_winds(fields, trig, new_thick, hops, winds.shape, lon))


def solution(mesh):
    return jax.shard_map(
        per_device,
        mesh=mesh,
        in_specs=(P(None, "lev", "lat", None), P("lev", "lat", None), P("lat")),
        out_specs=(P(None, "lev", "lat", None), P("lev", "lat", None)),
        check_vma=False,
    )
```

```python
import functools
import math

import jax
import jax.numpy as jnp
import ml_dtypes
import numpy as np
from jax import lax
from jax.experimental import pallas as pl
from jax.experimental.pallas import tpu as pltpu
from jax.sharding import PartitionSpec as P

time_step = 0.2
coriolis = 1.0
RADIX = 12
LANES = 128
WIDE = 2 * LANES
HALF_ROOT3 = math.sqrt(3.0) / 2.0
SPLIT_BATCH = 2
JOIN_BATCH = 4
LEVEL_BATCH = 4
f32 = jnp.float32
bf16 = jnp.bfloat16


def filter_tables(lon):
    chunk, half = lon // RADIX, RADIX // 2
    point = np.arange(chunk)
    angle = 2.0 * math.pi * (np.outer(point, point) % chunk) / chunk
    table = np.zeros((WIDE, WIDE), np.float64)
    near, far = slice(0, chunk), slice(LANES, LANES + chunk)
    table[near, near], table[near, far] = np.cos(angle), np.sin(angle)
    table[far, near], table[far, far] = np.sin(angle), -np.cos(angle)
    table /= math.sqrt(lon)
    high = table.astype(np.float32).astype(ml_dtypes.bfloat16)
    low = (table - high.astype(np.float64)).astype(np.float32).astype(ml_dtypes.bfloat16)
    twiddle = np.zeros((2, 2, 8, LANES), np.float64)
    for k in range(1, half + 1):
        turn = 2.0 * math.pi * (k * point % lon) / lon
        for way, scale in enumerate((1.0, 1.0 if k == half else 2.0)):
            twiddle[way, 0, k, :chunk] = scale * np.cos(turn)
            twiddle[way, 1, k, :chunk] = scale * np.sin(turn)
    return np.stack([high, low]), twiddle.astype(np.float32)


def split_radix(c):
    s = [c[j] + c[j + 6] for j in range(6)]
    d = [c[j] - c[j + 6] for j in range(6)]
    t = [s[j] + s[j + 3] for j in range(3)]
    e = [s[j] - s[j + 3] for j in range(3)]
    t12 = t[1] + t[2]
    e12 = e[1] - e[2]
    y0 = t[0] + t12
    y4 = (t[0] - 0.5 * t12, HALF_ROOT3 * (t[2] - t[1]))
    y6 = e[0] - e12
    y2 = (e[0] + 0.5 * e12, -HALF_ROOT3 * (e[1] + e[2]))
    p, q = d[1] - d[5], d[2] - d[4]
    r, w = d[1] + d[5], d[2] + d[4]
    y3 = (d[0] - q, d[3] - r)
    u, v = d[0] + 0.5 * q, -0.5 * r - d[3]
    sp, sw = HALF_ROOT3 * p, HALF_ROOT3 * w
    y1 = (u + sp, v - sw)
    y5 = (u - sp, v + sw)
    return [(y0, y6), y1, y2, y3, y4, y5]


def join_radix(z):
    (z0, z6), (r1, i1), (r2, i2), (r3, i3), (r4, i4), (r5, i5) = z
    hp, sp = z0 - 0.5 * r4, HALF_ROOT3 * i4
    p = [z0 + r4, hp - sp, hp + sp]
    hq, sq = z6 - 0.5 * r2, HALF_ROOT3 * i2
    q = [z6 + r2, -hq - sq, hq - sq]
    e = [p[j] + q[j] for j in range(3)] + [p[j] - q[j] for j in range(3)]
    a, b, c, d = r1 + r5, HALF_ROOT3 * (r1 - r5), i1 + i5, HALF_ROOT3 * (i1 - i5)
    g = r3 - 0.5 * a
    f = -0.5 * c - i3
    o = [a + r3, b + f, -g - d, i3 - c, g - d, f - b]
    return [e[j] + o[j] for j in range(6)] + [e[j] - o[j] for j in range(6)]


def rolled(x, left):
    shift = (-left) % LANES
    return x if shift == 0 else pltpu.roll(x, shift, 1)


def lane_index(rows=8):
    return lax.broadcasted_iota(jnp.int32, (rows, LANES), 1)


def two_parts(x):
    high = x.astype(bf16)
    return high, (x - high.astype(f32)).astype(bf16)


def rows_at(start, size=8):
    return pl.ds(start, size)


def edge_kernel(lat_count, winds, thick, cutoff_hbm, sent_a, sent_b, trig, cut, v, h, cutoff, sem):
    levels, lon = v.shape[1:]
    rows = thick.shape[1]
    tiles = -(-lon // LANES)
    tail = lon - (tiles - 1) * LANES
    copies = [pltpu.make_async_copy(cutoff_hbm, cutoff, sem.at[4])]
    for side, start in enumerate((0, rows - 1)):
        copies.append(pltpu.make_async_copy(winds.at[1, :, start], v.at[side], sem.at[2 * side]))
        copies.append(pltpu.make_async_copy(thick.at[:, start], h.at[side], sem.at[2 * side + 1]))
    for copy in copies:
        copy.start()

    place = lax.axis_index("lat")
    index = (place * rows + lax.broadcasted_iota(jnp.int32, (rows, LANES), 0)).astype(f32)
    step = math.pi / (lat_count * rows)
    centre = (index + 0.5) * step - 0.5 * math.pi
    trig[0] = jnp.sin(centre)
    trig[1] = jnp.cos(centre)
    trig[2] = jnp.sin(index * step)
    trig[3] = jnp.sin((index + 1.0) * step)

    copies[0].wait()
    for r in range(rows):
        cut[pl.ds(r, 1), :] = jnp.full((1, LANES), cutoff[r].astype(f32), f32)
    for copy in copies[1:]:
        copy.wait()
    last_first = 1 - place % 2
    for out, side in ((sent_a, last_first), (sent_b, 1 - last_first)):
        limit = cutoff[side * (rows - 1)].astype(f32)
        for j in range(tiles):
            wide = LANES if j < tiles - 1 else tail
            for f, block in enumerate((v, h)):
                got = block[side, :, pl.ds(LANES * j, wide)]
                if wide < LANES:
                    got = jnp.concatenate([got, jnp.full((levels, LANES - wide), limit, f32)], axis=1)
                out[pl.ds((2 * j + f) * levels, levels), :] = got


def in_vmem(x):
    return pltpu.with_memory_space_constraint(x, pltpu.VMEM)


def in_hbm(x):
    return pltpu.with_memory_space_constraint(x, pltpu.HBM)


def edges(winds, thick, cutoff, lat_count):
    levels, rows, lon = thick.shape
    tiles = -(-lon // LANES)
    vmem = pl.BlockSpec(memory_space=pltpu.VMEM)
    hbm = pl.BlockSpec(memory_space=pltpu.HBM)
    assert lon < tiles * LANES
    edge = pltpu.VMEM((2 * levels * tiles, LANES), f32)
    return pl.pallas_call(
        functools.partial(edge_kernel, lat_count),
        out_shape=[edge, edge, pltpu.VMEM((4, rows, LANES), f32), pltpu.VMEM((rows, LANES), f32)],
        in_specs=[hbm] * 3,
        out_specs=[vmem] * 4,
        scratch_shapes=[
            pltpu.VMEM((2, levels, lon), f32),
            pltpu.VMEM((2, levels, lon), f32),
            pltpu.SMEM((rows,), jnp.int32),
            pltpu.SemaphoreType.DMA((5,)),
        ],
        compiler_params=pltpu.CompilerParams(vmem_limit_bytes=16 << 20),
        cost_estimate=pl.CostEstimate(flops=4_000_000_000, bytes_accessed=8_000_000, transcendentals=0),
        name="edges",
    )(in_hbm(winds), in_hbm(thick), in_hbm(cutoff))


def forward(v, chunk, twiddle):
    gap, half = LANES - chunk, RADIX // 2
    lane = lane_index(v[0].shape[0])
    c = []
    for j in range(RADIX):
        turn = gap * j
        here = jnp.where(lane < LANES - turn, v[j], v[j - 1]) if turn else v[j]
        c.append(rolled(here, -turn))
    c[-1] = jnp.where(lane < chunk, c[-1], 0.0)
    (y0, y6), *pairs = split_radix(c)
    found = []
    for k in range(half + 1):
        cos, sin = twiddle[0, 0, k : k + 1, :], twiddle[0, 1, k : k + 1, :]
        if k == 0:
            both = (y0, jnp.zeros_like(y0))
        elif k == half:
            both = (y6 * cos, -(y6 * sin))
        else:
            re, im = pairs[k - 1]
            both = (re * cos + im * sin, im * cos - re * sin)
        re, im = (two_parts(value) for value in both)
        found.append((re[0], im[0], re[1], im[1]))
    return found


def put_parts(y, at, found):
    for k, parts in enumerate(found):
        for i, part in enumerate(parts):
            y[k, at, LANES * i : LANES * (i + 1)] = part


def three(high, low, tables):
    a = jnp.concatenate([high, low, high], axis=1)
    b = jnp.concatenate([tables[0], tables[0], tables[1]], axis=0)
    return lax.dot_general(a, b, (((1,), (0,)), ((), ())), preferred_element_type=f32)


def low_pass(lon, y, z, tables, keep):
    classes, count = y.shape[:2]
    shape = (classes, count, WIDE)
    both = y[...].reshape(classes * count, 2 * WIDE)
    coeffs = three(both[:, :WIDE], both[:, WIDE:], tables).reshape(shape)
    at = lax.broadcasted_iota(jnp.int32, (1, WIDE), 1)
    at = jnp.where(at < LANES, at, at - LANES)
    masked = []
    for k in range(classes):
        m = RADIX * at + k
        masked.append(jnp.where(jnp.minimum(m, lon - m).astype(f32) <= keep, coeffs[k], 0.0))
    high, low = two_parts(jnp.concatenate(masked, axis=0))
    z[...] = three(high, low, tables).reshape(shape)


def backward(z, at, chunk, twiddle):
    gap, half = LANES - chunk, RADIX // 2
    lane = lane_index()
    pairs = [(z[0, at, :LANES], None)]
    for k in range(1, half + 1):
        re, im = z[k, at, :LANES], z[k, at, LANES:]
        cos, sin = twiddle[1, 0, k : k + 1, :], twiddle[1, 1, k : k + 1, :]
        pairs.append((re * cos - im * sin, re * sin + im * cos if k < half else None))
    c = join_radix([(pairs[0][0], pairs[half][0])] + pairs[1:half])
    c = [rolled(c[j % RADIX], gap * j) for j in range(RADIX + 1)]
    return [jnp.where(lane < LANES - gap * (j + 1), c[j], c[j + 1]) for j in range(RADIX)]


def extended(v, tail):
    return v[:-1] + [jnp.where(lane_index() < tail, v[-1], rolled(v[0], LANES - tail))]


def filter_kernel(winds, thick, tables, twiddle, cut, trig, out, column, new_thick, y, z):
    levels, rows, lon = thick.shape
    tiles = out.shape[2]
    chunk = lon // RADIX
    tail = lon - (tiles - 1) * LANES
    order = (2, 0, 1)
    keep = cut[...]
    filtering = jnp.min(keep) < lon // 2

    def own_tiles(f, l, at):
        block, lead = (winds, (f, l)) if f < 2 else (thick, (l,))
        got = [block[(*lead, at, pl.ds(LANES * j, LANES))] for j in range(tiles - 1)]
        last = block[(*lead, at, pl.ds(LANES * (tiles - 1), tail))]
        return got + [jnp.concatenate([last, jnp.zeros((at.size, LANES - tail), f32)], axis=1)]

    @pl.when(jnp.logical_not(filtering))
    def _():
        for f in order:

            def as_is(l, _, f=f):
                for g in range(rows // 8):
                    v = extended(own_tiles(f, l, rows_at(8 * g)), tail)
                    for j in range(tiles):
                        out[f, l, j, rows_at(1 + 8 * g), :] = v[j]
                return 0

            lax.fori_loop(0, levels, as_is, 0)
        for g in range(1, rows // 8 - 1):
            thickness_rows(g, lon, out, trig, new_thick)

    @pl.when(filtering)
    def _():
        units = y.shape[0]
        per = 3 * levels // units
        wide = jnp.concatenate([jnp.concatenate([keep, keep], axis=1)] * per, axis=0)

        def members(n):
            return [(order[(n * per + i) // levels], (n * per + i) % levels, i * rows) for i in range(per)]


        def split(n):
            todo = [(f, l, start, g) for f, l, start in members(n) for g in range(rows // 16)]
            for i in range(0, len(todo), SPLIT_BATCH):
                batch = todo[i : i + SPLIT_BATCH]
                found = [forward(own_tiles(f, l, rows_at(16 * g, 16)), chunk, twiddle) for f, l, _, g in batch]
                for (f, l, start, g), parts in zip(batch, found):
                    put_parts(y.at[n], pl.ds(start + 16 * g, 16), parts)

        def join(n):
            todo = [(f, l, start, g) for f, l, start in members(n) for g in range(rows // 8)]
            for i in range(0, len(todo), JOIN_BATCH):
                batch = todo[i : i + JOIN_BATCH]
                found = [backward(z.at[n], rows_at(start + 8 * g), chunk, twiddle) for _, _, start, g in batch]
                for (f, l, _, g), v in zip(batch, found):
                    for j in range(tiles):
                        out[f, l, j, rows_at(1 + 8 * g), :] = v[j]

        split(0)
        for n in range(units):
            low_pass(lon, y.at[n], z.at[n], tables, wide)
            if n + 1 < units:
                split(n + 1)
            if n > 0:
                join(n - 1)
        join(units - 1)

    at = pl.ds(1, rows)
    for j in range(tiles):
        column[j, at, :] = functools.reduce(jnp.add, [out[2, l, j, at, :] for l in range(levels)])


def filtered_fields(winds, thick, cut, trig, tables, twiddle):
    levels, rows, lon = thick.shape
    tiles = -(-lon // LANES)
    assert lon % RADIX == 0 and lon // RADIX <= LANES and tiles == RADIX
    assert rows % 16 == 0 and levels % 2 == 0
    classes = RADIX // 2 + 1
    per = 2
    units = 3 * levels // per
    vmem = pl.BlockSpec(memory_space=pltpu.VMEM)
    hbm = pl.BlockSpec(memory_space=pltpu.HBM)
    return pl.pallas_call(
        filter_kernel,
        out_shape=[
            pltpu.VMEM((3, levels, tiles, rows + 8, LANES), f32),
            pltpu.VMEM((tiles, rows + 8, LANES), f32),
            pltpu.VMEM(thick.shape, f32),
        ],
        in_specs=[vmem] * 6,
        out_specs=[vmem] * 3,
        scratch_shapes=[
            pltpu.VMEM((units, classes, per * rows, 2 * WIDE), bf16),
            pltpu.VMEM((units, classes, per * rows, WIDE), f32),
        ],
        compiler_params=pltpu.CompilerParams(vmem_limit_bytes=24 << 20),
        cost_estimate=pl.CostEstimate(flops=10_000_000_000, bytes_accessed=8_000_000, transcendentals=0),
        name="filter",
    )(in_vmem(winds), in_vmem(thick), in_vmem(tables), in_vmem(twiddle), cut, trig)


def halo_kernel(lon, lat_count, got_a, got_b, tables, twiddle, _fields, _column, out, column, y, z):
    levels, tiles, rows = out.shape[1], out.shape[2], out.shape[3] - 8
    chunk = lon // RADIX
    tail = lon - (tiles - 1) * LANES
    place = lax.axis_index("lat")
    odd = place % 2
    refs = (got_a, got_b)
    at = (jnp.where(odd == 1, 0, rows + 1), jnp.where(odd == 1, rows + 1, 0))
    keep = jnp.concatenate([ref[rows_at(2 * levels * (tiles - 1), 2 * levels), :] for ref in refs], axis=0)
    keep = jnp.where(lane_index(16) < tail, rolled(keep, tail), keep)

    def edge_tiles(ref):
        v = [ref[rows_at(2 * levels * j, 2 * levels), :] for j in range(tiles)]
        return v[:-1] + [jnp.where(lane_index() < tail, v[-1], 0.0)]

    def put(side, v):
        end = jnp.where(at[side] == 0, place == 0, place == lat_count - 1)
        for j in range(tiles):
            value = jnp.where(end, 0.0, v[j])
            for f in range(2):
                lines = [value[f * levels + l : f * levels + l + 1] for l in range(levels)]
                for l in range(levels):
                    out[1 + f, l, j, pl.ds(at[side], 1), :] = lines[l]
            column[j, pl.ds(at[side], 1), :] = functools.reduce(jnp.add, lines)

    filtering = jnp.min(keep) < lon // 2

    @pl.when(jnp.logical_not(filtering))
    def _():
        for side in range(2):
            put(side, extended(edge_tiles(refs[side]), tail))

    @pl.when(filtering)
    def _():
        both = [jnp.concatenate(pair, axis=0) for pair in zip(edge_tiles(got_a), edge_tiles(got_b))]
        put_parts(y, pl.ds(0, 16), forward(both, chunk, twiddle))
        wide = jnp.concatenate([keep, keep], axis=1)
        low_pass(lon, y, z, tables, wide)
        for side in range(2):
            put(side, backward(z, rows_at(8 * side), chunk, twiddle))


def with_halo(fields, column, tables, twiddle, got_a, got_b, lon, lat_count):
    assert 2 * fields.shape[1] == 8
    classes = RADIX // 2 + 1
    vmem = pl.BlockSpec(memory_space=pltpu.VMEM)
    return pl.pallas_call(
        functools.partial(halo_kernel, lon, lat_count),
        out_shape=[pltpu.VMEM(fields.shape, f32), pltpu.VMEM(column.shape, f32)],
        in_specs=[vmem] * 6,
        out_specs=[vmem] * 2,
        scratch_shapes=[pltpu.VMEM((classes, 16, 2 * WIDE), bf16), pltpu.VMEM((classes, 16, WIDE), f32)],
        input_output_aliases={4: 0, 5: 1},
        compiler_params=pltpu.CompilerParams(vmem_limit_bytes=24 << 20),
        name="halo",
    )(got_a, got_b, tables, twiddle, fields, column)


def east(v):
    lane = lane_index()
    r = [rolled(a, 1) for a in v]
    return [jnp.where(lane < LANES - 1, a, b) for a, b in zip(r[:-1], r[1:])] + [r[-1]]


def west(v, tail):
    lane = lane_index()
    r = [rolled(a, -1) for a in v]
    r_before = [rolled(v[-1], tail - 1)] + r[:-1]
    return [jnp.where(lane > 0, a, b) for a, b in zip(r, r_before)]


def thickness_rows(g, lon, fields, trig, thick):
    levels, tiles = fields.shape[1:3]
    tail = lon - (tiles - 1) * LANES
    at = rows_at(8 * g)
    up, mid, down = 8 * g, 8 * g + 1, 8 * g + 2
    south, north = trig[2, at, :], trig[3, at, :]
    found = {}
    for l in range(levels):
        u, h = ([fields[f, l, j, rows_at(mid), :] for j in range(tiles)] for f in (0, 2))
        he, ue = east(h), east(u)
        flux = [(h[j] + he[j]) * (u[j] + ue[j]) for j in range(tiles)]
        flux_west = west(flux, tail)
        for j in range(tiles):
            v_up, v, v_down = (fields[1, l, j, rows_at(r), :] for r in (up, mid, down))
            h_up, h_down = (fields[2, l, j, rows_at(r), :] for r in (up, down))
            merid = (h[j] + h_down) * (v + v_down) * north - (h_up + h[j]) * (v_up + v) * south
            found[l, j] = h[j] - (0.25 * time_step) * (flux[j] - flux_west[j] + merid)
    for (l, j), new in found.items():
        wide = LANES if j < tiles - 1 else tail
        thick[l, at, pl.ds(LANES * j, wide)] = new[:, :wide]


def thickness_kernel(lon, fields, trig, cut, _thick, thick):
    groups = trig.shape[1] // 8

    @pl.when(jnp.min(cut[...]) < lon // 2)
    def _():
        for g in range(1, groups - 1):
            thickness_rows(g, lon, fields, trig, thick)

    for g in sorted({0, groups - 1}):
        thickness_rows(g, lon, fields, trig, thick)


def winds_kernel(lon, fields, trig, thick, *refs):
    *hops, winds_hbm, thick_hbm, winds, sem = refs
    levels, tiles = fields.shape[1:3]
    rows = trig.shape[1]
    tail = lon - (tiles - 1) * LANES
    place = lax.axis_index("lev")
    masks = [jnp.where(place + k + 1 <= len(hops), 1.0, 0.0) for k in range(len(hops))]
    copies = [pltpu.make_async_copy(thick, thick_hbm, sem.at[rows // 8])]
    copies[0].start()

    def below(j, at):
        terms = [ref[j, rows_at(at), :] * mask for ref, mask in zip(hops, masks)]
        return functools.reduce(jnp.add, terms) if terms else jnp.zeros((8, LANES), f32)

    for g in range(rows // 8):
        at = rows_at(8 * g)
        up, here, down = 8 * g, 8 * g + 1, 8 * g + 2
        sine, cosine = trig[0, at, :], trig[1, at, :]
        s = [below(j, here) for j in range(tiles)]
        sum_x = [a - b for a, b in zip(east(s), west(s, tail))]
        sum_y = [below(j, down) - below(j, up) for j in range(tiles)]
        found = {}
        for l in reversed(range(levels)):
            h = [fields[2, l, j, rows_at(here), :] for j in range(tiles)]
            he, hw = east(h), west(h, tail)
            for j in range(tiles):
                u, v = (fields[f, l, j, rows_at(here), :] for f in range(2))
                dx = he[j] - hw[j]
                dy = fields[2, l, j, rows_at(down), :] - fields[2, l, j, rows_at(up), :]
                new_u = u - time_step * (0.5 * (sum_x[j] + 0.5 * dx) - coriolis * sine * v)
                new_v = v - time_step * (0.5 * cosine * (sum_y[j] + 0.5 * dy) + coriolis * sine * u)
                sum_x[j] = sum_x[j] + dx
                sum_y[j] = sum_y[j] + dy
                found[l, j] = (new_u, new_v)
            if l % LEVEL_BATCH == 0:
                for (m, j), pair in found.items():
                    wide = LANES if j < tiles - 1 else tail
                    for f in range(2):
                        winds[f, m, at, pl.ds(LANES * j, wide)] = pair[f][:, :wide]
                found = {}
        copies.append(pltpu.make_async_copy(winds.at[:, :, at], winds_hbm.at[:, :, at], sem.at[g]))
        copies[-1].start()
    for copy in copies:
        copy.wait()


def stepped_thickness(fields, trig, cut, thick, lon):
    vmem = pl.BlockSpec(memory_space=pltpu.VMEM)
    return pl.pallas_call(
        functools.partial(thickness_kernel, lon),
        out_shape=pltpu.VMEM(thick.shape, f32),
        in_specs=[vmem] * 4,
        out_specs=vmem,
        input_output_aliases={3: 0},
        compiler_params=pltpu.CompilerParams(vmem_limit_bytes=24 << 20),
        cost_estimate=pl.CostEstimate(flops=4_000_000_000, bytes_accessed=4_000_000, transcendentals=0),
        name="thickness",
    )(fields, trig, cut, thick)


def stepped_winds(fields, trig, thick, hops, shape, lon):
    hbm = pl.BlockSpec(memory_space=pltpu.HBM)
    return pl.pallas_call(
        functools.partial(winds_kernel, lon),
        out_shape=[jax.ShapeDtypeStruct(shape, f32), jax.ShapeDtypeStruct(thick.shape, f32)],
        in_specs=[pl.BlockSpec(memory_space=pltpu.VMEM)] * (3 + len(hops)),
        out_specs=[hbm, hbm],
        scratch_shapes=[pltpu.VMEM(shape, f32), pltpu.SemaphoreType.DMA((trig.shape[1] // 8 + 1,))],
        compiler_params=pltpu.CompilerParams(vmem_limit_bytes=24 << 20),
        name="winds",
    )(fields, trig, thick, *hops)


def swaps(lat_count, lev_count, first):
    pairs = []
    for i in range(lat_count):
        other = i + 1 if (i - first) % 2 == 0 else i - 1
        for l in range(lev_count):
            if 0 <= other < lat_count:
                pairs.append((i * lev_count + l, other * lev_count + l))
            else:
                pairs.append((i * lev_count + l, i * lev_count + (l + 1) % lev_count))
    return pairs


def per_device(winds, thick, cutoff):
    lat_count, lev_count = lax.axis_size("lat"), lax.axis_size("lev")
    lon = thick.shape[-1]
    sent_a, sent_b, trig, cut = edges(winds, thick, cutoff, lat_count)
    got_a = lax.ppermute(sent_a, ("lat", "lev"), swaps(lat_count, lev_count, 0))
    got_b = lax.ppermute(sent_b, ("lat", "lev"), swaps(lat_count, lev_count, 1))
    tables, twiddle = (jnp.asarray(constant) for constant in filter_tables(lon))
    fields, column, new_thick = filtered_fields(winds, thick, cut, trig, tables, twiddle)
    fields, column = with_halo(fields, column, tables, twiddle, got_a, got_b, lon, lat_count)
    hops = [
        lax.ppermute(column, "lev", [(i, (i - hop) % lev_count) for i in range(lev_count)])
        for hop in range(1, lev_count)
    ]
    new_thick = stepped_thickness(fields, trig, cut, new_thick, lon)
    return tuple(stepped_winds(fields, trig, new_thick, hops, winds.shape, lon))


def solution(mesh):
    return jax.shard_map(
        per_device,
        mesh=mesh,
        in_specs=(P(None, "lev", "lat", None), P("lev", "lat", None), P("lat")),
        out_specs=(P(None, "lev", "lat", None), P("lev", "lat", None)),
        check_vma=False,
    )
```

```python
import functools
import math

import jax
import jax.numpy as jnp
import ml_dtypes
import numpy as np
from jax import lax
from jax.experimental import pallas as pl
from jax.experimental.pallas import tpu as pltpu
from jax.sharding import PartitionSpec as P

time_step = 0.2
coriolis = 1.0
RADIX = 12
LANES = 128
WIDE = 2 * LANES
HALF_ROOT3 = math.sqrt(3.0) / 2.0
LEVEL_BATCH = 4
f32 = jnp.float32
bf16 = jnp.bfloat16


def filter_tables(lon):
    chunk, half = lon // RADIX, RADIX // 2
    point = np.arange(chunk)
    angle = 2.0 * math.pi * (np.outer(point, point) % chunk) / chunk
    table = np.zeros((WIDE, WIDE), np.float64)
    near, far = slice(0, chunk), slice(LANES, LANES + chunk)
    table[near, near], table[near, far] = np.cos(angle), np.sin(angle)
    table[far, near], table[far, far] = np.sin(angle), -np.cos(angle)
    table /= math.sqrt(lon)
    high = table.astype(np.float32).astype(ml_dtypes.bfloat16)
    low = (table - high.astype(np.float64)).astype(np.float32).astype(ml_dtypes.bfloat16)
    twiddle = np.zeros((2, 2, 8, LANES), np.float64)
    for k in range(1, half + 1):
        turn = 2.0 * math.pi * (k * point % lon) / lon
        for way, scale in enumerate((1.0, 1.0 if k == half else 2.0)):
            twiddle[way, 0, k, :chunk] = scale * np.cos(turn)
            twiddle[way, 1, k, :chunk] = scale * np.sin(turn)
    return np.stack([high, low]), twiddle.astype(np.float32)


def split_radix(c):
    s = [c[j] + c[j + 6] for j in range(6)]
    d = [c[j] - c[j + 6] for j in range(6)]
    t = [s[j] + s[j + 3] for j in range(3)]
    e = [s[j] - s[j + 3] for j in range(3)]
    t12 = t[1] + t[2]
    e12 = e[1] - e[2]
    y0 = t[0] + t12
    y4 = (t[0] - 0.5 * t12, HALF_ROOT3 * (t[2] - t[1]))
    y6 = e[0] - e12
    y2 = (e[0] + 0.5 * e12, -HALF_ROOT3 * (e[1] + e[2]))
    p, q = d[1] - d[5], d[2] - d[4]
    r, w = d[1] + d[5], d[2] + d[4]
    y3 = (d[0] - q, d[3] - r)
    u, v = d[0] + 0.5 * q, -0.5 * r - d[3]
    sp, sw = HALF_ROOT3 * p, HALF_ROOT3 * w
    y1 = (u + sp, v - sw)
    y5 = (u - sp, v + sw)
    return [(y0, y6), y1, y2, y3, y4, y5]


def join_radix(z):
    (z0, z6), (r1, i1), (r2, i2), (r3, i3), (r4, i4), (r5, i5) = z
    hp, sp = z0 - 0.5 * r4, HALF_ROOT3 * i4
    p = [z0 + r4, hp - sp, hp + sp]
    hq, sq = z6 - 0.5 * r2, HALF_ROOT3 * i2
    q = [z6 + r2, -hq - sq, hq - sq]
    e = [p[j] + q[j] for j in range(3)] + [p[j] - q[j] for j in range(3)]
    a, b, c, d = r1 + r5, HALF_ROOT3 * (r1 - r5), i1 + i5, HALF_ROOT3 * (i1 - i5)
    g = r3 - 0.5 * a
    f = -0.5 * c - i3
    o = [a + r3, b + f, -g - d, i3 - c, g - d, f - b]
    return [e[j] + o[j] for j in range(6)] + [e[j] - o[j] for j in range(6)]


def rolled(x, left):
    shift = (-left) % LANES
    return x if shift == 0 else pltpu.roll(x, shift, 1)


def lane_index(rows=8):
    return lax.broadcasted_iota(jnp.int32, (rows, LANES), 1)


def two_parts(x):
    high = x.astype(bf16)
    return high, (x - high.astype(f32)).astype(bf16)


def rows_at(start, size=8):
    return pl.ds(start, size)


def edge_kernel(lat_count, winds, thick, cutoff_hbm, sent_a, sent_b, trig, cut, v, h, cutoff, sem):
    levels, lon = v.shape[1:]
    rows = thick.shape[1]
    tiles = -(-lon // LANES)
    tail = lon - (tiles - 1) * LANES
    copies = [pltpu.make_async_copy(cutoff_hbm, cutoff, sem.at[4])]
    for side, start in enumerate((0, rows - 1)):
        copies.append(pltpu.make_async_copy(winds.at[1, :, start], v.at[side], sem.at[2 * side]))
        copies.append(pltpu.make_async_copy(thick.at[:, start], h.at[side], sem.at[2 * side + 1]))
    for copy in copies:
        copy.start()

    place = lax.axis_index("lat")
    index = (place * rows + lax.broadcasted_iota(jnp.int32, (rows, LANES), 0)).astype(f32)
    step = math.pi / (lat_count * rows)
    centre = (index + 0.5) * step - 0.5 * math.pi
    trig[0] = jnp.sin(centre)
    trig[1] = jnp.cos(centre)
    trig[2] = jnp.sin(index * step)
    trig[3] = jnp.sin((index + 1.0) * step)

    copies[0].wait()
    for r in range(rows):
        cut[pl.ds(r, 1), :] = jnp.full((1, LANES), cutoff[r].astype(f32), f32)
    for copy in copies[1:]:
        copy.wait()
    last_first = 1 - place % 2
    for out, side in ((sent_a, last_first), (sent_b, 1 - last_first)):
        limit = cutoff[side * (rows - 1)].astype(f32)
        for j in range(tiles):
            wide = LANES if j < tiles - 1 else tail
            for f, block in enumerate((v, h)):
                got = block[side, :, pl.ds(LANES * j, wide)]
                if wide < LANES:
                    got = jnp.concatenate([got, jnp.full((levels, LANES - wide), limit, f32)], axis=1)
                out[pl.ds((2 * j + f) * levels, levels), :] = got


def in_vmem(x):
    return pltpu.with_memory_space_constraint(x, pltpu.VMEM)


def in_hbm(x):
    return pltpu.with_memory_space_constraint(x, pltpu.HBM)


def edges(winds, thick, cutoff, lat_count):
    levels, rows, lon = thick.shape
    tiles = -(-lon // LANES)
    vmem = pl.BlockSpec(memory_space=pltpu.VMEM)
    hbm = pl.BlockSpec(memory_space=pltpu.HBM)
    assert lon < tiles * LANES
    edge = pltpu.VMEM((2 * levels * tiles, LANES), f32)
    return pl.pallas_call(
        functools.partial(edge_kernel, lat_count),
        out_shape=[edge, edge, pltpu.VMEM((4, rows, LANES), f32), pltpu.VMEM((rows, LANES), f32)],
        in_specs=[hbm] * 3,
        out_specs=[vmem] * 4,
        scratch_shapes=[
            pltpu.VMEM((2, levels, lon), f32),
            pltpu.VMEM((2, levels, lon), f32),
            pltpu.SMEM((rows,), jnp.int32),
            pltpu.SemaphoreType.DMA((5,)),
        ],
        compiler_params=pltpu.CompilerParams(vmem_limit_bytes=16 << 20),
        cost_estimate=pl.CostEstimate(flops=4_000_000_000, bytes_accessed=8_000_000, transcendentals=0),
        name="edges",
    )(in_hbm(winds), in_hbm(thick), in_hbm(cutoff))


def forward(v, chunk, twiddle):
    gap, half = LANES - chunk, RADIX // 2
    lane = lane_index(v[0].shape[0])
    c = []
    for j in range(RADIX):
        turn = gap * j
        here = jnp.where(lane < LANES - turn, v[j], v[j - 1]) if turn else v[j]
        c.append(rolled(here, -turn))
    c[-1] = jnp.where(lane < chunk, c[-1], 0.0)
    (y0, y6), *pairs = split_radix(c)
    found = []
    for k in range(half + 1):
        cos, sin = twiddle[0, 0, k : k + 1, :], twiddle[0, 1, k : k + 1, :]
        if k == 0:
            both = (y0, jnp.zeros_like(y0))
        elif k == half:
            both = (y6 * cos, -(y6 * sin))
        else:
            re, im = pairs[k - 1]
            both = (re * cos + im * sin, im * cos - re * sin)
        re, im = (two_parts(value) for value in both)
        found.append((re[0], im[0], re[1], im[1]))
    return found


def put_parts(y, at, found):
    for k, parts in enumerate(found):
        for i, part in enumerate(parts):
            y[k, at, LANES * i : LANES * (i + 1)] = part


def three(high, low, tables):
    a = jnp.concatenate([high, low, high], axis=1)
    b = jnp.concatenate([tables[0], tables[0], tables[1]], axis=0)
    return lax.dot_general(a, b, (((1,), (0,)), ((), ())), preferred_element_type=f32)


def products(y, tables):
    classes, count = y.shape[:2]
    both = y[...].reshape(classes * count, 2 * WIDE)
    return three(both[:, :WIDE], both[:, WIDE:], tables).reshape(classes, count, WIDE)


def masked_parts(lon, coeffs, keep):
    at = lax.broadcasted_iota(jnp.int32, (1, WIDE), 1)
    at = jnp.where(at < LANES, at, at - LANES)
    found = []
    for k in range(coeffs.shape[0]):
        m = RADIX * at + k
        inside = jnp.minimum(m, lon - m).astype(f32) <= keep
        found.append(two_parts(jnp.where(inside, coeffs[k], 0.0)))
    return found


def put_masked(y, found):
    for k, parts in enumerate(found):
        for i, part in enumerate(parts):
            y[k, :, WIDE * i : WIDE * (i + 1)] = part


def backward(z, at, chunk, twiddle):
    gap, half = LANES - chunk, RADIX // 2
    lane = lane_index()
    pairs = [(z[0, at, :LANES], None)]
    for k in range(1, half + 1):
        re, im = z[k, at, :LANES], z[k, at, LANES:]
        cos, sin = twiddle[1, 0, k : k + 1, :], twiddle[1, 1, k : k + 1, :]
        pairs.append((re * cos - im * sin, re * sin + im * cos if k < half else None))
    c = join_radix([(pairs[0][0], pairs[half][0])] + pairs[1:half])
    c = [rolled(c[j % RADIX], gap * j) for j in range(RADIX + 1)]
    return [jnp.where(lane < LANES - gap * (j + 1), c[j], c[j + 1]) for j in range(RADIX)]


def extended(v, tail):
    return v[:-1] + [jnp.where(lane_index() < tail, v[-1], rolled(v[0], LANES - tail))]


def filter_kernel(winds, thick, tables, twiddle, cut, trig, out, column, new_thick, y, z):
    levels, rows, lon = thick.shape
    tiles = out.shape[2]
    chunk = lon // RADIX
    tail = lon - (tiles - 1) * LANES
    order = (2, 0, 1)
    keep = cut[...]
    filtering = jnp.min(keep) < lon // 2

    def own_tiles(f, l, at):
        block, lead = (winds, (f, l)) if f < 2 else (thick, (l,))
        got = [block[(*lead, at, pl.ds(LANES * j, LANES))] for j in range(tiles - 1)]
        last = block[(*lead, at, pl.ds(LANES * (tiles - 1), tail))]
        return got + [jnp.concatenate([last, jnp.zeros((at.size, LANES - tail), f32)], axis=1)]

    @pl.when(jnp.logical_not(filtering))
    def _():
        for f in order:

            def as_is(l, _, f=f):
                for g in range(rows // 8):
                    v = extended(own_tiles(f, l, rows_at(8 * g)), tail)
                    for j in range(tiles):
                        out[f, l, j, rows_at(1 + 8 * g), :] = v[j]
                return 0

            lax.fori_loop(0, levels, as_is, 0)
        for g in range(1, rows // 8 - 1):
            thickness_rows(g, lon, out, None, trig, new_thick)

    @pl.when(filtering)
    def _():
        units = y.shape[0]
        per = 3 * levels // units
        wide = jnp.concatenate([jnp.concatenate([keep, keep], axis=1)] * per, axis=0)

        def members(n):
            return [(order[(n * per + i) // levels], (n * per + i) % levels, i * rows) for i in range(per)]


        def split(n):
            found = []
            for f, l, start in members(n):
                for g in range(rows // 16):
                    parts = forward(own_tiles(f, l, rows_at(16 * g, 16)), chunk, twiddle)
                    found.append((pl.ds(start + 16 * g, 16), parts))
            return found

        def join(n):
            found = []
            for f, l, start in members(n):
                for g in range(rows // 8):
                    found.append((f, l, g, backward(z.at[n], rows_at(start + 8 * g), chunk, twiddle)))
            return found

        for n in range(-1, units + 2):
            coeffs = products(y.at[n], tables) if 0 <= n < units else None
            back = products(y.at[n - 1], tables) if 1 <= n <= units else None
            ahead = split(n + 1) if n + 1 < units else []
            behind = join(n - 2) if n >= 2 else []
            masked = masked_parts(lon, coeffs, wide) if 0 <= n < units else []
            put_masked(y.at[n], masked)
            if back is not None:
                z[n - 1] = back
            for at, parts in ahead:
                put_parts(y.at[n + 1], at, parts)
            for f, l, g, v in behind:
                for j in range(tiles):
                    out[f, l, j, rows_at(1 + 8 * g), :] = v[j]

    for j in range(tiles):
        lines = [out[2, l, j, pl.ds(1, rows), :] for l in range(levels)]
        column[j, pl.ds(0, rows), :] = functools.reduce(jnp.add, lines)


def filtered_fields(winds, thick, cut, trig, tables, twiddle):
    levels, rows, lon = thick.shape
    tiles = -(-lon // LANES)
    assert lon % RADIX == 0 and lon // RADIX <= LANES and tiles == RADIX
    assert rows % 16 == 0 and levels % 2 == 0
    classes = RADIX // 2 + 1
    per = 1
    units = 3 * levels // per
    vmem = pl.BlockSpec(memory_space=pltpu.VMEM)
    hbm = pl.BlockSpec(memory_space=pltpu.HBM)
    return pl.pallas_call(
        filter_kernel,
        out_shape=[
            pltpu.VMEM((3, levels, tiles, rows + 8, LANES), f32),
            pltpu.VMEM((tiles, rows + 8, LANES), f32),
            pltpu.VMEM(thick.shape, f32),
        ],
        in_specs=[vmem] * 6,
        out_specs=[vmem] * 3,
        scratch_shapes=[
            pltpu.VMEM((units, classes, per * rows, 2 * WIDE), bf16),
            pltpu.VMEM((units, classes, per * rows, WIDE), f32),
        ],
        compiler_params=pltpu.CompilerParams(vmem_limit_bytes=24 << 20),
        cost_estimate=pl.CostEstimate(flops=10_000_000_000, bytes_accessed=8_000_000, transcendentals=0),
        name="filter",
    )(in_vmem(winds), in_vmem(thick), in_vmem(tables), in_vmem(twiddle), cut, trig)


def halo_kernel(lon, lat_count, got_a, got_b, tables, twiddle, _column, halo, column, y, z):
    tiles, rows = column.shape[0], column.shape[1] - 8
    levels = got_a.shape[0] // (2 * tiles)
    chunk = lon // RADIX
    tail = lon - (tiles - 1) * LANES
    place = lax.axis_index("lat")
    odd = place % 2 == 1
    refs = (got_a, got_b)
    keep = jnp.concatenate([ref[rows_at(2 * levels * (tiles - 1), 2 * levels), :] for ref in refs], axis=0)
    keep = jnp.where(lane_index(16) < tail, rolled(keep, tail), keep)
    row = lax.broadcasted_iota(jnp.int32, (8, LANES), 0)

    def edge_tiles(ref):
        v = [ref[rows_at(2 * levels * j, 2 * levels), :] for j in range(tiles)]
        return v[:-1] + [jnp.where(lane_index() < tail, v[-1], 0.0)]

    def put(v_a, v_b):
        for j in range(tiles):
            before = jnp.where(place == 0, 0.0, jnp.where(odd, v_a[j], v_b[j]))
            after = jnp.where(place == lat_count - 1, 0.0, jnp.where(odd, v_b[j], v_a[j]))
            halo[0, j], halo[1, j] = before, after
            column[j, rows_at(rows), :] = jnp.where(row < levels, pltpu.roll(before, levels, 0), after)

    filtering = jnp.min(keep) < lon // 2

    @pl.when(jnp.logical_not(filtering))
    def _():
        put(*(extended(edge_tiles(ref), tail) for ref in refs))

    @pl.when(filtering)
    def _():
        both = [jnp.concatenate(pair, axis=0) for pair in zip(edge_tiles(got_a), edge_tiles(got_b))]
        put_parts(y, pl.ds(0, 16), forward(both, chunk, twiddle))
        wide = jnp.concatenate([keep, keep], axis=1)
        put_masked(y, masked_parts(lon, products(y, tables), wide))
        z[...] = products(y, tables)
        put(*(backward(z, rows_at(8 * side), chunk, twiddle) for side in range(2)))


def with_halo(column, tables, twiddle, got_a, got_b, lon, lat_count):
    tiles = column.shape[0]
    assert got_a.shape[0] == 8 * tiles
    classes = RADIX // 2 + 1
    vmem = pl.BlockSpec(memory_space=pltpu.VMEM)
    return pl.pallas_call(
        functools.partial(halo_kernel, lon, lat_count),
        out_shape=[pltpu.VMEM((2, tiles, 8, LANES), f32), pltpu.VMEM(column.shape, f32)],
        in_specs=[vmem] * 5,
        out_specs=[vmem] * 2,
        scratch_shapes=[pltpu.VMEM((classes, 16, 2 * WIDE), bf16), pltpu.VMEM((classes, 16, WIDE), f32)],
        input_output_aliases={4: 1},
        compiler_params=pltpu.CompilerParams(vmem_limit_bytes=24 << 20),
        name="halo",
    )(got_a, got_b, in_vmem(tables), in_vmem(twiddle), column)


def beside(fields, halo, f, l, j, g, toward):
    levels = fields.shape[1]
    value = fields[f, l, j, rows_at(8 * g + 1 + toward), :]
    row = lax.broadcasted_iota(jnp.int32, (8, LANES), 0)
    slot = pl.ds((f - 1) * levels + l, 1)
    if toward < 0 and g == 0:
        return jnp.where(row > 0, value, jnp.broadcast_to(halo[0, j, slot, :], value.shape))
    if toward > 0 and g == (fields.shape[3] - 8) // 8 - 1:
        return jnp.where(row < 7, value, jnp.broadcast_to(halo[1, j, slot, :], value.shape))
    return value


def east(v):
    lane = lane_index()
    r = [rolled(a, 1) for a in v]
    return [jnp.where(lane < LANES - 1, a, b) for a, b in zip(r[:-1], r[1:])] + [r[-1]]


def west(v, tail):
    lane = lane_index()
    r = [rolled(a, -1) for a in v]
    r_before = [rolled(v[-1], tail - 1)] + r[:-1]
    return [jnp.where(lane > 0, a, b) for a, b in zip(r, r_before)]


def thickness_rows(g, lon, fields, halo, trig, thick):
    levels, tiles = fields.shape[1:3]
    tail = lon - (tiles - 1) * LANES
    at = rows_at(8 * g)
    mid = 8 * g + 1
    south, north = trig[2, at, :], trig[3, at, :]
    found = {}
    for l in range(levels):
        u, h = ([fields[f, l, j, rows_at(mid), :] for j in range(tiles)] for f in (0, 2))
        he, ue = east(h), east(u)
        flux = [(h[j] + he[j]) * (u[j] + ue[j]) for j in range(tiles)]
        flux_west = west(flux, tail)
        for j in range(tiles):
            v = fields[1, l, j, rows_at(mid), :]
            v_up, v_down = (beside(fields, halo, 1, l, j, g, to) for to in (-1, 1))
            h_up, h_down = (beside(fields, halo, 2, l, j, g, to) for to in (-1, 1))
            merid = (h[j] + h_down) * (v + v_down) * north - (h_up + h[j]) * (v_up + v) * south
            found[l, j] = h[j] - (0.25 * time_step) * (flux[j] - flux_west[j] + merid)
    for (l, j), new in found.items():
        wide = LANES if j < tiles - 1 else tail
        thick[l, at, pl.ds(LANES * j, wide)] = new[:, :wide]


def thickness_kernel(lon, fields, halo, trig, cut, _thick, thick):
    groups = trig.shape[1] // 8

    @pl.when(jnp.min(cut[...]) < lon // 2)
    def _():
        for g in range(1, groups - 1):
            thickness_rows(g, lon, fields, halo, trig, thick)

    for g in sorted({0, groups - 1}):
        thickness_rows(g, lon, fields, halo, trig, thick)


def winds_kernel(lon, fields, halo, trig, thick, *refs):
    *hops, winds_hbm, thick_hbm, winds, sem = refs
    levels, tiles = fields.shape[1:3]
    rows = trig.shape[1]
    tail = lon - (tiles - 1) * LANES
    place = lax.axis_index("lev")
    masks = [jnp.where(place + k + 1 <= len(hops), 1.0, 0.0) for k in range(len(hops))]
    copies = [pltpu.make_async_copy(thick, thick_hbm, sem.at[rows // 8])]
    copies[0].start()

    row = lax.broadcasted_iota(jnp.int32, (8, LANES), 0)

    def total(load):
        terms = [load(ref) * mask for ref, mask in zip(hops, masks)]
        return functools.reduce(jnp.add, terms) if terms else jnp.zeros((8, LANES), f32)

    def below(j, at):
        return total(lambda ref: ref[j, rows_at(at), :])

    def below_halo(j, side):
        start = rows + side * levels
        lines = [total(lambda ref, l=l: ref[j, pl.ds(start + l, 1), :]) for l in range(levels)]
        return jnp.broadcast_to(functools.reduce(jnp.add, lines), (8, LANES))

    def below_beside(j, g, own, toward):
        if toward < 0 and g == 0:
            return jnp.where(row > 0, pltpu.roll(own, 1, 0), below_halo(j, 0))
        if toward > 0 and g == rows // 8 - 1:
            return jnp.where(row < 7, pltpu.roll(own, 7, 0), below_halo(j, 1))
        return below(j, 8 * g + toward)

    for g in range(rows // 8):
        at = rows_at(8 * g)
        here = 8 * g + 1
        sine, cosine = trig[0, at, :], trig[1, at, :]
        s = [below(j, 8 * g) for j in range(tiles)]
        sum_x = [a - b for a, b in zip(east(s), west(s, tail))]
        sum_y = [below_beside(j, g, s[j], 1) - below_beside(j, g, s[j], -1) for j in range(tiles)]
        found = {}
        for l in reversed(range(levels)):
            h = [fields[2, l, j, rows_at(here), :] for j in range(tiles)]
            he, hw = east(h), west(h, tail)
            for j in range(tiles):
                u, v = (fields[f, l, j, rows_at(here), :] for f in range(2))
                dx = he[j] - hw[j]
                h_up, h_down = (beside(fields, halo, 2, l, j, g, to) for to in (-1, 1))
                dy = h_down - h_up
                new_u = u - time_step * (0.5 * (sum_x[j] + 0.5 * dx) - coriolis * sine * v)
                new_v = v - time_step * (0.5 * cosine * (sum_y[j] + 0.5 * dy) + coriolis * sine * u)
                sum_x[j] = sum_x[j] + dx
                sum_y[j] = sum_y[j] + dy
                found[l, j] = (new_u, new_v)
            if l % LEVEL_BATCH == 0:
                for (m, j), pair in found.items():
                    wide = LANES if j < tiles - 1 else tail
                    for f in range(2):
                        winds[f, m, at, pl.ds(LANES * j, wide)] = pair[f][:, :wide]
                found = {}
        copies.append(pltpu.make_async_copy(winds.at[:, :, at], winds_hbm.at[:, :, at], sem.at[g]))
        copies[-1].start()
    for copy in copies:
        copy.wait()


def stepped_thickness(fields, halo, trig, cut, thick, lon):
    vmem = pl.BlockSpec(memory_space=pltpu.VMEM)
    return pl.pallas_call(
        functools.partial(thickness_kernel, lon),
        out_shape=pltpu.VMEM(thick.shape, f32),
        in_specs=[vmem] * 5,
        out_specs=vmem,
        input_output_aliases={4: 0},
        compiler_params=pltpu.CompilerParams(vmem_limit_bytes=24 << 20),
        cost_estimate=pl.CostEstimate(flops=4_000_000_000, bytes_accessed=4_000_000, transcendentals=0),
        name="thickness",
    )(fields, halo, trig, cut, thick)


def stepped_winds(fields, halo, trig, thick, hops, shape, lon):
    hbm = pl.BlockSpec(memory_space=pltpu.HBM)
    return pl.pallas_call(
        functools.partial(winds_kernel, lon),
        out_shape=[jax.ShapeDtypeStruct(shape, f32), jax.ShapeDtypeStruct(thick.shape, f32)],
        in_specs=[pl.BlockSpec(memory_space=pltpu.VMEM)] * (4 + len(hops)),
        out_specs=[hbm, hbm],
        scratch_shapes=[pltpu.VMEM(shape, f32), pltpu.SemaphoreType.DMA((trig.shape[1] // 8 + 1,))],
        compiler_params=pltpu.CompilerParams(vmem_limit_bytes=24 << 20),
        name="winds",
    )(fields, halo, trig, thick, *hops)


def swaps(lat_count, lev_count, first):
    pairs = []
    for i in range(lat_count):
        other = i + 1 if (i - first) % 2 == 0 else i - 1
        for l in range(lev_count):
            if 0 <= other < lat_count:
                pairs.append((i * lev_count + l, other * lev_count + l))
            else:
                pairs.append((i * lev_count + l, i * lev_count + (l + 1) % lev_count))
    return pairs


def per_device(winds, thick, cutoff):
    lat_count, lev_count = lax.axis_size("lat"), lax.axis_size("lev")
    lon = thick.shape[-1]
    sent_a, sent_b, trig, cut = edges(winds, thick, cutoff, lat_count)
    got_a = lax.ppermute(sent_a, ("lat", "lev"), swaps(lat_count, lev_count, 0))
    got_b = lax.ppermute(sent_b, ("lat", "lev"), swaps(lat_count, lev_count, 1))
    tables, twiddle = (jnp.asarray(constant) for constant in filter_tables(lon))
    fields, column, new_thick = filtered_fields(winds, thick, cut, trig, tables, twiddle)
    halo, column = with_halo(column, tables, twiddle, got_a, got_b, lon, lat_count)
    hops = [
        lax.ppermute(column, "lev", [(i, (i - hop) % lev_count) for i in range(lev_count)])
        for hop in range(1, lev_count)
    ]
    new_thick = stepped_thickness(fields, halo, trig, cut, new_thick, lon)
    return tuple(stepped_winds(fields, halo, trig, new_thick, hops, winds.shape, lon))


def solution(mesh):
    return jax.shard_map(
        per_device,
        mesh=mesh,
        in_specs=(P(None, "lev", "lat", None), P("lev", "lat", None), P("lat")),
        out_specs=(P(None, "lev", "lat", None), P("lev", "lat", None)),
        check_vma=False,
    )
```

```python
import functools
import math

import jax
import jax.numpy as jnp
import ml_dtypes
import numpy as np
from jax import lax
from jax.experimental import pallas as pl
from jax.experimental.pallas import tpu as pltpu
from jax.sharding import PartitionSpec as P

time_step = 0.2
coriolis = 1.0
RADIX = 12
LANES = 128
WIDE = 2 * LANES
HALF_ROOT3 = math.sqrt(3.0) / 2.0
LEVEL_BATCH = 4
f32 = jnp.float32
bf16 = jnp.bfloat16


def filter_tables(lon):
    chunk, half = lon // RADIX, RADIX // 2
    point = np.arange(chunk)
    angle = 2.0 * math.pi * (np.outer(point, point) % chunk) / chunk
    table = np.zeros((WIDE, WIDE), np.float64)
    near, far = slice(0, chunk), slice(LANES, LANES + chunk)
    table[near, near], table[near, far] = np.cos(angle), np.sin(angle)
    table[far, near], table[far, far] = np.sin(angle), -np.cos(angle)
    table /= math.sqrt(lon)
    high = table.astype(np.float32).astype(ml_dtypes.bfloat16)
    low = (table - high.astype(np.float64)).astype(np.float32).astype(ml_dtypes.bfloat16)
    twiddle = np.zeros((2, 2, 8, LANES), np.float64)
    for k in range(1, half + 1):
        turn = 2.0 * math.pi * (k * point % lon) / lon
        for way, scale in enumerate((1.0, 1.0 if k == half else 2.0)):
            twiddle[way, 0, k, :chunk] = scale * np.cos(turn)
            twiddle[way, 1, k, :chunk] = scale * np.sin(turn)
    return np.stack([high, low]), twiddle.astype(np.float32)


def split_radix(c):
    s = [c[j] + c[j + 6] for j in range(6)]
    d = [c[j] - c[j + 6] for j in range(6)]
    t = [s[j] + s[j + 3] for j in range(3)]
    e = [s[j] - s[j + 3] for j in range(3)]
    t12 = t[1] + t[2]
    e12 = e[1] - e[2]
    y0 = t[0] + t12
    y4 = (t[0] - 0.5 * t12, HALF_ROOT3 * (t[2] - t[1]))
    y6 = e[0] - e12
    y2 = (e[0] + 0.5 * e12, -HALF_ROOT3 * (e[1] + e[2]))
    p, q = d[1] - d[5], d[2] - d[4]
    r, w = d[1] + d[5], d[2] + d[4]
    y3 = (d[0] - q, d[3] - r)
    u, v = d[0] + 0.5 * q, -0.5 * r - d[3]
    sp, sw = HALF_ROOT3 * p, HALF_ROOT3 * w
    y1 = (u + sp, v - sw)
    y5 = (u - sp, v + sw)
    return [(y0, y6), y1, y2, y3, y4, y5]


def join_radix(z):
    (z0, z6), (r1, i1), (r2, i2), (r3, i3), (r4, i4), (r5, i5) = z
    hp, sp = z0 - 0.5 * r4, HALF_ROOT3 * i4
    p = [z0 + r4, hp - sp, hp + sp]
    hq, sq = z6 - 0.5 * r2, HALF_ROOT3 * i2
    q = [z6 + r2, -hq - sq, hq - sq]
    e = [p[j] + q[j] for j in range(3)] + [p[j] - q[j] for j in range(3)]
    a, b, c, d = r1 + r5, HALF_ROOT3 * (r1 - r5), i1 + i5, HALF_ROOT3 * (i1 - i5)
    g = r3 - 0.5 * a
    f = -0.5 * c - i3
    o = [a + r3, b + f, -g - d, i3 - c, g - d, f - b]
    return [e[j] + o[j] for j in range(6)] + [e[j] - o[j] for j in range(6)]


def rolled(x, left):
    shift = (-left) % LANES
    return x if shift == 0 else pltpu.roll(x, shift, 1)


def lane_index(rows=8):
    return lax.broadcasted_iota(jnp.int32, (rows, LANES), 1)


def two_parts(x):
    high = x.astype(bf16)
    return high, (x - high.astype(f32)).astype(bf16)


def rows_at(start, size=8):
    return pl.ds(start, size)


def edge_kernel(lat_count, winds, thick, cutoff_hbm, sent_a, sent_b, trig, cut, v, h, cutoff, sem):
    levels, lon = v.shape[1:]
    rows = thick.shape[1]
    tiles = -(-lon // LANES)
    tail = lon - (tiles - 1) * LANES
    copies = [pltpu.make_async_copy(cutoff_hbm, cutoff, sem.at[4])]
    for side, start in enumerate((0, rows - 1)):
        copies.append(pltpu.make_async_copy(winds.at[1, :, start], v.at[side], sem.at[2 * side]))
        copies.append(pltpu.make_async_copy(thick.at[:, start], h.at[side], sem.at[2 * side + 1]))
    for copy in copies:
        copy.start()

    place = lax.axis_index("lat")
    index = (place * rows + lax.broadcasted_iota(jnp.int32, (rows, LANES), 0)).astype(f32)
    step = math.pi / (lat_count * rows)
    centre = (index + 0.5) * step - 0.5 * math.pi
    trig[0] = jnp.sin(centre)
    trig[1] = jnp.cos(centre)
    trig[2] = jnp.sin(index * step)
    trig[3] = jnp.sin((index + 1.0) * step)

    copies[0].wait()
    for r in range(rows):
        cut[pl.ds(r, 1), :] = jnp.full((1, LANES), cutoff[r].astype(f32), f32)
    for copy in copies[1:]:
        copy.wait()
    last_first = 1 - place % 2
    for out, side in ((sent_a, last_first), (sent_b, 1 - last_first)):
        limit = cutoff[side * (rows - 1)].astype(f32)
        for j in range(tiles):
            wide = LANES if j < tiles - 1 else tail
            for f, block in enumerate((v, h)):
                got = block[side, :, pl.ds(LANES * j, wide)]
                if wide < LANES:
                    got = jnp.concatenate([got, jnp.full((levels, LANES - wide), limit, f32)], axis=1)
                out[pl.ds((2 * j + f) * levels, levels), :] = got


def in_vmem(x):
    return pltpu.with_memory_space_constraint(x, pltpu.VMEM)


def in_hbm(x):
    return pltpu.with_memory_space_constraint(x, pltpu.HBM)


def edges(winds, thick, cutoff, lat_count):
    levels, rows, lon = thick.shape
    tiles = -(-lon // LANES)
    vmem = pl.BlockSpec(memory_space=pltpu.VMEM)
    hbm = pl.BlockSpec(memory_space=pltpu.HBM)
    assert lon < tiles * LANES
    edge = pltpu.VMEM((2 * levels * tiles, LANES), f32)
    return pl.pallas_call(
        functools.partial(edge_kernel, lat_count),
        out_shape=[edge, edge, pltpu.VMEM((4, rows, LANES), f32), pltpu.VMEM((rows, LANES), f32)],
        in_specs=[hbm] * 3,
        out_specs=[vmem] * 4,
        scratch_shapes=[
            pltpu.VMEM((2, levels, lon), f32),
            pltpu.VMEM((2, levels, lon), f32),
            pltpu.SMEM((rows,), jnp.int32),
            pltpu.SemaphoreType.DMA((5,)),
        ],
        compiler_params=pltpu.CompilerParams(vmem_limit_bytes=16 << 20),
        cost_estimate=pl.CostEstimate(flops=4_000_000_000, bytes_accessed=8_000_000, transcendentals=0),
        name="edges",
    )(in_hbm(winds), in_hbm(thick), in_hbm(cutoff))


def forward(v, chunk, twiddle):
    gap, half = LANES - chunk, RADIX // 2
    lane = lane_index(v[0].shape[0])
    c = []
    for j in range(RADIX):
        turn = gap * j
        here = jnp.where(lane < LANES - turn, v[j], v[j - 1]) if turn else v[j]
        c.append(rolled(here, -turn))
    c[-1] = jnp.where(lane < chunk, c[-1], 0.0)
    (y0, y6), *pairs = split_radix(c)
    found = []
    for k in range(half + 1):
        cos, sin = twiddle[0, 0, k : k + 1, :], twiddle[0, 1, k : k + 1, :]
        if k == 0:
            both = (y0, jnp.zeros_like(y0))
        elif k == half:
            both = (y6 * cos, -(y6 * sin))
        else:
            re, im = pairs[k - 1]
            both = (re * cos + im * sin, im * cos - re * sin)
        re, im = (two_parts(value) for value in both)
        found.append((re[0], im[0], re[1], im[1]))
    return found


def put_parts(y, at, found):
    for k, parts in enumerate(found):
        for i, part in enumerate(parts):
            y[k, at, LANES * i : LANES * (i + 1)] = part


def three(high, low, tables):
    a = jnp.concatenate([high, low, high], axis=1)
    b = jnp.concatenate([tables[0], tables[0], tables[1]], axis=0)
    return lax.dot_general(a, b, (((1,), (0,)), ((), ())), preferred_element_type=f32)


def products(y, tables):
    classes, count = y.shape[:2]
    both = y[...].reshape(classes * count, 2 * WIDE)
    return three(both[:, :WIDE], both[:, WIDE:], tables).reshape(classes, count, WIDE)


def masked_parts(lon, coeffs, keep):
    at = lax.broadcasted_iota(jnp.int32, (1, WIDE), 1)
    at = jnp.where(at < LANES, at, at - LANES)
    found = []
    for k in range(coeffs.shape[0]):
        m = RADIX * at + k
        inside = jnp.minimum(m, lon - m).astype(f32) <= keep
        found.append(two_parts(jnp.where(inside, coeffs[k], 0.0)))
    return found


def put_masked(y, found):
    for k, parts in enumerate(found):
        for i, part in enumerate(parts):
            y[k, :, WIDE * i : WIDE * (i + 1)] = part


def backward(z, at, chunk, twiddle):
    gap, half = LANES - chunk, RADIX // 2
    lane = lane_index()
    pairs = [(z[0, at, :LANES], None)]
    for k in range(1, half + 1):
        re, im = z[k, at, :LANES], z[k, at, LANES:]
        cos, sin = twiddle[1, 0, k : k + 1, :], twiddle[1, 1, k : k + 1, :]
        pairs.append((re * cos - im * sin, re * sin + im * cos if k < half else None))
    c = join_radix([(pairs[0][0], pairs[half][0])] + pairs[1:half])
    c = [rolled(c[j % RADIX], gap * j) for j in range(RADIX + 1)]
    return [jnp.where(lane < LANES - gap * (j + 1), c[j], c[j + 1]) for j in range(RADIX)]


def extended(v, tail):
    return v[:-1] + [jnp.where(lane_index() < tail, v[-1], rolled(v[0], LANES - tail))]


def filter_kernel(winds, thick, tables, twiddle, cut, trig, out, column, new_thick, y, z):
    levels, rows, lon = thick.shape
    tiles = out.shape[2]
    chunk = lon // RADIX
    tail = lon - (tiles - 1) * LANES
    order = (2, 0, 1)
    keep = cut[...]
    filtering = jnp.min(keep) < lon // 2

    def own_tiles(f, l, at):
        block, lead = (winds, (f, l)) if f < 2 else (thick, (l,))
        got = [block[(*lead, at, pl.ds(LANES * j, LANES))] for j in range(tiles - 1)]
        last = block[(*lead, at, pl.ds(LANES * (tiles - 1), tail))]
        return got + [jnp.concatenate([last, jnp.zeros((at.size, LANES - tail), f32)], axis=1)]

    @pl.when(jnp.logical_not(filtering))
    def _():
        for f in order:

            def as_is(l, _, f=f):
                for g in range(rows // 8):
                    v = extended(own_tiles(f, l, rows_at(8 * g)), tail)
                    for j in range(tiles):
                        out[f, l, j, rows_at(1 + 8 * g), :] = v[j]
                return 0

            lax.fori_loop(0, levels, as_is, 0)
        for g in range(1, rows // 8 - 1):
            thickness_rows(g, lon, out, None, trig, new_thick)

    @pl.when(filtering)
    def _():
        units = y.shape[0]
        per = 3 * levels // units
        wide = jnp.concatenate([jnp.concatenate([keep, keep], axis=1)] * per, axis=0)

        def members(n):
            return [(order[(n * per + i) // levels], (n * per + i) % levels, i * rows) for i in range(per)]


        def split(n):
            found = []
            for f, l, start in members(n):
                for g in range(rows // 16):
                    parts = forward(own_tiles(f, l, rows_at(16 * g, 16)), chunk, twiddle)
                    found.append((pl.ds(start + 16 * g, 16), parts))
            return found

        def join(n):
            found = []
            for f, l, start in members(n):
                for g in range(rows // 8):
                    found.append((f, l, g, backward(z.at[n], rows_at(start + 8 * g), chunk, twiddle)))
            return found

        for n in range(-1, units + 2):
            coeffs = products(y.at[n], tables) if 0 <= n < units else None
            back = products(y.at[n - 1], tables) if 1 <= n <= units else None
            ahead = split(n + 1) if n + 1 < units else []
            behind = join(n - 2) if n >= 2 else []
            masked = masked_parts(lon, coeffs, wide) if 0 <= n < units else []
            put_masked(y.at[n], masked)
            if back is not None:
                z[n - 1] = back
            for at, parts in ahead:
                put_parts(y.at[n + 1], at, parts)
            for f, l, g, v in behind:
                for j in range(tiles):
                    out[f, l, j, rows_at(1 + 8 * g), :] = v[j]

    for j in range(tiles):
        lines = [out[2, l, j, pl.ds(1, rows), :] for l in range(levels)]
        column[j, pl.ds(0, rows), :] = functools.reduce(jnp.add, lines)


def filtered_fields(winds, thick, cut, trig, tables, twiddle):
    levels, rows, lon = thick.shape
    tiles = -(-lon // LANES)
    assert lon % RADIX == 0 and lon // RADIX <= LANES and tiles == RADIX
    assert rows % 16 == 0 and levels % 2 == 0
    classes = RADIX // 2 + 1
    per = 1
    units = 3 * levels // per
    vmem = pl.BlockSpec(memory_space=pltpu.VMEM)
    hbm = pl.BlockSpec(memory_space=pltpu.HBM)
    return pl.pallas_call(
        filter_kernel,
        out_shape=[
            pltpu.VMEM((3, levels, tiles, rows + 8, LANES), f32),
            pltpu.VMEM((tiles, rows + 8, LANES), f32),
            pltpu.VMEM(thick.shape, f32),
        ],
        in_specs=[vmem] * 6,
        out_specs=[vmem] * 3,
        scratch_shapes=[
            pltpu.VMEM((units, classes, per * rows, 2 * WIDE), bf16),
            pltpu.VMEM((units, classes, per * rows, WIDE), f32),
        ],
        compiler_params=pltpu.CompilerParams(vmem_limit_bytes=24 << 20),
        cost_estimate=pl.CostEstimate(flops=10_000_000_000, bytes_accessed=8_000_000, transcendentals=0),
        name="filter",
    )(in_vmem(winds), in_vmem(thick), in_vmem(tables), in_vmem(twiddle), cut, trig)


def edge_tiles(ref, tiles, tail):
    v = [ref[rows_at(8 * j), :] for j in range(tiles)]
    spare = lane_index() < tail
    return v[:-1] + [jnp.where(spare, v[-1], 0.0)], jnp.where(spare, rolled(v[-1], tail), v[-1])


def filtered_edges(lon, pair, tables, twiddle, y, z):
    chunk = lon // RADIX
    both = [jnp.concatenate(rows, axis=0) for rows in zip(*(v for v, _ in pair))]
    put_parts(y, pl.ds(0, 16), forward(both, chunk, twiddle))
    keep = jnp.concatenate([keep for _, keep in pair], axis=0)
    wide = jnp.concatenate([keep, keep], axis=1)
    put_masked(y, masked_parts(lon, products(y, tables), wide))
    z[...] = products(y, tables)
    return [backward(z, rows_at(8 * side), chunk, twiddle) for side in range(2)]


def near_kernel(lon, got_a, tables, twiddle, cut, near, y, z):
    tiles = near.shape[0]
    tail = lon - (tiles - 1) * LANES
    edge = edge_tiles(got_a, tiles, tail)
    idle = jnp.min(cut[...]) >= lon // 2
    filtering = jnp.min(edge[1]) < lon // 2

    @pl.when(jnp.logical_and(idle, filtering))
    def _():
        v = filtered_edges(lon, (edge, edge), tables, twiddle, y, z)[0]
        for j in range(tiles):
            near[j] = v[j]

    @pl.when(jnp.logical_and(idle, jnp.logical_not(filtering)))
    def _():
        for j, value in enumerate(extended(edge[0], tail)):
            near[j] = value


def halo_kernel(lon, lat_count, got_a, got_b, tables, twiddle, cut, near, _column, halo, column, y, z):
    tiles, rows = column.shape[0], column.shape[1] - 8
    levels = got_a.shape[0] // (2 * tiles)
    tail = lon - (tiles - 1) * LANES
    place = lax.axis_index("lat")
    odd = place % 2 == 1
    edges_got = [edge_tiles(ref, tiles, tail) for ref in (got_a, got_b)]
    row = lax.broadcasted_iota(jnp.int32, (8, LANES), 0)
    idle = jnp.min(cut[...]) >= lon // 2
    filtering = [jnp.min(keep) < lon // 2 for _, keep in edges_got]
    done = jnp.logical_and(idle, jnp.logical_not(filtering[1]))
    either = jnp.logical_or(*filtering)
    both = jnp.logical_and(jnp.logical_not(done), either)
    neither = jnp.logical_and(jnp.logical_not(done), jnp.logical_not(either))

    def put(v_a, v_b):
        for j in range(tiles):
            before = jnp.where(place == 0, 0.0, jnp.where(odd, v_a[j], v_b[j]))
            after = jnp.where(place == lat_count - 1, 0.0, jnp.where(odd, v_b[j], v_a[j]))
            halo[0, j], halo[1, j] = before, after
            column[j, rows_at(rows), :] = jnp.where(row < levels, pltpu.roll(before, levels, 0), after)

    @pl.when(done)
    def _():
        put([near[j] for j in range(tiles)], extended(edges_got[1][0], tail))

    @pl.when(neither)
    def _():
        put(*(extended(v, tail) for v, _ in edges_got))

    @pl.when(both)
    def _():
        put(*filtered_edges(lon, edges_got, tables, twiddle, y, z))


def near_edge(got_a, tables, twiddle, cut, lon):
    vmem = pl.BlockSpec(memory_space=pltpu.VMEM)
    classes = RADIX // 2 + 1
    return pl.pallas_call(
        functools.partial(near_kernel, lon),
        out_shape=pltpu.VMEM((got_a.shape[0] // 8, 8, LANES), f32),
        in_specs=[vmem] * 4,
        out_specs=vmem,
        scratch_shapes=[pltpu.VMEM((classes, 16, 2 * WIDE), bf16), pltpu.VMEM((classes, 16, WIDE), f32)],
        compiler_params=pltpu.CompilerParams(vmem_limit_bytes=24 << 20),
        name="near",
    )(got_a, in_vmem(tables), in_vmem(twiddle), cut)


def with_halo(column, tables, twiddle, cut, got_a, got_b, lon, lat_count):
    tiles = column.shape[0]
    assert got_a.shape[0] == 8 * tiles
    near = near_edge(got_a, tables, twiddle, cut, lon)
    classes = RADIX // 2 + 1
    vmem = pl.BlockSpec(memory_space=pltpu.VMEM)
    return pl.pallas_call(
        functools.partial(halo_kernel, lon, lat_count),
        out_shape=[pltpu.VMEM((2, tiles, 8, LANES), f32), pltpu.VMEM(column.shape, f32)],
        in_specs=[vmem] * 7,
        out_specs=[vmem] * 2,
        scratch_shapes=[pltpu.VMEM((classes, 16, 2 * WIDE), bf16), pltpu.VMEM((classes, 16, WIDE), f32)],
        input_output_aliases={6: 1},
        compiler_params=pltpu.CompilerParams(vmem_limit_bytes=24 << 20),
        name="halo",
    )(got_a, got_b, in_vmem(tables), in_vmem(twiddle), cut, near, column)


def beside(fields, halo, f, l, j, g, toward):
    levels = fields.shape[1]
    value = fields[f, l, j, rows_at(8 * g + 1 + toward), :]
    row = lax.broadcasted_iota(jnp.int32, (8, LANES), 0)
    slot = pl.ds((f - 1) * levels + l, 1)
    if toward < 0 and g == 0:
        return jnp.where(row > 0, value, jnp.broadcast_to(halo[0, j, slot, :], value.shape))
    if toward > 0 and g == (fields.shape[3] - 8) // 8 - 1:
        return jnp.where(row < 7, value, jnp.broadcast_to(halo[1, j, slot, :], value.shape))
    return value


def east(v):
    lane = lane_index()
    r = [rolled(a, 1) for a in v]
    return [jnp.where(lane < LANES - 1, a, b) for a, b in zip(r[:-1], r[1:])] + [r[-1]]


def west(v, tail):
    lane = lane_index()
    r = [rolled(a, -1) for a in v]
    r_before = [rolled(v[-1], tail - 1)] + r[:-1]
    return [jnp.where(lane > 0, a, b) for a, b in zip(r, r_before)]


def thickness_rows(g, lon, fields, halo, trig, thick):
    levels, tiles = fields.shape[1:3]
    tail = lon - (tiles - 1) * LANES
    at = rows_at(8 * g)
    mid = 8 * g + 1
    south, north = trig[2, at, :], trig[3, at, :]
    found = {}
    for l in range(levels):
        u, h = ([fields[f, l, j, rows_at(mid), :] for j in range(tiles)] for f in (0, 2))
        he, ue = east(h), east(u)
        flux = [(h[j] + he[j]) * (u[j] + ue[j]) for j in range(tiles)]
        flux_west = west(flux, tail)
        for j in range(tiles):
            v = fields[1, l, j, rows_at(mid), :]
            v_up, v_down = (beside(fields, halo, 1, l, j, g, to) for to in (-1, 1))
            h_up, h_down = (beside(fields, halo, 2, l, j, g, to) for to in (-1, 1))
            merid = (h[j] + h_down) * (v + v_down) * north - (h_up + h[j]) * (v_up + v) * south
            found[l, j] = h[j] - (0.25 * time_step) * (flux[j] - flux_west[j] + merid)
    for (l, j), new in found.items():
        wide = LANES if j < tiles - 1 else tail
        thick[l, at, pl.ds(LANES * j, wide)] = new[:, :wide]


def thickness_kernel(lon, fields, halo, trig, cut, _thick, thick):
    groups = trig.shape[1] // 8

    @pl.when(jnp.min(cut[...]) < lon // 2)
    def _():
        for g in range(1, groups - 1):
            thickness_rows(g, lon, fields, halo, trig, thick)

    for g in sorted({0, groups - 1}):
        thickness_rows(g, lon, fields, halo, trig, thick)


def winds_kernel(lon, fields, halo, trig, thick, *refs):
    *hops, winds_hbm, thick_hbm, winds, sem = refs
    levels, tiles = fields.shape[1:3]
    rows = trig.shape[1]
    tail = lon - (tiles - 1) * LANES
    place = lax.axis_index("lev")
    masks = [jnp.where(place + k + 1 <= len(hops), 1.0, 0.0) for k in range(len(hops))]
    copies = [pltpu.make_async_copy(thick, thick_hbm, sem.at[rows // 8])]
    copies[0].start()

    row = lax.broadcasted_iota(jnp.int32, (8, LANES), 0)

    def total(load):
        terms = [load(ref) * mask for ref, mask in zip(hops, masks)]
        return functools.reduce(jnp.add, terms) if terms else jnp.zeros((8, LANES), f32)

    def below(j, at):
        return total(lambda ref: ref[j, rows_at(at), :])

    def below_halo(j, side):
        start = rows + side * levels
        lines = [total(lambda ref, l=l: ref[j, pl.ds(start + l, 1), :]) for l in range(levels)]
        return jnp.broadcast_to(functools.reduce(jnp.add, lines), (8, LANES))

    def below_beside(j, g, own, toward):
        if toward < 0 and g == 0:
            return jnp.where(row > 0, pltpu.roll(own, 1, 0), below_halo(j, 0))
        if toward > 0 and g == rows // 8 - 1:
            return jnp.where(row < 7, pltpu.roll(own, 7, 0), below_halo(j, 1))
        return below(j, 8 * g + toward)

    for g in range(rows // 8):
        at = rows_at(8 * g)
        here = 8 * g + 1
        sine, cosine = trig[0, at, :], trig[1, at, :]
        s = [below(j, 8 * g) for j in range(tiles)]
        sum_x = [a - b for a, b in zip(east(s), west(s, tail))]
        sum_y = [below_beside(j, g, s[j], 1) - below_beside(j, g, s[j], -1) for j in range(tiles)]
        found = {}
        for l in reversed(range(levels)):
            h = [fields[2, l, j, rows_at(here), :] for j in range(tiles)]
            he, hw = east(h), west(h, tail)
            for j in range(tiles):
                u, v = (fields[f, l, j, rows_at(here), :] for f in range(2))
                dx = he[j] - hw[j]
                h_up, h_down = (beside(fields, halo, 2, l, j, g, to) for to in (-1, 1))
                dy = h_down - h_up
                new_u = u - time_step * (0.5 * (sum_x[j] + 0.5 * dx) - coriolis * sine * v)
                new_v = v - time_step * (0.5 * cosine * (sum_y[j] + 0.5 * dy) + coriolis * sine * u)
                sum_x[j] = sum_x[j] + dx
                sum_y[j] = sum_y[j] + dy
                found[l, j] = (new_u, new_v)
            if l % LEVEL_BATCH == 0:
                for (m, j), pair in found.items():
                    wide = LANES if j < tiles - 1 else tail
                    for f in range(2):
                        winds[f, m, at, pl.ds(LANES * j, wide)] = pair[f][:, :wide]
                found = {}
        copies.append(pltpu.make_async_copy(winds.at[:, :, at], winds_hbm.at[:, :, at], sem.at[g]))
        copies[-1].start()
    for copy in copies:
        copy.wait()


def stepped_thickness(fields, halo, trig, cut, thick, lon):
    vmem = pl.BlockSpec(memory_space=pltpu.VMEM)
    return pl.pallas_call(
        functools.partial(thickness_kernel, lon),
        out_shape=pltpu.VMEM(thick.shape, f32),
        in_specs=[vmem] * 5,
        out_specs=vmem,
        input_output_aliases={4: 0},
        compiler_params=pltpu.CompilerParams(vmem_limit_bytes=24 << 20),
        cost_estimate=pl.CostEstimate(flops=4_000_000_000, bytes_accessed=4_000_000, transcendentals=0),
        name="thickness",
    )(fields, halo, trig, cut, thick)


def stepped_winds(fields, halo, trig, thick, hops, shape, lon):
    hbm = pl.BlockSpec(memory_space=pltpu.HBM)
    return pl.pallas_call(
        functools.partial(winds_kernel, lon),
        out_shape=[jax.ShapeDtypeStruct(shape, f32), jax.ShapeDtypeStruct(thick.shape, f32)],
        in_specs=[pl.BlockSpec(memory_space=pltpu.VMEM)] * (4 + len(hops)),
        out_specs=[hbm, hbm],
        scratch_shapes=[pltpu.VMEM(shape, f32), pltpu.SemaphoreType.DMA((trig.shape[1] // 8 + 1,))],
        compiler_params=pltpu.CompilerParams(vmem_limit_bytes=24 << 20),
        name="winds",
    )(fields, halo, trig, thick, *hops)


def swaps(lat_count, lev_count, first):
    pairs = []
    for i in range(lat_count):
        other = i + 1 if (i - first) % 2 == 0 else i - 1
        for l in range(lev_count):
            if 0 <= other < lat_count:
                pairs.append((i * lev_count + l, other * lev_count + l))
            else:
                pairs.append((i * lev_count + l, i * lev_count + (l + 1) % lev_count))
    return pairs


def per_device(winds, thick, cutoff):
    lat_count, lev_count = lax.axis_size("lat"), lax.axis_size("lev")
    lon = thick.shape[-1]
    sent_a, sent_b, trig, cut = edges(winds, thick, cutoff, lat_count)
    got_a = lax.ppermute(sent_a, ("lat", "lev"), swaps(lat_count, lev_count, 0))
    got_b = lax.ppermute(sent_b, ("lat", "lev"), swaps(lat_count, lev_count, 1))
    tables, twiddle = (jnp.asarray(constant) for constant in filter_tables(lon))
    fields, column, new_thick = filtered_fields(winds, thick, cut, trig, tables, twiddle)
    halo, column = with_halo(column, tables, twiddle, cut, got_a, got_b, lon, lat_count)
    hops = [
        lax.ppermute(column, "lev", [(i, (i - hop) % lev_count) for i in range(lev_count)])
        for hop in range(1, lev_count)
    ]
    new_thick = stepped_thickness(fields, halo, trig, cut, new_thick, lon)
    return tuple(stepped_winds(fields, halo, trig, new_thick, hops, winds.shape, lon))


def solution(mesh):
    return jax.shard_map(
        per_device,
        mesh=mesh,
        in_specs=(P(None, "lev", "lat", None), P("lev", "lat", None), P("lat")),
        out_specs=(P(None, "lev", "lat", None), P("lev", "lat", None)),
        check_vma=False,
    )
```

```python
import functools
import math

import jax
import jax.numpy as jnp
import ml_dtypes
import numpy as np
from jax import lax
from jax.experimental import pallas as pl
from jax.experimental.pallas import tpu as pltpu
from jax.sharding import PartitionSpec as P

time_step = 0.2
coriolis = 1.0
RADIX = 12
LANES = 128
WIDE = 2 * LANES
HALF_ROOT3 = math.sqrt(3.0) / 2.0
LEVEL_BATCH = 4
f32 = jnp.float32
bf16 = jnp.bfloat16


def filter_tables(lon):
    chunk, half = lon // RADIX, RADIX // 2
    point = np.arange(chunk)
    angle = 2.0 * math.pi * (np.outer(point, point) % chunk) / chunk
    table = np.zeros((WIDE, WIDE), np.float64)
    near, far = slice(0, chunk), slice(LANES, LANES + chunk)
    table[near, near], table[near, far] = np.cos(angle), np.sin(angle)
    table[far, near], table[far, far] = np.sin(angle), -np.cos(angle)
    table /= math.sqrt(lon)
    high = table.astype(np.float32).astype(ml_dtypes.bfloat16)
    low = (table - high.astype(np.float64)).astype(np.float32).astype(ml_dtypes.bfloat16)
    twiddle = np.zeros((2, 2, 8, LANES), np.float64)
    for k in range(1, half + 1):
        turn = 2.0 * math.pi * (k * point % lon) / lon
        for way, scale in enumerate((1.0, 1.0 if k == half else 2.0)):
            twiddle[way, 0, k, :chunk] = scale * np.cos(turn)
            twiddle[way, 1, k, :chunk] = scale * np.sin(turn)
    return np.stack([high, low]), twiddle.astype(np.float32)


def split_radix(c):
    s = [c[j] + c[j + 6] for j in range(6)]
    d = [c[j] - c[j + 6] for j in range(6)]
    t = [s[j] + s[j + 3] for j in range(3)]
    e = [s[j] - s[j + 3] for j in range(3)]
    t12 = t[1] + t[2]
    e12 = e[1] - e[2]
    y0 = t[0] + t12
    y4 = (t[0] - 0.5 * t12, HALF_ROOT3 * (t[2] - t[1]))
    y6 = e[0] - e12
    y2 = (e[0] + 0.5 * e12, -HALF_ROOT3 * (e[1] + e[2]))
    p, q = d[1] - d[5], d[2] - d[4]
    r, w = d[1] + d[5], d[2] + d[4]
    y3 = (d[0] - q, d[3] - r)
    u, v = d[0] + 0.5 * q, -0.5 * r - d[3]
    sp, sw = HALF_ROOT3 * p, HALF_ROOT3 * w
    y1 = (u + sp, v - sw)
    y5 = (u - sp, v + sw)
    return [(y0, y6), y1, y2, y3, y4, y5]


def join_radix(z):
    (z0, z6), (r1, i1), (r2, i2), (r3, i3), (r4, i4), (r5, i5) = z
    hp, sp = z0 - 0.5 * r4, HALF_ROOT3 * i4
    p = [z0 + r4, hp - sp, hp + sp]
    hq, sq = z6 - 0.5 * r2, HALF_ROOT3 * i2
    q = [z6 + r2, -hq - sq, hq - sq]
    e = [p[j] + q[j] for j in range(3)] + [p[j] - q[j] for j in range(3)]
    a, b, c, d = r1 + r5, HALF_ROOT3 * (r1 - r5), i1 + i5, HALF_ROOT3 * (i1 - i5)
    g = r3 - 0.5 * a
    f = -0.5 * c - i3
    o = [a + r3, b + f, -g - d, i3 - c, g - d, f - b]
    return [e[j] + o[j] for j in range(6)] + [e[j] - o[j] for j in range(6)]


def rolled(x, left):
    shift = (-left) % LANES
    return x if shift == 0 else pltpu.roll(x, shift, 1)


def lane_index(rows=8):
    return lax.broadcasted_iota(jnp.int32, (rows, LANES), 1)


def two_parts(x):
    high = x.astype(bf16)
    return high, (x - high.astype(f32)).astype(bf16)


def rows_at(start, size=8):
    return pl.ds(start, size)


def edge_kernel(lat_count, winds, thick, cutoff_hbm, sent_a, sent_b, trig, cut, v, h, cutoff, sem):
    levels, lon = v.shape[1:]
    rows = thick.shape[1]
    tiles = -(-lon // LANES)
    tail = lon - (tiles - 1) * LANES
    copies = [pltpu.make_async_copy(cutoff_hbm, cutoff, sem.at[4])]
    for side, start in enumerate((0, rows - 1)):
        copies.append(pltpu.make_async_copy(winds.at[1, :, start], v.at[side], sem.at[2 * side]))
        copies.append(pltpu.make_async_copy(thick.at[:, start], h.at[side], sem.at[2 * side + 1]))
    for copy in copies:
        copy.start()

    place = lax.axis_index("lat")
    index = (place * rows + lax.broadcasted_iota(jnp.int32, (rows, LANES), 0)).astype(f32)
    step = math.pi / (lat_count * rows)
    centre = (index + 0.5) * step - 0.5 * math.pi
    trig[0] = jnp.sin(centre)
    trig[1] = jnp.cos(centre)
    trig[2] = jnp.sin(index * step)
    trig[3] = jnp.sin((index + 1.0) * step)

    copies[0].wait()
    for r in range(rows):
        cut[pl.ds(r, 1), :] = jnp.full((1, LANES), cutoff[r].astype(f32), f32)
    for copy in copies[1:]:
        copy.wait()
    last_first = 1 - place % 2
    for out, side in ((sent_a, last_first), (sent_b, 1 - last_first)):
        limit = cutoff[side * (rows - 1)].astype(f32)
        for j in range(tiles):
            wide = LANES if j < tiles - 1 else tail
            for f, block in enumerate((v, h)):
                got = block[side, :, pl.ds(LANES * j, wide)]
                if wide < LANES:
                    got = jnp.concatenate([got, jnp.full((levels, LANES - wide), limit, f32)], axis=1)
                out[pl.ds((2 * j + f) * levels, levels), :] = got


def in_vmem(x):
    return pltpu.with_memory_space_constraint(x, pltpu.VMEM)


def in_hbm(x):
    return pltpu.with_memory_space_constraint(x, pltpu.HBM)


def edges(winds, thick, cutoff, lat_count):
    levels, rows, lon = thick.shape
    tiles = -(-lon // LANES)
    vmem = pl.BlockSpec(memory_space=pltpu.VMEM)
    hbm = pl.BlockSpec(memory_space=pltpu.HBM)
    assert lon < tiles * LANES
    edge = pltpu.VMEM((2 * levels * tiles, LANES), f32)
    return pl.pallas_call(
        functools.partial(edge_kernel, lat_count),
        out_shape=[edge, edge, pltpu.VMEM((4, rows, LANES), f32), pltpu.VMEM((rows, LANES), f32)],
        in_specs=[hbm] * 3,
        out_specs=[vmem] * 4,
        scratch_shapes=[
            pltpu.VMEM((2, levels, lon), f32),
            pltpu.VMEM((2, levels, lon), f32),
            pltpu.SMEM((rows,), jnp.int32),
            pltpu.SemaphoreType.DMA((5,)),
        ],
        compiler_params=pltpu.CompilerParams(vmem_limit_bytes=16 << 20),
        cost_estimate=pl.CostEstimate(flops=4_000_000_000, bytes_accessed=8_000_000, transcendentals=0),
        name="edges",
    )(in_hbm(winds), in_hbm(thick), in_hbm(cutoff))


def forward(v, chunk, twiddle):
    gap, half = LANES - chunk, RADIX // 2
    lane = lane_index(v[0].shape[0])
    c = []
    for j in range(RADIX):
        turn = gap * j
        here = jnp.where(lane < LANES - turn, v[j], v[j - 1]) if turn else v[j]
        c.append(rolled(here, -turn))
    c[-1] = jnp.where(lane < chunk, c[-1], 0.0)
    (y0, y6), *pairs = split_radix(c)
    found = []
    for k in range(half + 1):
        cos, sin = twiddle[0, 0, k : k + 1, :], twiddle[0, 1, k : k + 1, :]
        if k == 0:
            both = (y0, jnp.zeros_like(y0))
        elif k == half:
            both = (y6 * cos, -(y6 * sin))
        else:
            re, im = pairs[k - 1]
            both = (re * cos + im * sin, im * cos - re * sin)
        re, im = (two_parts(value) for value in both)
        found.append((re[0], im[0], re[1], im[1]))
    return found


def put_parts(y, at, found):
    for k, parts in enumerate(found):
        for i, part in enumerate(parts):
            y[k, at, LANES * i : LANES * (i + 1)] = part


def three(high, low, tables):
    a = jnp.concatenate([high, low, high], axis=1)
    b = jnp.concatenate([tables[0], tables[0], tables[1]], axis=0)
    return lax.dot_general(a, b, (((1,), (0,)), ((), ())), preferred_element_type=f32)


def products(y, tables):
    classes, count = y.shape[:2]
    both = y[...].reshape(classes * count, 2 * WIDE)
    return three(both[:, :WIDE], both[:, WIDE:], tables).reshape(classes, count, WIDE)


def masked_parts(lon, coeffs, keep):
    at = lax.broadcasted_iota(jnp.int32, (1, WIDE), 1)
    at = jnp.where(at < LANES, at, at - LANES)
    found = []
    for k in range(coeffs.shape[0]):
        m = RADIX * at + k
        inside = jnp.minimum(m, lon - m).astype(f32) <= keep
        found.append(two_parts(jnp.where(inside, coeffs[k], 0.0)))
    return found


def put_masked(y, found):
    for k, parts in enumerate(found):
        for i, part in enumerate(parts):
            y[k, :, WIDE * i : WIDE * (i + 1)] = part


def backward(z, at, chunk, twiddle):
    gap, half = LANES - chunk, RADIX // 2
    lane = lane_index()
    pairs = [(z[0, at, :LANES], None)]
    for k in range(1, half + 1):
        re, im = z[k, at, :LANES], z[k, at, LANES:]
        cos, sin = twiddle[1, 0, k : k + 1, :], twiddle[1, 1, k : k + 1, :]
        pairs.append((re * cos - im * sin, re * sin + im * cos if k < half else None))
    c = join_radix([(pairs[0][0], pairs[half][0])] + pairs[1:half])
    c = [rolled(c[j % RADIX], gap * j) for j in range(RADIX + 1)]
    return [jnp.where(lane < LANES - gap * (j + 1), c[j], c[j + 1]) for j in range(RADIX)]


def extended(v, tail):
    return v[:-1] + [jnp.where(lane_index() < tail, v[-1], rolled(v[0], LANES - tail))]


def filter_kernel(winds, thick, tables, twiddle, cut, trig, out, column, new_thick, y, z):
    levels, rows, lon = thick.shape
    tiles = out.shape[2]
    chunk = lon // RADIX
    tail = lon - (tiles - 1) * LANES
    order = (2, 0, 1)
    keep = cut[...]
    filtering = jnp.min(keep) < lon // 2

    def own_tiles(f, l, at):
        block, lead = (winds, (f, l)) if f < 2 else (thick, (l,))
        got = [block[(*lead, at, pl.ds(LANES * j, LANES))] for j in range(tiles - 1)]
        last = block[(*lead, at, pl.ds(LANES * (tiles - 1), tail))]
        return got + [jnp.concatenate([last, jnp.zeros((at.size, LANES - tail), f32)], axis=1)]

    @pl.when(jnp.logical_not(filtering))
    def _():
        for f in order:

            def as_is(l, _, f=f):
                for g in range(rows // 8):
                    v = extended(own_tiles(f, l, rows_at(8 * g)), tail)
                    for j in range(tiles):
                        out[f, l, j, rows_at(1 + 8 * g), :] = v[j]
                return 0

            lax.fori_loop(0, levels, as_is, 0)
        for g in range(1, rows // 8 - 1):
            thickness_rows(g, lon, out, None, trig, new_thick)

    @pl.when(filtering)
    def _():
        units = y.shape[0]
        per = 3 * levels // units
        wide = jnp.concatenate([jnp.concatenate([keep, keep], axis=1)] * per, axis=0)

        def members(n):
            return [(order[(n * per + i) // levels], (n * per + i) % levels, i * rows) for i in range(per)]


        def split(n):
            found = []
            for f, l, start in members(n):
                for g in range(rows // 16):
                    parts = forward(own_tiles(f, l, rows_at(16 * g, 16)), chunk, twiddle)
                    found.append((pl.ds(start + 16 * g, 16), parts))
            return found

        def join(n):
            found = []
            for f, l, start in members(n):
                for g in range(rows // 8):
                    found.append((f, l, g, backward(z.at[n], rows_at(start + 8 * g), chunk, twiddle)))
            return found

        for n in range(-1, units + 2):
            coeffs = products(y.at[n], tables) if 0 <= n < units else None
            back = products(y.at[n - 1], tables) if 1 <= n <= units else None
            ahead = split(n + 1) if n + 1 < units else []
            behind = join(n - 2) if n >= 2 else []
            masked = masked_parts(lon, coeffs, wide) if 0 <= n < units else []
            put_masked(y.at[n], masked)
            if back is not None:
                z[n - 1] = back
            for at, parts in ahead:
                put_parts(y.at[n + 1], at, parts)
            for f, l, g, v in behind:
                for j in range(tiles):
                    out[f, l, j, rows_at(1 + 8 * g), :] = v[j]

    for j in range(tiles):
        lines = [out[2, l, j, pl.ds(1, rows), :] for l in range(levels)]
        column[j, pl.ds(0, rows), :] = functools.reduce(jnp.add, lines)


def filtered_fields(winds, thick, cut, trig, tables, twiddle):
    levels, rows, lon = thick.shape
    tiles = -(-lon // LANES)
    assert lon % RADIX == 0 and lon // RADIX <= LANES and tiles == RADIX
    assert rows % 16 == 0 and levels % 2 == 0
    classes = RADIX // 2 + 1
    per = 1
    units = 3 * levels // per
    vmem = pl.BlockSpec(memory_space=pltpu.VMEM)
    hbm = pl.BlockSpec(memory_space=pltpu.HBM)
    return pl.pallas_call(
        filter_kernel,
        out_shape=[
            pltpu.VMEM((3, levels, tiles, rows + 8, LANES), f32),
            pltpu.VMEM((tiles, rows + 8, LANES), f32),
            pltpu.VMEM(thick.shape, f32),
        ],
        in_specs=[vmem] * 6,
        out_specs=[vmem] * 3,
        scratch_shapes=[
            pltpu.VMEM((units, classes, per * rows, 2 * WIDE), bf16),
            pltpu.VMEM((units, classes, per * rows, WIDE), f32),
        ],
        compiler_params=pltpu.CompilerParams(vmem_limit_bytes=24 << 20),
        cost_estimate=pl.CostEstimate(flops=10_000_000_000, bytes_accessed=8_000_000, transcendentals=0),
        name="filter",
    )(in_vmem(winds), in_vmem(thick), in_vmem(tables), in_vmem(twiddle), cut, trig)


def edge_tiles(ref, tiles, tail):
    v = [ref[rows_at(8 * j), :] for j in range(tiles)]
    spare = lane_index() < tail
    return v[:-1] + [jnp.where(spare, v[-1], 0.0)], jnp.where(spare, rolled(v[-1], tail), v[-1])


def filtered_edges(lon, pair, tables, twiddle, y, z):
    chunk = lon // RADIX
    both = [jnp.concatenate(rows, axis=0) for rows in zip(*(v for v, _ in pair))]
    put_parts(y, pl.ds(0, 16), forward(both, chunk, twiddle))
    keep = jnp.concatenate([keep for _, keep in pair], axis=0)
    wide = jnp.concatenate([keep, keep], axis=1)
    put_masked(y, masked_parts(lon, products(y, tables), wide))
    z[...] = products(y, tables)
    return [backward(z, rows_at(8 * side), chunk, twiddle) for side in range(2)]


def near_kernel(lon, got_a, tables, twiddle, cut, near, y, z):
    tiles = near.shape[0]
    tail = lon - (tiles - 1) * LANES

    @pl.when(jnp.min(cut[...]) >= lon // 2)
    def _():
        edge = edge_tiles(got_a, tiles, tail)
        filtering = jnp.min(edge[1]) < lon // 2

        @pl.when(filtering)
        def _():
            v = filtered_edges(lon, (edge, edge), tables, twiddle, y, z)[0]
            for j in range(tiles):
                near[j] = v[j]

        @pl.when(jnp.logical_not(filtering))
        def _():
            for j, value in enumerate(extended(edge[0], tail)):
                near[j] = value


def halo_kernel(lon, lat_count, got_a, got_b, tables, twiddle, cut, near, _column, halo, column, y, z):
    tiles, rows = column.shape[0], column.shape[1] - 8
    levels = got_a.shape[0] // (2 * tiles)
    tail = lon - (tiles - 1) * LANES
    place = lax.axis_index("lat")
    odd = place % 2 == 1
    edges_got = [edge_tiles(ref, tiles, tail) for ref in (got_a, got_b)]
    row = lax.broadcasted_iota(jnp.int32, (8, LANES), 0)
    idle = jnp.min(cut[...]) >= lon // 2
    filtering = [jnp.min(keep) < lon // 2 for _, keep in edges_got]
    done = jnp.logical_and(idle, jnp.logical_not(filtering[1]))
    either = jnp.logical_or(*filtering)
    both = jnp.logical_and(jnp.logical_not(done), either)
    neither = jnp.logical_and(jnp.logical_not(done), jnp.logical_not(either))

    def put(v_a, v_b):
        for j in range(tiles):
            before = jnp.where(place == 0, 0.0, jnp.where(odd, v_a[j], v_b[j]))
            after = jnp.where(place == lat_count - 1, 0.0, jnp.where(odd, v_b[j], v_a[j]))
            halo[0, j], halo[1, j] = before, after
            column[j, rows_at(rows), :] = jnp.where(row < levels, pltpu.roll(before, levels, 0), after)

    @pl.when(done)
    def _():
        put([near[j] for j in range(tiles)], extended(edges_got[1][0], tail))

    @pl.when(neither)
    def _():
        put(*(extended(v, tail) for v, _ in edges_got))

    @pl.when(both)
    def _():
        put(*filtered_edges(lon, edges_got, tables, twiddle, y, z))


def near_edge(got_a, tables, twiddle, cut, lon):
    vmem = pl.BlockSpec(memory_space=pltpu.VMEM)
    classes = RADIX // 2 + 1
    return pl.pallas_call(
        functools.partial(near_kernel, lon),
        out_shape=pltpu.VMEM((got_a.shape[0] // 8, 8, LANES), f32),
        in_specs=[vmem] * 4,
        out_specs=vmem,
        scratch_shapes=[pltpu.VMEM((classes, 16, 2 * WIDE), bf16), pltpu.VMEM((classes, 16, WIDE), f32)],
        compiler_params=pltpu.CompilerParams(vmem_limit_bytes=24 << 20),
        name="near",
    )(got_a, in_vmem(tables), in_vmem(twiddle), cut)


def with_halo(column, tables, twiddle, cut, got_a, got_b, lon, lat_count):
    tiles = column.shape[0]
    assert got_a.shape[0] == 8 * tiles
    near = near_edge(got_a, tables, twiddle, cut, lon)
    classes = RADIX // 2 + 1
    vmem = pl.BlockSpec(memory_space=pltpu.VMEM)
    return pl.pallas_call(
        functools.partial(halo_kernel, lon, lat_count),
        out_shape=[pltpu.VMEM((2, tiles, 8, LANES), f32), pltpu.VMEM(column.shape, f32)],
        in_specs=[vmem] * 7,
        out_specs=[vmem] * 2,
        scratch_shapes=[pltpu.VMEM((classes, 16, 2 * WIDE), bf16), pltpu.VMEM((classes, 16, WIDE), f32)],
        input_output_aliases={6: 1},
        compiler_params=pltpu.CompilerParams(vmem_limit_bytes=24 << 20),
        name="halo",
    )(got_a, got_b, in_vmem(tables), in_vmem(twiddle), cut, near, column)


def beside(fields, halo, f, l, j, g, toward):
    levels = fields.shape[1]
    value = fields[f, l, j, rows_at(8 * g + 1 + toward), :]
    row = lax.broadcasted_iota(jnp.int32, (8, LANES), 0)
    slot = pl.ds((f - 1) * levels + l, 1)
    if toward < 0 and g == 0:
        return jnp.where(row > 0, value, jnp.broadcast_to(halo[0, j, slot, :], value.shape))
    if toward > 0 and g == (fields.shape[3] - 8) // 8 - 1:
        return jnp.where(row < 7, value, jnp.broadcast_to(halo[1, j, slot, :], value.shape))
    return value


def east(v):
    lane = lane_index()
    r = [rolled(a, 1) for a in v]
    return [jnp.where(lane < LANES - 1, a, b) for a, b in zip(r[:-1], r[1:])] + [r[-1]]


def west(v, tail):
    lane = lane_index()
    r = [rolled(a, -1) for a in v]
    r_before = [rolled(v[-1], tail - 1)] + r[:-1]
    return [jnp.where(lane > 0, a, b) for a, b in zip(r, r_before)]


def thickness_rows(g, lon, fields, halo, trig, thick):
    levels, tiles = fields.shape[1:3]
    tail = lon - (tiles - 1) * LANES
    at = rows_at(8 * g)
    mid = 8 * g + 1
    south, north = trig[2, at, :], trig[3, at, :]
    found = {}
    for l in range(levels):
        u, h = ([fields[f, l, j, rows_at(mid), :] for j in range(tiles)] for f in (0, 2))
        he, ue = east(h), east(u)
        flux = [(h[j] + he[j]) * (u[j] + ue[j]) for j in range(tiles)]
        flux_west = west(flux, tail)
        for j in range(tiles):
            v = fields[1, l, j, rows_at(mid), :]
            v_up, v_down = (beside(fields, halo, 1, l, j, g, to) for to in (-1, 1))
            h_up, h_down = (beside(fields, halo, 2, l, j, g, to) for to in (-1, 1))
            merid = (h[j] + h_down) * (v + v_down) * north - (h_up + h[j]) * (v_up + v) * south
            found[l, j] = h[j] - (0.25 * time_step) * (flux[j] - flux_west[j] + merid)
    for (l, j), new in found.items():
        wide = LANES if j < tiles - 1 else tail
        thick[l, at, pl.ds(LANES * j, wide)] = new[:, :wide]


def thickness_kernel(lon, fields, halo, trig, cut, _thick, thick):
    groups = trig.shape[1] // 8

    @pl.when(jnp.min(cut[...]) < lon // 2)
    def _():
        for g in range(1, groups - 1):
            thickness_rows(g, lon, fields, halo, trig, thick)

    for g in sorted({0, groups - 1}):
        thickness_rows(g, lon, fields, halo, trig, thick)


def winds_kernel(lon, fields, halo, trig, thick, *refs):
    *hops, winds_hbm, thick_hbm, winds, sem = refs
    levels, tiles = fields.shape[1:3]
    rows = trig.shape[1]
    tail = lon - (tiles - 1) * LANES
    place = lax.axis_index("lev")
    masks = [jnp.where(place + k + 1 <= len(hops), 1.0, 0.0) for k in range(len(hops))]
    copies = [pltpu.make_async_copy(thick, thick_hbm, sem.at[rows // 8])]
    copies[0].start()

    row = lax.broadcasted_iota(jnp.int32, (8, LANES), 0)

    def total(load):
        terms = [load(ref) * mask for ref, mask in zip(hops, masks)]
        return functools.reduce(jnp.add, terms) if terms else jnp.zeros((8, LANES), f32)

    def below(j, at):
        return total(lambda ref: ref[j, rows_at(at), :])

    def below_halo(j, side):
        start = rows + side * levels
        lines = [total(lambda ref, l=l: ref[j, pl.ds(start + l, 1), :]) for l in range(levels)]
        return jnp.broadcast_to(functools.reduce(jnp.add, lines), (8, LANES))

    def below_beside(j, g, own, toward):
        if toward < 0 and g == 0:
            return jnp.where(row > 0, pltpu.roll(own, 1, 0), below_halo(j, 0))
        if toward > 0 and g == rows // 8 - 1:
            return jnp.where(row < 7, pltpu.roll(own, 7, 0), below_halo(j, 1))
        return below(j, 8 * g + toward)

    for g in range(rows // 8):
        at = rows_at(8 * g)
        here = 8 * g + 1
        sine, cosine = trig[0, at, :], trig[1, at, :]
        s = [below(j, 8 * g) for j in range(tiles)]
        sum_x = [a - b for a, b in zip(east(s), west(s, tail))]
        sum_y = [below_beside(j, g, s[j], 1) - below_beside(j, g, s[j], -1) for j in range(tiles)]
        found = {}
        for l in reversed(range(levels)):
            h = [fields[2, l, j, rows_at(here), :] for j in range(tiles)]
            he, hw = east(h), west(h, tail)
            for j in range(tiles):
                u, v = (fields[f, l, j, rows_at(here), :] for f in range(2))
                dx = he[j] - hw[j]
                h_up, h_down = (beside(fields, halo, 2, l, j, g, to) for to in (-1, 1))
                dy = h_down - h_up
                new_u = u - time_step * (0.5 * (sum_x[j] + 0.5 * dx) - coriolis * sine * v)
                new_v = v - time_step * (0.5 * cosine * (sum_y[j] + 0.5 * dy) + coriolis * sine * u)
                sum_x[j] = sum_x[j] + dx
                sum_y[j] = sum_y[j] + dy
                found[l, j] = (new_u, new_v)
            if l % LEVEL_BATCH == 0:
                for (m, j), pair in found.items():
                    wide = LANES if j < tiles - 1 else tail
                    for f in range(2):
                        winds[f, m, at, pl.ds(LANES * j, wide)] = pair[f][:, :wide]
                found = {}
        copies.append(pltpu.make_async_copy(winds.at[:, :, at], winds_hbm.at[:, :, at], sem.at[g]))
        copies[-1].start()
    for copy in copies:
        copy.wait()


def stepped_thickness(fields, halo, trig, cut, thick, lon):
    vmem = pl.BlockSpec(memory_space=pltpu.VMEM)
    return pl.pallas_call(
        functools.partial(thickness_kernel, lon),
        out_shape=pltpu.VMEM(thick.shape, f32),
        in_specs=[vmem] * 5,
        out_specs=vmem,
        input_output_aliases={4: 0},
        compiler_params=pltpu.CompilerParams(vmem_limit_bytes=24 << 20),
        cost_estimate=pl.CostEstimate(flops=4_000_000_000, bytes_accessed=4_000_000, transcendentals=0),
        name="thickness",
    )(fields, halo, trig, cut, thick)


def stepped_winds(fields, halo, trig, thick, hops, shape, lon):
    hbm = pl.BlockSpec(memory_space=pltpu.HBM)
    return pl.pallas_call(
        functools.partial(winds_kernel, lon),
        out_shape=[jax.ShapeDtypeStruct(shape, f32), jax.ShapeDtypeStruct(thick.shape, f32)],
        in_specs=[pl.BlockSpec(memory_space=pltpu.VMEM)] * (4 + len(hops)),
        out_specs=[hbm, hbm],
        scratch_shapes=[pltpu.VMEM(shape, f32), pltpu.SemaphoreType.DMA((trig.shape[1] // 8 + 1,))],
        compiler_params=pltpu.CompilerParams(vmem_limit_bytes=24 << 20),
        name="winds",
    )(fields, halo, trig, thick, *hops)


def swaps(lat_count, lev_count, first):
    pairs = []
    for i in range(lat_count):
        other = i + 1 if (i - first) % 2 == 0 else i - 1
        for l in range(lev_count):
            if 0 <= other < lat_count:
                pairs.append((i * lev_count + l, other * lev_count + l))
            else:
                pairs.append((i * lev_count + l, i * lev_count + (l + 1) % lev_count))
    return pairs


def per_device(winds, thick, cutoff):
    lat_count, lev_count = lax.axis_size("lat"), lax.axis_size("lev")
    lon = thick.shape[-1]
    sent_a, sent_b, trig, cut = edges(winds, thick, cutoff, lat_count)
    got_a = lax.ppermute(sent_a, ("lat", "lev"), swaps(lat_count, lev_count, 0))
    got_b = lax.ppermute(sent_b, ("lat", "lev"), swaps(lat_count, lev_count, 1))
    tables, twiddle = (jnp.asarray(constant) for constant in filter_tables(lon))
    fields, column, new_thick = filtered_fields(winds, thick, cut, trig, tables, twiddle)
    halo, column = with_halo(column, tables, twiddle, cut, got_a, got_b, lon, lat_count)
    hops = [
        lax.ppermute(column, "lev", [(i, (i - hop) % lev_count) for i in range(lev_count)])
        for hop in range(1, lev_count)
    ]
    new_thick = stepped_thickness(fields, halo, trig, cut, new_thick, lon)
    return tuple(stepped_winds(fields, halo, trig, new_thick, hops, winds.shape, lon))


def solution(mesh):
    return jax.shard_map(
        per_device,
        mesh=mesh,
        in_specs=(P(None, "lev", "lat", None), P("lev", "lat", None), P("lat")),
        out_specs=(P(None, "lev", "lat", None), P("lev", "lat", None)),
        check_vma=False,
    )
```
